32 devices in a mesh: grp: 4 (over y, x), dom: 8 (over z, core).
Axes of the slice: x: 2, y: 2, z: 4, core: 2. Of those that a mesh axis runs over, the one named last changes fastest.
Arguments:
- features: bfloat16 [16384, 1024], P(('grp', 'dom')), may hold values from -6 to 6
- node_order: int32 [16384], P(('grp', 'dom')), may hold values from 0 to 16383, as said below
- block_cols: int32 [128, 16], P(('grp', 'dom')), may hold values from 0 to 31
- block_count: int32 [128], P(('grp', 'dom')), may hold values from 1 to 16, as said below
- block_vals: bfloat16 [128, 16, 128, 128], P(('grp', 'dom')), may hold values from -0.1875 to 0.1875
- weight: bfloat16 [1024, 512], replicated, may hold values from -0.1875 to 0.1875
- cotangent: bfloat16 [16384, 512], P(('grp', 'dom')), may hold values from -12 to 12
Outputs:
- hidden: bfloat16 [16384, 512], P(('grp', 'dom'))
- grad_weight: float32 [1024, 512], replicated
The draws below stay inside these ranges and needn't reach their ends.
Inputs may be any that keep to these rules, and one draw needn't show every extreme that they name: `node_order`: A permutation of the crawl rows; the positions of one device's block of 512 take exactly 16 crawl rows from each device's block of 512 crawl rows. `block_count`: some row of blocks holds exactly 16 live blocks.
All inputs are finite; a program needn't handle non-finite values.
Results may differ from the reference program's by a relative error of at most 0.014.
Values may be sent and summed in bfloat16 or wider, within the bound.
No kernel may reach another device: no remote copies, remote signals or barrier semaphores. Data moves between devices by JAX's collectives and lax.ppermute only.
A program may use at most 128 MiB of HBM per device.

```python
import jax
import jax.numpy as jnp
from jax import lax

F = 1024
H = 512
TILE = 128
BLOCKS = 16
ROWS_DEV = 512
GROUP_TILES = 32
N_NODES = 16384
TILES = 128
N_GRP = 4
N_DOM = 8


def draw_node_order(key, part):
    key = jax.random.fold_in(key, 71)
    devices = N_GRP * N_DOM
    pair_rows = ROWS_DEV // devices
    key_src, key_dst = jax.random.split(key)
    source = jax.vmap(lambda subkey: jax.random.permutation(subkey, ROWS_DEV))(jax.random.split(key_src, devices)).astype(jnp.int32)
    target = jax.vmap(lambda subkey: jax.random.permutation(subkey, ROWS_DEV))(jax.random.split(key_dst, devices)).astype(jnp.int32)
    offsets = (jnp.arange(devices, dtype=jnp.int32) * ROWS_DEV)[:, None, None]
    values = (source.reshape(devices, devices, pair_rows) + offsets).transpose(1, 0, 2).reshape(devices, ROWS_DEV)
    result = jnp.zeros((devices, ROWS_DEV), jnp.int32).at[jnp.arange(devices, dtype=jnp.int32)[:, None], target].set(values)
    return result.reshape(-1)


def draw_block_count(key, part):
    key = jax.random.fold_in(key, 72)
    devices = N_GRP * N_DOM
    tiles_dev = ROWS_DEV // TILE
    key_cap, key_count, key_busy = jax.random.split(key, 3)
    capacity = jax.random.randint(key_cap, (devices,), BLOCKS // 4, BLOCKS + 1).astype(jnp.int32)
    busiest = jax.random.randint(key_busy, (), 0, devices).astype(jnp.int32)
    capacity = capacity.at[busiest].set(BLOCKS)
    counts = jax.random.randint(key_count, (devices, tiles_dev), 1, capacity[:, None] + 1).astype(jnp.int32)
    counts = counts.at[busiest, 0].set(BLOCKS)
    return counts.reshape(-1)


def draw_cotangent(key, part):
    key = jax.random.fold_in(key, 73)
    key_main = jax.random.fold_in(key, 0)
    position = jnp.arange(N_NODES, dtype=jnp.float32) / N_NODES
    row_scale = (3.0 ** position)[:, None]
    values = jnp.clip(jax.random.normal(key_main, (N_NODES, H), jnp.float32), -4.0, 4.0) * row_scale
    return values.astype(jnp.bfloat16)


def plant(values, rng, least, top_value):
    place = [jax.random.randint(jax.random.fold_in(rng, axis), (), 0, length) for axis, length in enumerate(values.shape)]
    longest = values.shape.index(max(values.shape))
    next_to = place[:longest] + [(place[longest] + 1) % values.shape[longest]] + place[longest + 1:]
    return values.at[tuple(place)].set(least).at[tuple(next_to)].set(top_value)


def level_of(key, dims, pieces, least, top_value):
    loudness, own = 1.0, jax.random.fold_in(key, 6)
    for dim, blocks in pieces:
        heights = jnp.exp(jax.random.uniform(jax.random.fold_in(own, dim), (blocks,), jnp.float32, least / len(pieces), top_value / len(pieces)))
        loudness = loudness * jnp.repeat(heights, dims[dim] // blocks).reshape([-1 if axis == dim else 1 for axis in range(len(dims))])
    return loudness


def gaussian(rng, extent, scale, bound, cuts=(), held_as=jnp.bfloat16):
    values = scale * jax.random.normal(rng, extent, jnp.float32)
    if cuts:
        values = values * level_of(rng, extent, cuts, -0.22, 0.18)
    return jnp.clip(values, -bound, bound).astype(held_as)


def setup_inputs(seed: int = 0) -> dict:
    streams_of = jax.random.split(jax.random.key(seed), 8)
    features = gaussian(streams_of[0], (N_NODES, F), 1.0, 6.0, ((0, 32),))
    node_order = draw_node_order(jax.random.fold_in(streams_of[7], 71), 0)
    block_cols = plant(jax.random.randint(streams_of[2], (TILES, BLOCKS), 0, GROUP_TILES), jax.random.fold_in(streams_of[2], 1), 0, GROUP_TILES - 1).astype(jnp.int32)
    block_count = draw_block_count(jax.random.fold_in(streams_of[7], 71), 0)
    block_vals = gaussian(streams_of[4], (TILES, BLOCKS, TILE, TILE), (TILE * BLOCKS // 2) ** -0.5, 0.1875, ((0, 32),))
    weight = gaussian(streams_of[5], (F, H), F ** -0.5, 0.1875)
    cotangent = draw_cotangent(jax.random.fold_in(streams_of[7], 71), 0)
    return dict(features=features, node_order=node_order, block_cols=block_cols, block_count=block_count, block_vals=block_vals, weight=weight, cotangent=cotangent)


def silu_slope(values):
    sig = jax.nn.sigmoid(values)
    return sig * (1.0 + values * (1.0 - sig))


def reference(features, node_order, block_cols, block_count, block_vals, weight, cotangent):
    ordered = features[node_order]
    transformed = jnp.dot(ordered, weight, preferred_element_type=jnp.float32).astype(jnp.bfloat16)
    tiles_dev = ROWS_DEV // TILE
    z_tiles = transformed.reshape(N_GRP, GROUP_TILES, TILE, H)
    cols_all = block_cols.reshape(N_GRP, N_DOM, tiles_dev, BLOCKS)
    live_all = (jnp.arange(BLOCKS, dtype=jnp.int32)[None, :] < block_count[:, None]).reshape(N_GRP, N_DOM, tiles_dev, BLOCKS)
    vals_all = block_vals.reshape(N_GRP, N_DOM, tiles_dev, BLOCKS, TILE, TILE)
    cot_all = cotangent.reshape(N_GRP, N_DOM, tiles_dev, TILE, H)

    def group_pass(inputs):
        gathered, cols_grp, live_grp, vals_grp, cot_grp = inputs

        def device_forward(dev_in):
            cols_dev, live_dev, vals_dev = dev_in
            masked_vals = jnp.where(live_dev[:, :, None, None], vals_dev.astype(jnp.float32), 0.0)
            selected = gathered[cols_dev].astype(jnp.float32)
            return jnp.einsum('tkij,tkjh->tih', masked_vals, selected)

        aggregate = lax.map(device_forward, (cols_grp, live_grp, vals_grp))
        hidden_grp = jax.nn.silu(aggregate).astype(jnp.bfloat16)
        grad_agg = (cot_grp.astype(jnp.float32) * silu_slope(aggregate)).astype(jnp.bfloat16)

        def device_backward(carry, dev_in):
            cols_dev, live_dev, vals_dev, grad_dev = dev_in
            masked_vals = jnp.where(live_dev[:, :, None, None], vals_dev.astype(jnp.float32), 0.0)
            contrib = jnp.einsum('tkij,tih->tkjh', masked_vals, grad_dev.astype(jnp.float32))
            partial_value = jnp.zeros((GROUP_TILES, TILE, H), jnp.float32).at[cols_dev.reshape(-1)].add(contrib.reshape(-1, TILE, H))
            partial_value = lax.optimization_barrier(partial_value.astype(jnp.bfloat16)).astype(jnp.float32)
            return carry + partial_value, None

        summed, unused = lax.scan(device_backward, jnp.zeros((GROUP_TILES, TILE, H), jnp.float32),
                                  (cols_grp, live_grp, vals_grp, grad_agg))
        return hidden_grp, summed

    hidden_all, grad_rows = lax.map(group_pass, (z_tiles, cols_all, live_all, vals_all, cot_all))
    hidden = hidden_all.reshape(N_NODES, H)
    grad_transformed = grad_rows.reshape(N_NODES, H)
    grad_weight = jnp.dot(ordered.astype(jnp.float32).T, grad_transformed, precision=lax.Precision.HIGHEST)
    return hidden, grad_weight
```

```python
import math

import jax
import jax.numpy as jnp
from jax import lax
from jax.experimental import pallas as pl
from jax.experimental.pallas import tpu as pltpu
from jax.sharding import Mesh, PartitionSpec as P

BF16 = jnp.bfloat16
F32 = jnp.float32
SWAP = [(0, 1), (1, 0)]


def iota(shape, dim):
    return lax.broadcasted_iota(jnp.int32, shape, dim)


def dot(a, b):
    return jnp.dot(a, b, preferred_element_type=F32)


def dot_rows(a, b):
    return lax.dot_general(a, b, (((0,), (0,)), ((), ())), preferred_element_type=F32)


def params(mib):
    return pltpu.CompilerParams(vmem_limit_bytes=mib << 20)


def index_kernel(n_grp, n_zz, n_core, per_pair, order_ref, want_ref, slot_ref):
    rows = order_ref.shape[1]
    devices = n_grp * n_zz * n_core
    shift = int(math.log2(rows))
    order_r = order_ref[...]
    down, across = iota((rows, rows), 0), iota((rows, rows), 1)
    order_c = jnp.sum(
        jnp.where(down == across, order_r.astype(F32), 0.0), axis=1, keepdims=True
    ).astype(jnp.int32)
    source_r, source_c = order_r >> shift, order_c >> shift
    row_c = order_c & (rows - 1)
    same = jnp.where(source_c == source_r, 1.0, 0.0)
    rank_c = jnp.sum(jnp.where(across < down, same, 0.0), axis=1, keepdims=True).astype(jnp.int32)
    rank_r = jnp.sum(jnp.where(down < across, same, 0.0), axis=0, keepdims=True).astype(jnp.int32)
    owner = jnp.where(iota((devices, rows), 0) == source_r, 1.0, 0.0).astype(BF16)
    at_rank = iota((rows, per_pair), 1) == rank_c
    high = jnp.where(at_rank, (row_c >> 4).astype(F32), 0.0).astype(BF16)
    low = jnp.where(at_rank, (row_c & 15).astype(F32), 0.0).astype(BF16)
    want_ref[...] = (dot(owner, high) * 16.0 + dot(owner, low)).astype(jnp.int32)
    per_grp = n_zz * n_core
    grp_at = jnp.right_shift(source_r, int(math.log2(per_grp)))
    inner = source_r & (per_grp - 1)
    slot_ref[...] = (inner * n_grp + grp_at) * per_pair + rank_r


def send_kernel(n_grp, per_pair, asked_ref, features_ref, weight_ref, rows_ref, z_ref):
    devices = asked_ref.shape[0]
    rows = features_ref.shape[0]
    half = z_ref.shape[2]
    asked = asked_ref[...]
    spread = jnp.where(
        iota((rows, devices), 0) // per_pair == iota((rows, devices), 1), 1.0, 0.0
    ).astype(BF16)
    high = dot(spread, (asked >> 4).astype(F32).astype(BF16))
    low = dot(spread, (asked & 15).astype(F32).astype(BF16))
    mine = iota((rows, per_pair), 1) == (iota((rows, per_pair), 0) & (per_pair - 1))
    row_c = jnp.sum(jnp.where(mine, high * 16.0 + low, 0.0), axis=1, keepdims=True).astype(jnp.int32)
    pick = jnp.where(iota((rows, rows), 1) == row_c, 1.0, 0.0).astype(BF16)
    rows_ref[...] = dot(pick, features_ref[...]).astype(BF16)
    z = dot(rows_ref[...], weight_ref[...]).astype(BF16)
    per_dest = rows // n_grp
    for g in range(n_grp):
        for c in range(2):
            z_ref[2 * g + c] = z[g * per_dest:(g + 1) * per_dest, c * half:(c + 1) * half]


def layer_kernel(
    cols_ref, slot_ref, z_ref, vals_a, vals_b, cot_a, cot_b,
    hidden_a, hidden_b, partial_ref, panel, total,
):
    n_src, n_blk, piece, half = z_ref.shape
    rows = n_src * piece
    tiles, blocks, tile = vals_a.shape[0], vals_a.shape[1], vals_a.shape[2]

    def pick_of(n):
        return jnp.where(
            iota((rows, rows), 0) == slot_ref[pl.ds(n, 1), :], 1.0, 0.0
        ).astype(BF16)

    total[...] = jnp.zeros_like(total)
    panel[pl.ds(n_blk * rows, tile), :] = jnp.zeros((tile, half), BF16)

    @pl.loop(0, n_blk)
    def _(n):
        held = jnp.concatenate([z_ref[s, n] for s in range(n_src)], axis=0)
        at = pl.multiple_of(n * rows, rows)
        panel[pl.ds(at, rows), :] = dot_rows(pick_of(n), held).astype(BF16)

    for side, (vals, cot, hidden) in enumerate(
        ((vals_a, cot_a, hidden_a), (vals_b, cot_b, hidden_b))
    ):
        @pl.loop(0, tiles)
        def _(t):
            at = pl.multiple_of(t * tile, tile)
            starts = [
                pl.multiple_of(cols_ref[side * tiles + t, k] * tile, tile) for k in range(blocks)
            ]
            left = jnp.concatenate([vals[t, k] for k in range(blocks)], axis=1)
            right = jnp.concatenate([panel[pl.ds(s, tile), :] for s in starts], axis=0)
            agg = dot(left, right)
            sig = jax.nn.sigmoid(agg)
            hidden[pl.ds(at, tile), :] = (agg * sig).astype(BF16)
            slope = sig * (1.0 + agg * (1.0 - sig))
            grad = (cot[pl.ds(at, tile), :].astype(F32) * slope).astype(BF16)
            for k in range(blocks):
                total[pl.ds(starts[k], tile), :] += dot_rows(vals[t, k], grad)

    @pl.loop(0, n_blk)
    def _(n):
        at = pl.multiple_of(n * rows, rows)
        back = dot(pick_of(n), total[pl.ds(at, rows), :].astype(BF16)).astype(BF16)
        for s in range(n_src):
            partial_ref[s, n] = back[s * piece:(s + 1) * piece, :]


def shards(features, node_order, block_cols, block_count, block_vals, weight, cotangent):
    rows, width_in = features.shape
    hidden_units = weight.shape[1]
    half = hidden_units // 2
    tiles, blocks, tile = block_vals.shape[0], block_vals.shape[1], block_vals.shape[-1]
    n_grp, n_zz, n_core = lax.axis_size("grp"), lax.axis_size("zz"), lax.axis_size("core")
    n_dom = n_zz * n_core
    devices = n_grp * n_dom
    per_pair = rows // devices
    piece = n_grp * per_pair
    core = lax.axis_index("core")
    everyone = ("grp", "zz", "core")

    vals_b = lax.ppermute(block_vals, "core", SWAP)
    cot_a = lax.dynamic_slice_in_dim(cotangent, core * half, half, axis=1)
    cot_b = lax.ppermute(
        lax.dynamic_slice_in_dim(cotangent, (1 - core) * half, half, axis=1), "core", SWAP
    )
    live = iota((tiles, blocks), 1) < block_count[:, None]
    cols_a = jnp.where(live, block_cols, n_dom * tiles)
    cols = jnp.concatenate([cols_a, lax.ppermute(cols_a, "core", SWAP)], axis=0)

    want, slot = pl.pallas_call(
        lambda *refs: index_kernel(n_grp, n_zz, n_core, per_pair, *refs),
        out_shape=(
            jax.ShapeDtypeStruct((devices, per_pair), jnp.int32),
            jax.ShapeDtypeStruct((1, rows), jnp.int32),
        ),
        compiler_params=params(32),
        name="index",
    )(node_order.reshape(1, rows))
    asked = lax.all_to_all(want, everyone, split_axis=0, concat_axis=0, tiled=True)
    slots = lax.all_gather(slot, ("zz", "core"), axis=0, tiled=True)

    rows_out, z_out = pl.pallas_call(
        lambda *refs: send_kernel(n_grp, per_pair, *refs),
        out_shape=(
            jax.ShapeDtypeStruct((rows, width_in), BF16),
            jax.ShapeDtypeStruct((n_grp * n_core, rows // n_grp, half), BF16),
        ),
        compiler_params=params(40),
        name="send",
    )(asked, features, weight)

    z_in = lax.all_to_all(z_out, ("grp", "core"), split_axis=0, concat_axis=0, tiled=True)
    z_in = z_in.reshape(n_grp, n_core, n_dom, per_pair, half).transpose(1, 2, 0, 3, 4)
    z_in = z_in.reshape(n_core, n_dom, piece, half)
    z_all = lax.all_gather(z_in, "zz", axis=0, tiled=True)

    held = lax.all_to_all(
        rows_out.reshape(n_grp, rows // n_grp, width_in), "grp", split_axis=0, concat_axis=0, tiled=True
    )
    held = held.reshape(n_grp, n_dom, per_pair, width_in).transpose(1, 0, 2, 3).reshape(rows, width_in)
    held = jnp.concatenate([held, lax.ppermute(held, "core", SWAP)], axis=0)

    smem = pl.BlockSpec(memory_space=pltpu.SMEM)
    vmem = pl.BlockSpec(memory_space=pltpu.VMEM)
    hidden_a, hidden_b, partial = pl.pallas_call(
        layer_kernel,
        out_shape=(
            jax.ShapeDtypeStruct((rows, half), BF16),
            jax.ShapeDtypeStruct((rows, half), BF16),
            jax.ShapeDtypeStruct((n_dom, n_dom, piece, half), BF16),
        ),
        in_specs=[smem] + [vmem] * 6,
        out_specs=(vmem,) * 3,
        scratch_shapes=[
            pltpu.VMEM((n_dom * rows + tile, half), BF16),
            pltpu.VMEM((n_dom * rows + tile, half), F32),
        ],
        compiler_params=params(52),
        name="layer",
    )(cols, slots, z_all, block_vals, vals_b, cot_a, cot_b)

    other = lax.ppermute(hidden_b, "core", SWAP)
    first = core == 0
    hidden = jnp.concatenate(
        [jnp.where(first, hidden_a, other), jnp.where(first, other, hidden_a)], axis=1
    )

    grad = lax.psum_scatter(
        partial.reshape(n_dom * n_dom * piece, half), "zz", scatter_dimension=0, tiled=True
    )
    grad = jnp.concatenate(
        [
            lax.dynamic_slice_in_dim(grad, core * rows, rows, axis=0),
            lax.dynamic_slice_in_dim(grad, (1 - core) * rows, rows, axis=0),
        ],
        axis=0,
    )
    local = dot_rows(held, grad).astype(BF16)
    chips = n_grp * n_zz
    share = width_in // chips
    terms = lax.all_to_all(
        local.reshape(chips, share, half), ("grp", "zz"), split_axis=0, concat_axis=0, tiled=True
    )
    summed = jnp.sum(terms.astype(F32), axis=0).astype(BF16)
    whole = lax.all_gather(summed, everyone, axis=0, tiled=False)
    whole = whole.reshape(chips, n_core, share, half).transpose(0, 2, 1, 3)
    grad_weight = whole.reshape(width_in, hidden_units).astype(F32)
    return hidden, grad_weight


def solution(mesh):
    n_grp, n_dom = mesh.shape["grp"], mesh.shape["dom"]
    split = Mesh(mesh.devices.reshape(n_grp, n_dom // 2, 2), ("grp", "zz", "core"))
    by_rows = ("grp", "zz", "core")
    placed = (
        P(by_rows, None),
        P(by_rows),
        P(by_rows, None),
        P(by_rows),
        P(by_rows, None, None, None),
        P(),
        P(by_rows, None),
    )
    return jax.shard_map(
        shards,
        mesh=split,
        in_specs=placed,
        out_specs=(P(by_rows, None), P()),
        check_vma=False,
    )
```

```python
import jax
import jax.numpy as jnp
from jax import lax
from jax.experimental import pallas as pl
from jax.experimental.pallas import tpu as pltpu
from jax.sharding import Mesh, PartitionSpec as P

BF16 = jnp.bfloat16
F32 = jnp.float32
I32 = jnp.int32


def log2(n):
    assert n & (n - 1) == 0
    return n.bit_length() - 1


def iota(shape, dim):
    return lax.broadcasted_iota(I32, shape, dim)


def one_hot(mask):
    return jnp.where(mask, 1.0, 0.0).astype(BF16)


def dot(a, b):
    return jnp.dot(a, b, preferred_element_type=F32)


def dot_rows(a, b):
    return lax.dot_general(a, b, (((0,), (0,)), ((), ())), preferred_element_type=F32)


def call(body, outs, ins, name, mib, scratch=()):
    smem = pl.BlockSpec(memory_space=pltpu.SMEM)
    vmem = pl.BlockSpec(memory_space=pltpu.VMEM)
    return pl.pallas_call(
        body,
        out_shape=tuple(jax.ShapeDtypeStruct(s, d) for s, d in outs),
        in_specs=[smem if where == "s" else vmem for where, _ in ins],
        out_specs=tuple(vmem for _ in outs),
        scratch_shapes=list(scratch),
        compiler_params=pltpu.CompilerParams(vmem_limit_bytes=mib << 20),
        name=name,
    )(*(value for _, value in ins))


class Sizes:
    def __init__(self, rows, tiles):
        self.grp, self.zz = lax.axis_size("grp"), lax.axis_size("zz")
        self.dom = 2 * self.zz
        self.rows, self.tiles = rows, tiles
        self.pair = rows // (self.grp * self.dom)
        self.piece = self.grp * self.pair
        self.per_grp = self.dom * self.pair


def index_kernel(z, me_ref, order_ref, *outs):
    want_refs, slot_ref = outs[:-1], outs[-1]
    rows = z.rows
    shift = log2(rows)
    flip = me_ref[0] * z.dom
    order_r = order_ref[...]
    down, across = iota((rows, rows), 0), iota((rows, rows), 1)
    order_c = jnp.sum(
        jnp.where(down == across, order_r.astype(F32), 0.0), axis=1, keepdims=True
    ).astype(I32)
    source_r, source_c = order_r >> shift, order_c >> shift
    row_c = order_c & (rows - 1)
    same = jnp.where(source_c == source_r, 1.0, 0.0)
    rank_c = jnp.sum(jnp.where(across < down, same, 0.0), axis=1, keepdims=True).astype(I32)
    rank_r = jnp.sum(jnp.where(down < across, same, 0.0), axis=0, keepdims=True).astype(I32)
    owner = one_hot(iota((z.grp * z.dom, rows), 0) == (source_r ^ flip))
    at_rank = iota((rows, z.pair), 1) == rank_c
    high = jnp.where(at_rank, (row_c >> 4).astype(F32), 0.0).astype(BF16)
    low = jnp.where(at_rank, (row_c & 15).astype(F32), 0.0).astype(BF16)
    want = (dot(owner, high) * 16.0 + dot(owner, low)).astype(I32)
    for s in range(z.grp):
        want_refs[s][...] = want[s * z.dom:(s + 1) * z.dom, :]
    across_grp = (source_r >> log2(z.dom)) ^ me_ref[0]
    inner = source_r & (z.dom - 1)
    slot_ref[...] = (inner * z.grp + across_grp) * z.pair + rank_r


def product_kernel(z, me_ref, features_ref, weight_ref, own_ref, other_ref):
    half = own_ref.shape[1]
    for flip, out in ((0, own_ref), (1, other_ref)):
        at = pl.multiple_of((me_ref[2] ^ flip) * half, half)
        out[...] = dot(features_ref[...], weight_ref[:, pl.ds(at, half)]).astype(BF16)


def picks(z, at_zz, table, source):
    shape = (z.rows, table.shape[0])
    row = iota(shape, 0)
    s, n = row >> log2(z.per_grp), (row >> log2(z.pair)) & (z.dom - 1)
    held_at = ((at_zz - (n >> 1)) & (z.zz - 1)) * 2 + (n & 1)
    spread = one_hot(iota(shape, 1) == (held_at * z.grp + s) * z.dom + source)
    high = dot(spread, (table >> 4).astype(F32).astype(BF16))
    low = dot(spread, (table & 15).astype(F32).astype(BF16))
    mine = iota((z.rows, z.pair), 1) == (iota((z.rows, z.pair), 0) & (z.pair - 1))
    wanted = jnp.sum(jnp.where(mine, high * 16.0 + low, 0.0), axis=1, keepdims=True).astype(I32)
    return one_hot(iota((z.rows, z.rows), 1) == wanted)


def select_kernel(z, k, me_ref, table_ref, *refs):
    ins, outs = refs[:2 if k else 3], refs[2 if k else 3:]
    table = table_ref[...]
    at_zz = (me_ref[1] - k) & (z.zz - 1)
    for rel in range(2):
        pick = picks(z, me_ref[1], table, at_zz * 2 + (me_ref[2] ^ rel))
        got = dot(pick, ins[rel][...]).astype(BF16)
        for s in range(z.grp):
            outs[s][rel] = got[s * z.per_grp:(s + 1) * z.per_grp, :]
        if k == 0 and rel == 0:
            for s in range(z.grp):
                part = pick[s * z.per_grp:(s + 1) * z.per_grp, :]
                outs[z.grp + s][...] = dot(part, ins[2][...]).astype(BF16)


def layer_kernel(z, packed, me_ref, cols_ref, slot_ref, *refs):
    count = 1 if packed else z.zz * z.grp
    y_refs, refs = refs[:count], refs[count:]
    vals_a, vals_b, cot_a, cot_b, hidden_a, hidden_b = refs[:6]
    partial_refs, (panel, total) = refs[6:-2], refs[-2:]
    rows, tile = z.rows, vals_a.shape[2]
    blocks = vals_a.shape[1]
    half = cot_a.shape[1]

    def pick_of(n):
        held_at = ((me_ref[1] - (n >> 1)) & (z.zz - 1)) * 2 + (n & 1)
        slot = slot_ref[pl.ds(held_at, 1), :]
        at = slot >> log2(z.piece)
        zz = (me_ref[1] - (at >> 1)) & (z.zz - 1)
        at = zz * 2 + ((at & 1) ^ me_ref[2])
        slot = at * z.piece + (slot & (z.piece - 1))
        return one_hot(iota((rows, rows), 0) == slot)

    def held_of(n):
        if packed:
            return y_refs[0][n]
        return jnp.concatenate(
            [
                y_refs[k * z.grp + s][rel, pl.ds(pl.multiple_of(n * z.pair, z.pair), z.pair), :]
                for k in range(z.zz)
                for rel in range(2)
                for s in range(z.grp)
            ],
            axis=0,
        )

    total[...] = jnp.zeros_like(total)
    panel[pl.ds(z.dom * rows, tile), :] = jnp.zeros((tile, half), BF16)

    @pl.loop(0, z.dom)
    def _(n):
        at = pl.multiple_of(n * rows, rows)
        panel[pl.ds(at, rows), :] = dot_rows(pick_of(n), held_of(n)).astype(BF16)

    for side, (vals, cot, hidden) in enumerate(
        ((vals_a, cot_a, hidden_a), (vals_b, cot_b, hidden_b))
    ):
        @pl.loop(0, z.tiles)
        def _(t):
            at = pl.multiple_of(t * tile, tile)
            starts = [
                pl.multiple_of(cols_ref[side * z.tiles + t, k] * tile, tile) for k in range(blocks)
            ]
            left = jnp.concatenate([vals[t, k] for k in range(blocks)], axis=1)
            right = jnp.concatenate([panel[pl.ds(s, tile), :] for s in starts], axis=0)
            agg = dot(left, right)
            sig = jax.nn.sigmoid(agg)
            hidden[pl.ds(at, tile), :] = (agg * sig).astype(BF16)
            slope = sig * (1.0 + agg * (1.0 - sig))
            grad = (cot[pl.ds(at, tile), :].astype(F32) * slope).astype(BF16)
            for k in range(blocks):
                total[pl.ds(starts[k], tile), :] += dot_rows(vals[t, k], grad)

    @pl.loop(0, z.dom)
    def _(n):
        at = pl.multiple_of(n * rows, rows)
        back = dot(pick_of(n), total[pl.ds(at, rows), :].astype(BF16)).astype(BF16)
        for p in range(z.dom):
            partial_refs[p][n] = back[p * z.piece:(p + 1) * z.piece, :]


def grad_kernel(z, me_ref, left_a, left_b, mine_a, mine_b, come_a, come_b, *refs):
    outs, whole = refs[:-1], refs[-1]
    grad_a = (mine_a[...].astype(F32) + come_a[...].astype(F32)).astype(BF16)
    grad_b = (mine_b[...].astype(F32) + come_b[...].astype(F32)).astype(BF16)
    grad_b = jnp.concatenate(
        [grad_b[(n ^ 1) * z.piece:((n ^ 1) + 1) * z.piece, :] for n in range(z.dom)], axis=0
    )
    whole[...] = (dot(left_a[...], grad_a) + dot(left_b[...], grad_b)).astype(BF16)
    share = whole.shape[0] // z.grp
    for s in range(z.grp):
        at = pl.multiple_of((me_ref[0] ^ s) * share, share)
        outs[s][...] = whole[pl.ds(at, share), :]


def sum_kernel(z, me_ref, *refs):
    terms, outs, whole = refs[:z.grp], refs[z.grp:-1], refs[-1]
    whole[...] = sum(term[...].astype(F32) for term in terms).astype(BF16)
    share = whole.shape[0] // z.zz
    for k in range(z.zz):
        at = pl.multiple_of(((me_ref[1] - k) & (z.zz - 1)) * share, share)
        outs[k][...] = whole[pl.ds(at, share), :]


def last_kernel(z, me_ref, *refs):
    pieces, out = refs[:-1], refs[-1]
    share, half = pieces[0].shape[1], pieces[0].shape[2]
    for rel in range(2):
        left = pl.multiple_of((me_ref[2] ^ rel) * half, half)
        for s in range(z.grp):
            for k in range(z.zz):
                at = (me_ref[0] ^ s) * z.zz + ((me_ref[1] - k) & (z.zz - 1))
                out[pl.ds(pl.multiple_of(at * share, share), share), pl.ds(left, half)] = (
                    pieces[rel * z.grp + s][k].astype(F32)
                )


def shards(features, node_order, block_cols, block_count, block_vals, weight, cotangent):
    rows, width_in = features.shape
    hidden_units = weight.shape[1]
    half = hidden_units // 2
    tiles, blocks, tile = block_vals.shape[0], block_vals.shape[1], block_vals.shape[-1]
    z = Sizes(rows, tiles)
    at_grp, at_zz, core = lax.axis_index("grp"), lax.axis_index("zz"), lax.axis_index("core")
    me = jnp.stack([at_grp, at_zz, core]).astype(I32)

    def to_core(x):
        return lax.ppermute(x, "core", [(0, 1), (1, 0)])

    def to_grp(x, s):
        return lax.ppermute(x, "grp", [(i, i ^ s) for i in range(z.grp)]) if s else x

    def to_zz(x, k):
        return lax.ppermute(x, "zz", [(i, (i + k) % z.zz) for i in range(z.zz)]) if k else x

    own, other = call(
        lambda *refs: product_kernel(z, *refs),
        [((rows, half), BF16)] * 2,
        [("s", me), ("v", features), ("v", weight)],
        "product", 24,
    )
    ring = [[own, to_core(other)]]
    for k in range(1, z.zz):
        ring.append([to_zz(part, 1) for part in ring[-1]])

    index = call(
        lambda *refs: index_kernel(z, *refs),
        [((z.dom, z.pair), I32)] * z.grp + [((1, rows), I32)],
        [("s", me), ("v", node_order.reshape(1, rows))],
        "index", 32,
    )
    table = jnp.concatenate([to_grp(index[s], s) for s in range(z.grp)], axis=0)
    table = jnp.concatenate([table, to_core(table)], axis=0)
    table = jnp.concatenate([to_zz(table, k) for k in range(z.zz)], axis=0)
    slots = jnp.concatenate([index[-1], to_core(index[-1])], axis=0)
    slots = jnp.concatenate([to_zz(slots, k) for k in range(z.zz)], axis=0)

    vals_b = to_core(block_vals)
    cot_a = lax.dynamic_slice_in_dim(cotangent, core * half, half, axis=1)
    cot_b = to_core(lax.dynamic_slice_in_dim(cotangent, (1 - core) * half, half, axis=1))
    cols_a = jnp.where(iota((tiles, blocks), 1) < block_count[:, None], block_cols, -1)
    cols = jnp.concatenate([cols_a, to_core(cols_a)], axis=0)
    dev = cols >> log2(tiles)
    cols = jnp.where(cols < 0, z.dom * tiles, (dev ^ core) * tiles + (cols & (tiles - 1)))

    y, picked = [], None
    for k in range(z.zz):
        outs = [((2, z.per_grp, half), BF16)] * z.grp
        ins = [("s", me), ("v", table), ("v", ring[k][0]), ("v", ring[k][1])]
        if k == 0:
            outs, ins = outs + [((z.per_grp, width_in), BF16)] * z.grp, ins + [("v", features)]
        got = call(
            lambda *refs, k=k: select_kernel(z, k, *refs), outs, ins, "select", 32
        )
        if k == 0:
            picked = got[z.grp:]
        y += [to_grp(got[s], s) for s in range(z.grp)]

    packed = z.pair % 16 != 0
    if packed:
        y = jnp.stack(y).reshape(z.zz, z.grp, 2, z.dom, z.pair, half)
        y = [y.transpose(3, 0, 2, 1, 4, 5).reshape(z.dom, rows, half)]
    layer = call(
        lambda *refs: layer_kernel(z, packed, *refs),
        [((rows, half), BF16)] * 2 + [((z.dom, z.piece, half), BF16)] * z.dom,
        [("s", me), ("s", cols), ("v", slots)]
        + [("v", part) for part in y]
        + [("v", block_vals), ("v", vals_b), ("v", cot_a), ("v", cot_b)],
        "layer", 52,
        (pltpu.VMEM((z.dom * rows + tile, half), BF16), pltpu.VMEM((z.dom * rows + tile, half), F32)),
    )
    hidden_a, hidden_b, partial = layer[0], layer[1], layer[2:]

    held = jnp.stack([to_grp(picked[s], s) for s in range(z.grp)])
    held = held.reshape(z.grp, z.dom, z.pair, width_in).transpose(3, 1, 0, 2).reshape(width_in, rows)
    held_b = to_core(held)

    came = [partial[2 * (z.zz - 1) + rel] for rel in range(2)]
    for k in range(z.zz - 2, -1, -1):
        came = [to_zz(part, -1) for part in came]
        if k:
            came = [
                (part.astype(F32) + partial[2 * k + rel].astype(F32)).astype(BF16)
                for rel, part in enumerate(came)
            ]

    come = to_core(hidden_b)
    first = core == 0
    hidden = jnp.concatenate(
        [jnp.where(first, hidden_a, come), jnp.where(first, come, hidden_a)], axis=1
    )

    share = width_in // z.grp
    terms = call(
        lambda *refs: grad_kernel(z, *refs),
        [((share, half), BF16)] * z.grp,
        [("s", me), ("v", held), ("v", held_b)]
        + [("v", part.reshape(rows, half)) for part in (partial[0], partial[1], came[0], came[1])],
        "grad", 32,
        (pltpu.VMEM((width_in, half), BF16),),
    )
    terms = [to_grp(terms[s], s) for s in range(z.grp)]
    parts = call(
        lambda *refs: sum_kernel(z, *refs),
        [((share // z.zz, half), BF16)] * z.zz,
        [("s", me)] + [("v", term) for term in terms],
        "sum", 16,
        (pltpu.VMEM((share, half), BF16),),
    )
    mine = sum(to_zz(parts[k], -k).astype(F32) for k in range(z.zz)).astype(BF16)
    mine = jnp.stack([to_zz(mine, k) for k in range(z.zz)])
    mine = [to_grp(mine, s) for s in range(z.grp)]
    pieces = mine + [to_core(part) for part in mine]
    (grad_weight,) = call(
        lambda *refs: last_kernel(z, *refs),
        [((width_in, hidden_units), F32)],
        [("s", me)] + [("v", part) for part in pieces],
        "last", 16,
    )
    return hidden, grad_weight


def solution(mesh):
    n_grp, n_dom = mesh.shape["grp"], mesh.shape["dom"]
    split = Mesh(mesh.devices.reshape(n_grp, n_dom // 2, 2), ("grp", "zz", "core"))
    by_rows = ("grp", "zz", "core")
    placed = (
        P(by_rows, None),
        P(by_rows),
        P(by_rows, None),
        P(by_rows),
        P(by_rows, None, None, None),
        P(),
        P(by_rows, None),
    )
    return jax.shard_map(
        shards,
        mesh=split,
        in_specs=placed,
        out_specs=(P(by_rows, None), P()),
        check_vma=False,
    )
```

```python
import jax
import jax.numpy as jnp
from jax import lax
from jax.experimental import pallas as pl
from jax.experimental.pallas import tpu as pltpu
from jax.sharding import Mesh, PartitionSpec as P

BF16 = jnp.bfloat16
F32 = jnp.float32
I32 = jnp.int32


def log2(n):
    assert n & (n - 1) == 0
    return n.bit_length() - 1


def iota(shape, dim):
    return lax.broadcasted_iota(I32, shape, dim)


def one_hot(mask):
    return jnp.where(mask, 1.0, 0.0).astype(BF16)


def dot(a, b):
    return jnp.dot(a, b, preferred_element_type=F32)


def dot_rows(a, b):
    return lax.dot_general(a, b, (((0,), (0,)), ((), ())), preferred_element_type=F32)


def call(body, outs, ins, name, mib, us, scratch=()):
    smem = pl.BlockSpec(memory_space=pltpu.SMEM)
    vmem = pl.BlockSpec(memory_space=pltpu.VMEM)
    return pl.pallas_call(
        body,
        out_shape=tuple(jax.ShapeDtypeStruct(s, d) for s, d in outs),
        in_specs=[smem if where == "s" else vmem for where, _ in ins],
        out_specs=tuple(vmem for _ in outs),
        scratch_shapes=list(scratch),
        compiler_params=pltpu.CompilerParams(vmem_limit_bytes=mib << 20),
        cost_estimate=pl.CostEstimate(flops=int(us * 1e9), bytes_accessed=0, transcendentals=0),
        name=name,
    )(*(value for _, value in ins))


class Sizes:
    def __init__(self, rows, tiles):
        self.grp, self.zz = lax.axis_size("grp"), lax.axis_size("zz")
        self.dom = 2 * self.zz
        self.rows, self.tiles = rows, tiles
        self.pair = rows // (self.grp * self.dom)
        self.piece = self.grp * self.pair
        self.per_grp = self.dom * self.pair


def column(row):
    n = row.shape[1]
    on = iota((n, n), 0) == iota((n, n), 1)
    return jnp.sum(jnp.where(on, row.astype(F32), 0.0), axis=1, keepdims=True).astype(I32)


def index_kernel(z, me_ref, order_ref, out_ref):
    rows = z.rows
    shift = log2(rows)
    order_r = order_ref[...]
    order_c = column(order_r)
    down, across = iota((rows, rows), 0), iota((rows, rows), 1)
    source_r, source_c = order_r >> shift, order_c >> shift
    same = jnp.where(source_c == source_r, 1.0, 0.0)
    rank_c = jnp.sum(jnp.where(across < down, same, 0.0), axis=1, keepdims=True).astype(I32)
    rank_r = jnp.sum(jnp.where(down < across, same, 0.0), axis=0, keepdims=True).astype(I32)
    row_c = (order_c & (rows - 1)).astype(F32)
    asked = jnp.where(source_c * z.pair + rank_c == across, row_c, 0.0)
    out_ref[0:1, :] = jnp.sum(asked, axis=0, keepdims=True).astype(I32)
    across_grp = (source_r >> log2(z.dom)) ^ me_ref[0]
    inner = source_r & (z.dom - 1)
    out_ref[1:2, :] = (inner * z.grp + across_grp) * z.pair + rank_r


def product_kernel(z, me_ref, features_ref, weight_ref, own_ref, other_ref):
    half = own_ref.shape[1]
    for flip, out in ((0, own_ref), (1, other_ref)):
        at = pl.multiple_of((me_ref[2] ^ flip) * half, half)
        out[...] = dot(features_ref[...], weight_ref[:, pl.ds(at, half)]).astype(BF16)


def asked_rows(z, me_ref, table):
    shape = (z.rows, table.shape[0])
    row = iota(shape, 0)
    s, n = row >> log2(z.per_grp), (row >> log2(z.pair)) & (z.dom - 1)
    k = (me_ref[1] - (n >> 1)) & (z.zz - 1)
    spread = one_hot(iota(shape, 1) == ((s * 2 + (n & 1)) * z.zz + k) * 2)
    high = dot(spread, (table >> 4).astype(F32).astype(BF16))
    return high * 16.0 + dot(spread, (table & 15).astype(F32).astype(BF16))


def pick_of_source(z, me_ref, asked, k, rel):
    shape = (z.rows, z.rows)
    source = me_ref[0] * z.dom + ((me_ref[1] - k) & (z.zz - 1)) * 2 + (me_ref[2] ^ rel)
    mine = iota(shape, 1) == source * z.pair + (iota(shape, 0) & (z.pair - 1))
    wanted = jnp.sum(jnp.where(mine, asked, 0.0), axis=1, keepdims=True).astype(I32)
    return one_hot(iota(shape, 1) == wanted)


def select_own_kernel(z, me_ref, table_ref, own_ref, other_ref, features_ref, *outs):
    asked = asked_rows(z, me_ref, table_ref[...])
    for rel, part in enumerate((own_ref, other_ref)):
        pick = pick_of_source(z, me_ref, asked, 0, rel)
        got = dot(pick, part[...]).astype(BF16)
        for s in range(z.grp):
            outs[s][rel] = got[s * z.per_grp:(s + 1) * z.per_grp, :]
        if rel == 0:
            for s in range(z.grp):
                rows = pick[s * z.per_grp:(s + 1) * z.per_grp, :]
                outs[z.grp + s][...] = dot(rows, features_ref[...]).astype(BF16)


def picks_kernel(z, me_ref, table_ref, *outs):
    asked = asked_rows(z, me_ref, table_ref[...])
    for k in range(1, z.zz):
        for rel in range(2):
            outs[k - 1][rel] = pick_of_source(z, me_ref, asked, k, rel)


def select_kernel(z, pick_ref, own_ref, other_ref, *outs):
    for rel, part in enumerate((own_ref, other_ref)):
        got = dot(pick_ref[rel], part[...]).astype(BF16)
        for s in range(z.grp):
            outs[s][rel] = got[s * z.per_grp:(s + 1) * z.per_grp, :]


def place_kernel(z, me_ref, table_ref, pick_ref, back_ref):
    shape = (z.rows, z.rows)

    @pl.loop(0, z.dom)
    def _(n):
        k = (me_ref[1] - (n >> 1)) & (z.zz - 1)
        slot = table_ref[pl.ds(((n & 1) * z.zz + k) * 2 + 1, 1), :]
        at = slot >> log2(z.piece)
        zz = (me_ref[1] - (at >> 1)) & (z.zz - 1)
        at = zz * 2 + ((at & 1) ^ me_ref[2])
        slot = at * z.piece + (slot & (z.piece - 1))
        back_ref[n] = one_hot(iota(shape, 0) == slot)
        pick_ref[n] = one_hot(iota(shape, 1) == column(slot))


def turn_kernel(vals_ref, out_ref):
    tiles, blocks, tile, _ = vals_ref.shape

    @pl.loop(0, tiles)
    def _(t):
        for k in range(blocks):
            out_ref[t, k] = vals_ref[t, k].T


def layer_kernel(z, packed, cols_ref, pick_ref, back_ref, *refs):
    count = 1 if packed else z.zz * z.grp
    y_refs, refs = refs[:count], refs[count:]
    vals_a, vals_b, turned_a, turned_b, cot_a, cot_b, hidden_a, hidden_b = refs[:8]
    partial_refs, (panel, total) = refs[8:-2], refs[-2:]
    rows, blocks, tile = z.rows, vals_a.shape[1], vals_a.shape[2]
    half = cot_a.shape[1]

    def held_of(n):
        if packed:
            return y_refs[0][n]
        return jnp.concatenate(
            [
                y_refs[k * z.grp + s][rel, pl.ds(pl.multiple_of(n * z.pair, z.pair), z.pair), :]
                for k in range(z.zz)
                for rel in range(2)
                for s in range(z.grp)
            ],
            axis=0,
        )

    panel[pl.ds(z.dom * rows, tile), :] = jnp.zeros((tile, half), BF16)

    @pl.loop(0, z.dom)
    def _(n):
        at = pl.multiple_of(n * rows, rows)
        panel[pl.ds(at, rows), :] = dot(pick_ref[n], held_of(n)).astype(BF16)
        total[pl.ds(at, rows), :] = jnp.zeros((rows, half), F32)

    for side, (vals, turned, cot, hidden) in enumerate(
        ((vals_a, turned_a, cot_a, hidden_a), (vals_b, turned_b, cot_b, hidden_b))
    ):
        @pl.loop(0, z.tiles)
        def _(t):
            at = pl.multiple_of(t * tile, tile)
            starts = [
                pl.multiple_of(cols_ref[side * z.tiles + t, k] * tile, tile) for k in range(blocks)
            ]
            left = jnp.concatenate([vals[t, k] for k in range(blocks)], axis=1)
            right = jnp.concatenate([panel[pl.ds(s, tile), :] for s in starts], axis=0)
            agg = dot(left, right)
            sig = jax.nn.sigmoid(agg)
            hidden[pl.ds(at, tile), :] = (agg * sig).astype(BF16)
            slope = sig * (1.0 + agg * (1.0 - sig))
            grad = (cot[pl.ds(at, tile), :].astype(F32) * slope).astype(BF16)
            for k in range(blocks):
                total[pl.ds(starts[k], tile), :] += dot(turned[t, k], grad)

    @pl.loop(0, z.dom)
    def _(n):
        at = pl.multiple_of(n * rows, rows)
        back = dot(back_ref[n], total[pl.ds(at, rows), :].astype(BF16)).astype(BF16)
        for p in range(z.dom):
            partial_refs[p][n] = back[p * z.piece:(p + 1) * z.piece, :]


def grad_kernel(z, me_ref, left_a, left_b, mine_a, mine_b, come_a, come_b, *refs):
    outs, whole = refs[:-1], refs[-1]
    grad_a = (mine_a[...].astype(F32) + come_a[...].astype(F32)).astype(BF16)
    grad_b = (mine_b[...].astype(F32) + come_b[...].astype(F32)).astype(BF16)
    grad_b = jnp.concatenate(
        [grad_b[(n ^ 1) * z.piece:((n ^ 1) + 1) * z.piece, :] for n in range(z.dom)], axis=0
    )
    whole[...] = (dot(left_a[...], grad_a) + dot(left_b[...], grad_b)).astype(BF16)
    share = whole.shape[0] // z.grp
    for s in range(z.grp):
        at = pl.multiple_of((me_ref[0] ^ s) * share, share)
        outs[s][...] = whole[pl.ds(at, share), :]


def sum_kernel(*refs):
    refs[-1][...] = sum(term[...].astype(F32) for term in refs[:-1]).astype(BF16)


def last_kernel(z, me_ref, *refs):
    pieces, out = refs[:-1], refs[-1]
    share, half = pieces[0].shape
    for rel in range(2):
        left = pl.multiple_of((me_ref[2] ^ rel) * half, half)
        for s in range(z.grp):
            at = pl.multiple_of((me_ref[0] ^ s) * share, share)
            out[pl.ds(at, share), pl.ds(left, half)] = pieces[rel * z.grp + s][...].astype(F32)


def shards(features, node_order, block_cols, block_count, block_vals, weight, cotangent):
    rows, width_in = features.shape
    hidden_units = weight.shape[1]
    half = hidden_units // 2
    tiles, blocks, tile = block_vals.shape[0], block_vals.shape[1], block_vals.shape[-1]
    z = Sizes(rows, tiles)
    at_grp, at_zz, core = lax.axis_index("grp"), lax.axis_index("zz"), lax.axis_index("core")
    me = jnp.stack([at_grp, at_zz, core]).astype(I32)

    def to_core(x):
        return lax.ppermute(x, "core", [(0, 1), (1, 0)])

    def to_grp(x, s):
        return lax.ppermute(x, "grp", [(i, i ^ s) for i in range(z.grp)]) if s else x

    def to_zz(x, k):
        return lax.ppermute(x, "zz", [(i, (i + k) % z.zz) for i in range(z.zz)]) if k else x

    (index,) = call(
        lambda *refs: index_kernel(z, *refs),
        [((2, rows), I32)],
        [("s", me), ("v", node_order.reshape(1, rows))],
        "index", 24, 1,
    )
    domain = jnp.concatenate([to_zz(index, k) for k in range(z.zz)], axis=0)
    features, domain = lax.optimization_barrier((features, domain))
    domain = jnp.concatenate([domain, to_core(domain)], axis=0)
    table = jnp.concatenate([to_grp(domain, s) for s in range(z.grp)], axis=0)

    own, other = call(
        lambda *refs: product_kernel(z, *refs),
        [((rows, half), BF16)] * 2,
        [("s", me), ("v", features), ("v", weight)],
        "product", 16, 1.5,
    )
    ring = [[own, to_core(other)]]
    for k in range(1, z.zz):
        ring.append([to_zz(part, 1) for part in ring[-1]])

    vals_b = to_core(block_vals)
    cot_a = lax.dynamic_slice_in_dim(cotangent, core * half, half, axis=1)
    cot_b = to_core(lax.dynamic_slice_in_dim(cotangent, (1 - core) * half, half, axis=1))
    cols_a = jnp.where(iota((tiles, blocks), 1) < block_count[:, None], block_cols, -1)
    cols = jnp.concatenate([cols_a, to_core(cols_a)], axis=0)
    dev = cols >> log2(tiles)
    cols = jnp.where(cols < 0, z.dom * tiles, (dev ^ core) * tiles + (cols & (tiles - 1)))

    pieces = [((2, z.per_grp, half), BF16)] * z.grp
    got = call(
        lambda *refs: select_own_kernel(z, *refs),
        pieces + [((z.per_grp, width_in), BF16)] * z.grp,
        [("s", me), ("v", table), ("v", ring[0][0]), ("v", ring[0][1]), ("v", features)],
        "select_own", 24, 2.5,
    )
    y = [to_grp(got[s], s) for s in range(z.grp)]
    held = jnp.stack([to_grp(got[z.grp + s], s) for s in range(z.grp)])
    held = held.reshape(z.grp, z.dom, z.pair, width_in).transpose(3, 1, 0, 2).reshape(width_in, rows)
    held_b = to_core(held)
    picks = call(
        lambda *refs: picks_kernel(z, *refs),
        [((2, rows, rows), BF16)] * (z.zz - 1),
        [("s", me), ("v", table)],
        "picks", 24, 4,
    )
    for k in range(1, z.zz):
        got = call(
            lambda *refs: select_kernel(z, *refs), pieces,
            [("v", picks[k - 1]), ("v", ring[k][0]), ("v", ring[k][1])],
            "select", 16, 0.7,
        )
        y += [to_grp(got[s], s) for s in range(z.grp)]

    pick, back = call(
        lambda *refs: place_kernel(z, *refs),
        [((z.dom, rows, rows), BF16)] * 2,
        [("s", me), ("v", domain)],
        "place", 24, 6,
    )
    turned_a, turned_b = (
        call(turn_kernel, [(block_vals.shape, BF16)], [("v", vals)], "turn", 16, 3)[0]
        for vals in (block_vals, vals_b)
    )

    packed = z.pair % 16 != 0
    if packed:
        y = jnp.stack(y).reshape(z.zz, z.grp, 2, z.dom, z.pair, half)
        y = [y.transpose(3, 0, 2, 1, 4, 5).reshape(z.dom, rows, half)]
    layer = call(
        lambda *refs: layer_kernel(z, packed, *refs),
        [((rows, half), BF16)] * 2 + [((z.dom, z.piece, half), BF16)] * z.dom,
        [("s", cols), ("v", pick), ("v", back)]
        + [("v", part) for part in y]
        + [("v", block_vals), ("v", vals_b), ("v", turned_a), ("v", turned_b)]
        + [("v", cot_a), ("v", cot_b)],
        "layer", 36, 10,
        (pltpu.VMEM((z.dom * rows + tile, half), BF16), pltpu.VMEM((z.dom * rows + tile, half), F32)),
    )
    hidden_a, hidden_b, partial = layer[0], layer[1], layer[2:]

    come = to_core(hidden_b)
    came = [partial[2 * (z.zz - 1) + rel] for rel in range(2)]
    for k in range(z.zz - 2, -1, -1):
        came = [to_zz(part, -1) for part in came]
        if k:
            came = [
                (part.astype(F32) + partial[2 * k + rel].astype(F32)).astype(BF16)
                for rel, part in enumerate(came)
            ]
        if k == 1:
            came, come, held_b = lax.optimization_barrier((came, come, held_b))

    first = core == 0
    hidden = jnp.concatenate(
        [jnp.where(first, hidden_a, come), jnp.where(first, come, hidden_a)], axis=1
    )

    share = width_in // z.grp
    terms = call(
        lambda *refs: grad_kernel(z, *refs),
        [((share, half), BF16)] * z.grp,
        [("s", me), ("v", held), ("v", held_b)]
        + [("v", part.reshape(rows, half)) for part in (partial[0], partial[1], came[0], came[1])],
        "grad", 16, 1.5,
        (pltpu.VMEM((width_in, half), BF16),),
    )

    def total_of(parts):
        return call(
            sum_kernel, [((share, half), BF16)], [("v", part) for part in parts], "sum", 16, 0.5
        )[0]

    mine = total_of([to_grp(terms[s], s) for s in range(z.grp)])
    step = 1
    while step < z.zz:
        mine = total_of(
            [mine, lax.ppermute(mine, "zz", [(i, i ^ step) for i in range(z.zz)])]
        )
        step *= 2
    mine = [to_grp(mine, s) for s in range(z.grp)]
    (grad_weight,) = call(
        lambda *refs: last_kernel(z, *refs),
        [((width_in, hidden_units), F32)],
        [("s", me)] + [("v", part) for part in mine + [to_core(part) for part in mine]],
        "last", 16, 2,
    )
    return hidden, grad_weight


def solution(mesh):
    n_grp, n_dom = mesh.shape["grp"], mesh.shape["dom"]
    split = Mesh(mesh.devices.reshape(n_grp, n_dom // 2, 2), ("grp", "zz", "core"))
    by_rows = ("grp", "zz", "core")
    placed = (
        P(by_rows, None),
        P(by_rows),
        P(by_rows, None),
        P(by_rows),
        P(by_rows, None, None, None),
        P(),
        P(by_rows, None),
    )
    return jax.shard_map(
        shards,
        mesh=split,
        in_specs=placed,
        out_specs=(P(by_rows, None), P()),
        check_vma=False,
    )
```

```python
import jax
import jax.numpy as jnp
from jax import lax
from jax.experimental import pallas as pl
from jax.experimental.pallas import tpu as pltpu
from jax.sharding import Mesh, PartitionSpec as P

BF16 = jnp.bfloat16
F32 = jnp.float32
I32 = jnp.int32


def log2(n):
    assert n & (n - 1) == 0
    return n.bit_length() - 1


def iota(shape, dim):
    return lax.broadcasted_iota(I32, shape, dim)


def one_hot(mask):
    return jnp.where(mask, 1.0, 0.0).astype(BF16)


def dot(a, b):
    return jnp.dot(a, b, preferred_element_type=F32)


def dot_rows(a, b):
    return lax.dot_general(a, b, (((0,), (0,)), ((), ())), preferred_element_type=F32)


def call(body, outs, ins, name, mib, us, scratch=()):
    smem = pl.BlockSpec(memory_space=pltpu.SMEM)
    vmem = pl.BlockSpec(memory_space=pltpu.VMEM)
    return pl.pallas_call(
        body,
        out_shape=tuple(jax.ShapeDtypeStruct(s, d) for s, d in outs),
        in_specs=[smem if where == "s" else vmem for where, _ in ins],
        out_specs=tuple(vmem for _ in outs),
        scratch_shapes=list(scratch),
        compiler_params=pltpu.CompilerParams(vmem_limit_bytes=mib << 20),
        cost_estimate=pl.CostEstimate(flops=int(us * 1e9), bytes_accessed=0, transcendentals=0),
        name=name,
    )(*(value for _, value in ins))


class Sizes:
    def __init__(self, rows, tiles):
        self.grp, self.zz = lax.axis_size("grp"), lax.axis_size("zz")
        self.dom = 2 * self.zz
        self.rows, self.tiles = rows, tiles
        self.pair = rows // (self.grp * self.dom)
        self.piece = self.grp * self.pair
        self.per_grp = self.dom * self.pair


def column(row):
    n = row.shape[1]
    on = iota((n, n), 0) == iota((n, n), 1)
    return jnp.sum(jnp.where(on, row.astype(F32), 0.0), axis=1, keepdims=True).astype(I32)


def index_kernel(z, me_ref, order_ref, out_ref):
    rows = z.rows
    shift = log2(rows)
    order_r = order_ref[...]
    order_c = column(order_r)
    down, across = iota((rows, rows), 0), iota((rows, rows), 1)
    source_r, source_c = order_r >> shift, order_c >> shift
    same = jnp.where(source_c == source_r, 1.0, 0.0)
    rank_c = jnp.sum(jnp.where(across < down, same, 0.0), axis=1, keepdims=True).astype(I32)
    rank_r = jnp.sum(jnp.where(down < across, same, 0.0), axis=0, keepdims=True).astype(I32)
    row_c = (order_c & (rows - 1)).astype(F32)
    asked = jnp.where(source_c * z.pair + rank_c == across, row_c, 0.0)
    out_ref[0:1, :] = jnp.sum(asked, axis=0, keepdims=True).astype(I32)
    across_grp = (source_r >> log2(z.dom)) ^ me_ref[0]
    inner = source_r & (z.dom - 1)
    out_ref[1:2, :] = (inner * z.grp + across_grp) * z.pair + rank_r


def product_kernel(z, me_ref, features_ref, weight_ref, own_ref, other_ref):
    half = own_ref.shape[1]
    for flip, out in ((0, own_ref), (1, other_ref)):
        at = pl.multiple_of((me_ref[2] ^ flip) * half, half)
        out[...] = dot(features_ref[...], weight_ref[:, pl.ds(at, half)]).astype(BF16)


def asked_rows(z, me_ref, table):
    shape = (z.rows, table.shape[0])
    row = iota(shape, 0)
    s, n = row >> log2(z.per_grp), (row >> log2(z.pair)) & (z.dom - 1)
    k, rel = (me_ref[1] - (n >> 1)) & (z.zz - 1), (n & 1) ^ me_ref[2]
    spread = one_hot(iota(shape, 1) == ((s * 2 + rel) * z.zz + k) * 2)
    high = dot(spread, (table >> 4).astype(F32).astype(BF16))
    return high * 16.0 + dot(spread, (table & 15).astype(F32).astype(BF16))


def pick_of_source(z, me_ref, asked, k, rel):
    shape = (z.rows, z.rows)
    source = me_ref[0] * z.dom + ((me_ref[1] - k) & (z.zz - 1)) * 2 + (me_ref[2] ^ rel)
    mine = iota(shape, 1) == source * z.pair + (iota(shape, 0) & (z.pair - 1))
    wanted = jnp.sum(jnp.where(mine, asked, 0.0), axis=1, keepdims=True).astype(I32)
    return one_hot(iota(shape, 1) == wanted)


def select_own_kernel(z, me_ref, table_ref, own_ref, other_ref, features_ref, *outs):
    asked = asked_rows(z, me_ref, table_ref[...])
    for rel, part in enumerate((own_ref, other_ref)):
        pick = pick_of_source(z, me_ref, asked, 0, rel)
        got = dot(pick, part[...]).astype(BF16)
        for s in range(z.grp):
            outs[s][rel] = got[s * z.per_grp:(s + 1) * z.per_grp, :]
        if rel == 0:
            for s in range(z.grp):
                rows = pick[s * z.per_grp:(s + 1) * z.per_grp, :]
                outs[z.grp + s][...] = dot(rows, features_ref[...]).astype(BF16)


def picks_kernel(z, me_ref, table_ref, *outs):
    asked = asked_rows(z, me_ref, table_ref[...])
    for k in range(1, z.zz):
        for rel in range(2):
            outs[k - 1][rel] = pick_of_source(z, me_ref, asked, k, rel)


def select_kernel(z, pick_ref, own_ref, other_ref, *outs):
    for rel, part in enumerate((own_ref, other_ref)):
        got = dot(pick_ref[rel], part[...]).astype(BF16)
        for s in range(z.grp):
            outs[s][rel] = got[s * z.per_grp:(s + 1) * z.per_grp, :]


def place_kernel(z, me_ref, domain_ref, out_ref):
    @pl.loop(0, z.dom)
    def _(n):
        k, rel = (me_ref[1] - (n >> 1)) & (z.zz - 1), (n & 1) ^ me_ref[2]
        slot = domain_ref[pl.ds((rel * z.zz + k) * 2 + 1, 1), :]
        rank, at = slot & (z.pair - 1), slot >> log2(z.pair)
        s, at = at & (z.grp - 1), at >> log2(z.grp)
        k, rel = (me_ref[1] - (at >> 1)) & (z.zz - 1), (at & 1) ^ me_ref[2]
        slot = ((k * z.grp + s) * 2 + rel) * z.pair + rank
        out_ref[n] = one_hot(iota((z.rows, z.rows), 0) == slot)


def dense_kernel(cols_ref, vals_ref, out_ref, total):
    tiles, blocks, tile, _ = vals_ref.shape
    count = out_ref.shape[0]

    @pl.loop(0, tiles)
    def _(t):
        total[...] = jnp.zeros_like(total)
        for k in range(blocks):
            at = pl.multiple_of(cols_ref[t, k] * tile, tile)
            total[pl.ds(at, tile), :] += vals_ref[t, k].T.astype(F32)
        left = pl.multiple_of(t * tile, tile)
        out_ref[:, pl.ds(left, tile)] = total[pl.ds(0, count), :].astype(BF16)


def arrange_kernel(z, place_ref, dense_ref, *outs):
    turned, plain = outs[:z.zz], outs[z.zz:]

    @pl.loop(0, z.dom)
    def _(n):
        at = pl.multiple_of(n * z.rows, z.rows)
        part = dot(place_ref[n], dense_ref[pl.ds(at, z.rows), :]).astype(BF16)
        for k in range(z.zz):
            for p in range(2 * z.grp):
                first = (k * 2 * z.grp + p) * z.pair
                to = p * z.per_grp + n * z.pair
                if z.pair % 16 == 0:
                    to = pl.multiple_of(to, z.pair)
                    turned[k][pl.ds(to, z.pair), :] = part[first:first + z.pair, :]
                else:
                    turned[k][p, n] = part[first:first + z.pair, :]

    for out, source in zip(plain, turned):
        out[...] = source[...].reshape(out.shape[::-1]).T


def turn_kernel(*refs):
    out, height = refs[-1], refs[0].shape[0]
    for i, ref in enumerate(refs[:-1]):
        out[:, i * height:(i + 1) * height] = ref[...].T


def forward_kernel(z, first, last, *refs):
    plain, refs = refs[:2], refs[2:]
    pieces, refs = refs[:z.grp], refs[z.grp:]
    half = pieces[0].shape[2]
    rows = jnp.concatenate([ref[...].reshape(2 * z.per_grp, half) for ref in pieces], axis=0)
    agg = [dot(ref[...], rows) for ref in plain]
    if not first:
        agg = [part + ref[...] for part, ref in zip(agg, refs)]
        refs = refs[2:]
    if not last:
        for ref, part in zip(refs, agg):
            ref[...] = part
        return
    cots, turned, hiddens, grads, parts = (refs[2 * i:2 * i + 2] for i in range(5))
    for part, cot, hidden, grad in zip(agg, cots, hiddens, grads):
        sig = jax.nn.sigmoid(part)
        hidden[...] = (part * sig).astype(BF16)
        grad[...] = (cot[...].astype(F32) * (sig * (1.0 + part * (1.0 - sig)))).astype(BF16)
    back_into(parts, turned, grads)


def back_into(outs, turned, grads):
    size = outs[0].shape[0]
    for i, out in enumerate(outs):
        rows = pl.ds(i * size, size)
        value = dot(turned[0][rows, :], grads[0][...]) + dot(turned[1][rows, :], grads[1][...])
        out[...] = value.astype(out.dtype)


def back_kernel(turned_a, turned_b, grad_a, grad_b, *outs):
    back_into(outs, (turned_a, turned_b), (grad_a, grad_b))


def pass_kernel(mine_ref, come_ref, out_ref):
    out_ref[...] = (mine_ref[...] + come_ref[...].astype(F32)).astype(BF16)


def grad_kernel(z, me_ref, left_a, left_b, mine_a, mine_b, come_a, come_b, *refs):
    outs, whole = refs[:-1], refs[-1]
    grads = jnp.concatenate(
        [
            (mine[...] + come[...].astype(F32)).astype(BF16)
            for mine, come in ((mine_a, come_a), (mine_b, come_b))
        ],
        axis=0,
    )
    total = 0.0
    for rel, left in enumerate((left_a, left_b)):
        of_rel = [
            grads[(2 * s + rel) * z.per_grp:(2 * s + rel + 1) * z.per_grp] for s in range(z.grp)
        ]
        total = total + dot(left[...], jnp.concatenate(of_rel, axis=0))
    whole[...] = total.astype(BF16)
    share = whole.shape[0] // z.grp
    for s in range(z.grp):
        at = pl.multiple_of((me_ref[0] ^ s) * share, share)
        outs[s][...] = whole[pl.ds(at, share), :]


def sum_kernel(*refs):
    refs[-1][...] = sum(term[...].astype(F32) for term in refs[:-1]).astype(BF16)


def last_kernel(z, me_ref, *refs):
    pieces, out = refs[:-1], refs[-1]
    share, half = pieces[0].shape
    for rel in range(2):
        left = pl.multiple_of((me_ref[2] ^ rel) * half, half)
        for s in range(z.grp):
            at = pl.multiple_of((me_ref[0] ^ s) * share, share)
            out[pl.ds(at, share), pl.ds(left, half)] = pieces[rel * z.grp + s][...].astype(F32)


def arrange(z, place, dense, wide):
    inner = (wide, z.rows) if z.pair % 16 == 0 else (2 * z.grp, z.dom, z.pair, z.rows)
    got = call(
        lambda *refs: arrange_kernel(z, *refs),
        [(inner, BF16)] * z.zz + [((z.rows, wide), BF16)] * z.zz,
        [("v", place), ("v", dense)],
        "arrange", 32, 4,
    )
    return [part.reshape(wide, z.rows) for part in got[:z.zz]] + list(got[z.zz:])


def shards(features, node_order, block_cols, block_count, block_vals, weight, cotangent):
    rows, width_in = features.shape
    hidden_units = weight.shape[1]
    half = hidden_units // 2
    tiles, blocks, tile = block_vals.shape[0], block_vals.shape[1], block_vals.shape[-1]
    z = Sizes(rows, tiles)
    at_grp, at_zz, core = lax.axis_index("grp"), lax.axis_index("zz"), lax.axis_index("core")
    me = jnp.stack([at_grp, at_zz, core]).astype(I32)

    def to_core(x):
        return lax.ppermute(x, "core", [(0, 1), (1, 0)])

    def to_grp(x, s):
        return lax.ppermute(x, "grp", [(i, i ^ s) for i in range(z.grp)]) if s else x

    def to_zz(x, k):
        return lax.ppermute(x, "zz", [(i, (i + k) % z.zz) for i in range(z.zz)]) if k else x

    (index,) = call(
        lambda *refs: index_kernel(z, *refs),
        [((2, rows), I32)],
        [("s", me), ("v", node_order.reshape(1, rows))],
        "index", 24, 1,
    )
    domain = jnp.concatenate([to_zz(index, k) for k in range(z.zz)], axis=0)
    domain = jnp.concatenate([domain, to_core(domain)], axis=0)
    table = jnp.concatenate([to_grp(domain, s) for s in range(z.grp)], axis=0)

    own, other = call(
        lambda *refs: product_kernel(z, *refs),
        [((rows, half), BF16)] * 2,
        [("s", me), ("v", features), ("v", weight)],
        "product", 16, 1.5,
    )
    ring = [[own, to_core(other)]]
    for k in range(1, z.zz):
        ring.append([to_zz(part, 1) for part in ring[-1]])

    vals_b = to_core(block_vals)
    cot_a = lax.dynamic_slice_in_dim(cotangent, core * half, half, axis=1)
    cot_b = to_core(lax.dynamic_slice_in_dim(cotangent, (1 - core) * half, half, axis=1))
    live = iota((tiles, blocks), 1) < block_count[:, None]
    cols_a = jnp.where(live, block_cols, z.dom * tiles)
    cols_b = to_core(cols_a)

    pieces = [((2, z.per_grp, half), BF16)] * z.grp
    got = call(
        lambda *refs: select_own_kernel(z, *refs),
        pieces + [((z.per_grp, width_in), BF16)] * z.grp,
        [("s", me), ("v", table), ("v", ring[0][0]), ("v", ring[0][1]), ("v", features)],
        "select_own", 24, 2.5,
    )
    picked = got[z.grp:]
    y = [[to_grp(got[s], s) for s in range(z.grp)]]
    picks = call(
        lambda *refs: picks_kernel(z, *refs),
        [((2, rows, rows), BF16)] * (z.zz - 1),
        [("s", me), ("v", table)],
        "picks", 24, 2.5,
    )
    for k in range(1, z.zz):
        got = call(
            lambda *refs: select_kernel(z, *refs), pieces,
            [("v", picks[k - 1]), ("v", ring[k][0]), ("v", ring[k][1])],
            "select", 16, 0.5,
        )
        y.append([to_grp(got[s], s) for s in range(z.grp)])

    (place,) = call(
        lambda *refs: place_kernel(z, *refs),
        [((z.dom, rows, rows), BF16)],
        [("s", me), ("v", domain)],
        "place", 16, 1.5,
    )
    wide = 2 * z.grp * z.per_grp
    turned, plain = [], []
    for cols, vals in ((cols_a, block_vals), (cols_b, vals_b)):
        (dense,) = call(
            dense_kernel,
            [((z.dom * rows, rows), BF16)],
            [("s", cols), ("v", vals)],
            "dense", 24, 2.5,
            (pltpu.VMEM((z.dom * rows + tile, tile), F32),),
        )
        got = arrange(z, place, dense, wide)
        turned.append(got[:z.zz])
        plain.append(got[z.zz:])

    agg = []
    for k in range(z.zz):
        ins = [("v", plain[0][k]), ("v", plain[1][k])] + [("v", part) for part in y[k]]
        ins += [("v", part) for part in agg]
        outs = [((rows, half), F32)] * 2
        last = k == z.zz - 1
        if last:
            ins += [("v", part) for part in (cot_a, cot_b, turned[0][k], turned[1][k])]
            outs = [((rows, half), BF16)] * 4 + [((wide // 2, half), BF16)] * 2
        agg = call(
            lambda *refs, k=k, last=last: forward_kernel(z, k == 0, last, *refs),
            outs, ins, "forward", 24, 3 if last else 1,
        )
    hidden_a, hidden_b, grad_a, grad_b = agg[:4]
    came = agg[4:]

    came, picked, hidden_b = lax.optimization_barrier((came, picked, hidden_b))
    come = to_core(hidden_b)
    for k in range(z.zz - 2, -1, -1):
        came = [to_zz(part, -1) for part in came]
        mine = call(
            back_kernel,
            [((wide // 2, half), F32)] * 2,
            [("v", part) for part in (turned[0][k], turned[1][k], grad_a, grad_b)],
            "back", 16, 1,
        )
        if k:
            came = [
                call(
                    pass_kernel, [((wide // 2, half), BF16)], [("v", part), ("v", moved)],
                    "pass", 16, 0.5,
                )[0]
                for part, moved in zip(mine, came)
            ]
    held = [to_grp(picked[s], s) for s in range(z.grp)]
    (held,) = call(
        turn_kernel, [((width_in, rows), BF16)], [("v", part) for part in held], "turn", 16, 1
    )
    held_b = to_core(held)
    first = core == 0
    hidden = jnp.concatenate(
        [jnp.where(first, hidden_a, come), jnp.where(first, come, hidden_a)], axis=1
    )

    share = width_in // z.grp
    terms = call(
        lambda *refs: grad_kernel(z, *refs),
        [((share, half), BF16)] * z.grp,
        [("s", me), ("v", held), ("v", held_b)] + [("v", part) for part in (*mine, *came)],
        "grad", 16, 1.5,
        (pltpu.VMEM((width_in, half), BF16),),
    )

    def total_of(parts):
        return call(
            sum_kernel, [((share, half), BF16)], [("v", part) for part in parts], "sum", 16, 0.5
        )[0]

    mine = total_of([to_grp(terms[s], s) for s in range(z.grp)])
    step = 1
    while step < z.zz:
        mine = total_of(
            [mine, lax.ppermute(mine, "zz", [(i, i ^ step) for i in range(z.zz)])]
        )
        step *= 2
    mine = [to_grp(mine, s) for s in range(z.grp)]
    (grad_weight,) = call(
        lambda *refs: last_kernel(z, *refs),
        [((width_in, hidden_units), F32)],
        [("s", me)] + [("v", part) for part in mine + [to_core(part) for part in mine]],
        "last", 16, 2,
    )
    return hidden, grad_weight


def solution(mesh):
    n_grp, n_dom = mesh.shape["grp"], mesh.shape["dom"]
    split = Mesh(mesh.devices.reshape(n_grp, n_dom // 2, 2), ("grp", "zz", "core"))
    by_rows = ("grp", "zz", "core")
    placed = (
        P(by_rows, None),
        P(by_rows),
        P(by_rows, None),
        P(by_rows),
        P(by_rows, None, None, None),
        P(),
        P(by_rows, None),
    )
    return jax.shard_map(
        shards,
        mesh=split,
        in_specs=placed,
        out_specs=(P(by_rows, None), P()),
        check_vma=False,
    )
```

```python
import jax
import jax.numpy as jnp
from jax import lax
from jax.experimental import pallas as pl
from jax.experimental.pallas import tpu as pltpu
from jax.sharding import Mesh, PartitionSpec as P

BF16 = jnp.bfloat16
F32 = jnp.float32
I32 = jnp.int32


def log2(n):
    assert n & (n - 1) == 0
    return n.bit_length() - 1


def iota(shape, dim):
    return lax.broadcasted_iota(I32, shape, dim)


def one_hot(mask):
    return jnp.where(mask, 1.0, 0.0).astype(BF16)


def dot(a, b):
    return jnp.dot(a, b, preferred_element_type=F32)


def dot_rows(a, b):
    return lax.dot_general(a, b, (((0,), (0,)), ((), ())), preferred_element_type=F32)


def call(body, outs, ins, name, us, scratch=()):
    smem = pl.BlockSpec(memory_space=pltpu.SMEM)
    vmem = pl.BlockSpec(memory_space=pltpu.VMEM)
    arrays = [jax.ShapeDtypeStruct(s, d) for s, d in outs] + [value for _, value in ins]
    size = sum(a.size * a.dtype.itemsize for a in arrays + [m.get_array_aval() for m in scratch])
    return pl.pallas_call(
        body,
        out_shape=tuple(jax.ShapeDtypeStruct(s, d) for s, d in outs),
        in_specs=[smem if where == "s" else vmem for where, _ in ins],
        out_specs=tuple(vmem for _ in outs),
        scratch_shapes=list(scratch),
        compiler_params=pltpu.CompilerParams(vmem_limit_bytes=size + (6 << 20)),
        cost_estimate=pl.CostEstimate(flops=int(us * 1e9), bytes_accessed=0, transcendentals=0),
        name=name,
    )(*(value for _, value in ins))


class Sizes:
    def __init__(self, rows, tiles):
        self.grp, self.zz = lax.axis_size("grp"), lax.axis_size("zz")
        self.dom = 2 * self.zz
        self.rows, self.tiles = rows, tiles
        self.pair = rows // (self.grp * self.dom)
        self.piece = self.grp * self.pair
        self.per_grp = self.dom * self.pair


def column(row):
    n = row.shape[1]
    on = iota((n, n), 0) == iota((n, n), 1)
    return jnp.sum(jnp.where(on, row.astype(F32), 0.0), axis=1, keepdims=True).astype(I32)


def index_kernel(z, me_ref, order_ref, want_ref, slot_ref):
    rows = z.rows
    shift = log2(rows)
    order_r = order_ref[...]
    order_c = column(order_r)
    down, across = iota((rows, rows), 0), iota((rows, rows), 1)
    source_r, source_c = order_r >> shift, order_c >> shift
    row_c = order_c & (rows - 1)
    same = jnp.where(source_c == source_r, 1.0, 0.0)
    rank_c = jnp.sum(jnp.where(across < down, same, 0.0), axis=1, keepdims=True).astype(I32)
    rank_r = jnp.sum(jnp.where(down < across, same, 0.0), axis=0, keepdims=True).astype(I32)
    owner = one_hot(iota((z.grp * z.dom, rows), 0) == source_r)
    at_rank = iota((rows, z.pair), 1) == rank_c
    high = jnp.where(at_rank, (row_c >> 4).astype(F32), 0.0).astype(BF16)
    low = jnp.where(at_rank, (row_c & 15).astype(F32), 0.0).astype(BF16)
    want_ref[...] = (dot(owner, high) * 16.0 + dot(owner, low)).astype(I32)
    across_grp = (source_r >> log2(z.dom)) ^ me_ref[0]
    inner = source_r & (z.dom - 1)
    slot_ref[...] = (inner * z.grp + across_grp) * z.pair + rank_r


def send_kernel(z, me_ref, asked_ref, features_ref, weight_ref, *refs):
    picked_refs, out_refs, rows_ref = refs[:z.grp], refs[z.grp:-1], refs[-1]
    asked = asked_ref[...]
    devices, half = asked.shape[0], out_refs[0].shape[2]
    row, device = iota((z.rows, devices), 0), iota((z.rows, devices), 1)
    asker = (row >> log2(z.pair)) ^ (me_ref[0] * z.dom)
    spread = one_hot(device == asker)
    high = dot(spread, (asked >> 4).astype(F32).astype(BF16))
    low = dot(spread, (asked & 15).astype(F32).astype(BF16))
    mine = iota((z.rows, z.pair), 1) == (iota((z.rows, z.pair), 0) & (z.pair - 1))
    wanted = jnp.sum(jnp.where(mine, high * 16.0 + low, 0.0), axis=1, keepdims=True).astype(I32)
    pick = one_hot(iota((z.rows, z.rows), 1) == wanted)
    rows_ref[...] = dot(pick, features_ref[...]).astype(BF16)
    for flip in range(2):
        at = pl.multiple_of((me_ref[2] ^ flip) * half, half)
        product = dot(rows_ref[...], weight_ref[:, pl.ds(at, half)]).astype(BF16)
        for s in range(z.grp):
            out_refs[s][flip] = product[s * z.per_grp:(s + 1) * z.per_grp, :]
    for s in range(z.grp):
        picked_refs[s][...] = rows_ref[s * z.per_grp:(s + 1) * z.per_grp, :]


def pack_kernel(z, *refs):
    ins, outs = refs[:z.grp], refs[z.grp:]
    for flip in range(2):
        for s in range(z.grp):
            outs[flip][s * z.per_grp:(s + 1) * z.per_grp, :] = ins[s][flip]


def place_kernel(z, me_ref, domain_ref, out_ref):
    @pl.loop(0, z.dom)
    def _(n):
        k, rel = (me_ref[1] - (n >> 1)) & (z.zz - 1), (n & 1) ^ me_ref[2]
        slot = domain_ref[pl.ds(rel * z.zz + k, 1), :]
        rank, at = slot & (z.pair - 1), slot >> log2(z.pair)
        s, at = at & (z.grp - 1), at >> log2(z.grp)
        k, rel = (me_ref[1] - (at >> 1)) & (z.zz - 1), (at & 1) ^ me_ref[2]
        slot = ((k * 2 + rel) * z.grp + s) * z.pair + rank
        out_ref[n] = one_hot(iota((z.rows, z.rows), 0) == slot)


def dense_kernel(cols_ref, vals_ref, out_ref, total):
    tiles, blocks, tile, _ = vals_ref.shape
    count = out_ref.shape[0]

    @pl.loop(0, tiles)
    def _(t):
        total[...] = jnp.zeros_like(total)
        for k in range(blocks):
            at = pl.multiple_of(cols_ref[t, k] * tile, tile)
            total[pl.ds(at, tile), :] += vals_ref[t, k].T.astype(F32)
        left = pl.multiple_of(t * tile, tile)
        out_ref[:, pl.ds(left, tile)] = total[pl.ds(0, count), :].astype(BF16)


def arrange_kernel(z, place_ref, dense_ref, *outs):
    turned, plain = outs[:z.zz], outs[z.zz:]

    @pl.loop(0, z.dom)
    def _(n):
        at = pl.multiple_of(n * z.rows, z.rows)
        part = dot(place_ref[n], dense_ref[pl.ds(at, z.rows), :]).astype(BF16)
        for k in range(z.zz):
            for p in range(2 * z.grp):
                first = (k * 2 * z.grp + p) * z.pair
                to = p * z.per_grp + n * z.pair
                if z.pair % 16 == 0:
                    to = pl.multiple_of(to, z.pair)
                    turned[k][pl.ds(to, z.pair), :] = part[first:first + z.pair, :]
                else:
                    turned[k][p, n] = part[first:first + z.pair, :]

    for out, source in zip(plain, turned):
        out[...] = source[...].reshape(out.shape[::-1]).T


def turn_kernel(*refs):
    out, height = refs[-1], refs[0].shape[0]
    for i, ref in enumerate(refs[:-1]):
        out[:, i * height:(i + 1) * height] = ref[...].T


def forward_kernel(z, first, last, *refs):
    plain, refs = refs[:2], refs[2:]
    pieces, refs = refs[:2], refs[2:]
    rows = jnp.concatenate([ref[...] for ref in pieces], axis=0)
    agg = [dot(ref[...], rows) for ref in plain]
    if not first:
        agg = [part + ref[...] for part, ref in zip(agg, refs)]
        refs = refs[2:]
    if not last:
        for ref, part in zip(refs, agg):
            ref[...] = part
        return
    cots, turned, hiddens, grads, parts = (refs[2 * i:2 * i + 2] for i in range(5))
    for part, cot, hidden, grad in zip(agg, cots, hiddens, grads):
        sig = jax.nn.sigmoid(part)
        hidden[...] = (part * sig).astype(BF16)
        grad[...] = (cot[...].astype(F32) * (sig * (1.0 + part * (1.0 - sig)))).astype(BF16)
    back_into(parts, turned, grads)


def back_into(outs, turned, grads):
    size = outs[0].shape[0]
    for i, out in enumerate(outs):
        rows = pl.ds(i * size, size)
        value = dot(turned[0][rows, :], grads[0][...]) + dot(turned[1][rows, :], grads[1][...])
        out[...] = value.astype(out.dtype)


def back_kernel(turned_a, turned_b, grad_a, grad_b, *outs):
    back_into(outs, (turned_a, turned_b), (grad_a, grad_b))


def pass_kernel(mine_ref, come_ref, out_ref):
    out_ref[...] = (mine_ref[...] + come_ref[...].astype(F32)).astype(BF16)


def grad_kernel(z, me_ref, left_a, left_b, mine_a, mine_b, come_a, come_b, *refs):
    outs, whole = refs[:-1], refs[-1]
    grads = [
        (mine[...] + come[...].astype(F32)).astype(BF16)
        for mine, come in ((mine_a, come_a), (mine_b, come_b))
    ]
    whole[...] = (dot(left_a[...], grads[0]) + dot(left_b[...], grads[1])).astype(BF16)
    share = whole.shape[0] // z.grp
    for s in range(z.grp):
        at = pl.multiple_of((me_ref[0] ^ s) * share, share)
        outs[s][...] = whole[pl.ds(at, share), :]


def sum_kernel(*refs):
    refs[-1][...] = sum(term[...].astype(F32) for term in refs[:-1]).astype(BF16)


def last_kernel(z, me_ref, *refs):
    pieces, out = refs[:-1], refs[-1]
    share, half = pieces[0].shape
    for rel in range(2):
        left = pl.multiple_of((me_ref[2] ^ rel) * half, half)
        for s in range(z.grp):
            at = pl.multiple_of((me_ref[0] ^ s) * share, share)
            out[pl.ds(at, share), pl.ds(left, half)] = pieces[rel * z.grp + s][...].astype(F32)


def arrange(z, place, dense, wide):
    inner = (wide, z.rows) if z.pair % 16 == 0 else (2 * z.grp, z.dom, z.pair, z.rows)
    got = call(
        lambda *refs: arrange_kernel(z, *refs),
        [(inner, BF16)] * z.zz + [((z.rows, wide), BF16)] * z.zz,
        [("v", place), ("v", dense)],
        "arrange", 4,
    )
    return [part.reshape(wide, z.rows) for part in got[:z.zz]] + list(got[z.zz:])


def shards(features, node_order, block_cols, block_count, block_vals, weight, cotangent):
    rows, width_in = features.shape
    hidden_units = weight.shape[1]
    half = hidden_units // 2
    tiles, blocks, tile = block_vals.shape[0], block_vals.shape[1], block_vals.shape[-1]
    z = Sizes(rows, tiles)
    at_grp, at_zz, core = lax.axis_index("grp"), lax.axis_index("zz"), lax.axis_index("core")
    me = jnp.stack([at_grp, at_zz, core]).astype(I32)

    def to_core(x):
        return lax.ppermute(x, "core", [(0, 1), (1, 0)])

    def to_grp(x, s):
        return lax.ppermute(x, "grp", [(i, i ^ s) for i in range(z.grp)]) if s else x

    def to_zz(x, k):
        return lax.ppermute(x, "zz", [(i, (i + k) % z.zz) for i in range(z.zz)]) if k else x

    want, slot = call(
        lambda *refs: index_kernel(z, *refs),
        [((z.grp * z.dom, z.pair), I32), ((1, rows), I32)],
        [("s", me), ("v", node_order.reshape(1, rows))],
        "index", 1,
    )
    asked = lax.all_to_all(want, ("grp", "zz", "core"), split_axis=0, concat_axis=0, tiled=True)
    domain = jnp.concatenate([to_zz(slot, k) for k in range(z.zz)], axis=0)
    domain = jnp.concatenate([domain, to_core(domain)], axis=0)

    vals_b = to_core(block_vals)
    cot_a = lax.dynamic_slice_in_dim(cotangent, core * half, half, axis=1)
    cot_b = to_core(lax.dynamic_slice_in_dim(cotangent, (1 - core) * half, half, axis=1))
    live = iota((tiles, blocks), 1) < block_count[:, None]
    cols_a = jnp.where(live, block_cols, z.dom * tiles)
    cols_b = to_core(cols_a)

    got = call(
        lambda *refs: send_kernel(z, *refs),
        [((z.per_grp, width_in), BF16)] * z.grp + [((2, z.per_grp, half), BF16)] * z.grp,
        [("s", me), ("v", asked), ("v", features), ("v", weight)],
        "send", 2,
        (pltpu.VMEM((rows, width_in), BF16),),
    )
    picked = got[:z.grp]
    came = [to_grp(got[z.grp + s], s) for s in range(z.grp)]

    dense = [
        call(
            dense_kernel,
            [((z.dom * rows, rows), BF16)],
            [("s", cols), ("v", vals)],
            "dense", 2.5,
            (pltpu.VMEM((z.dom * rows + tile, tile), F32),),
        )[0]
        for cols, vals in ((cols_a, block_vals), (cols_b, vals_b))
    ]
    came, dense, domain, cot_b = lax.optimization_barrier((came, dense, domain, cot_b))

    own, other = call(
        lambda *refs: pack_kernel(z, *refs),
        [((rows, half), BF16)] * 2,
        [("v", part) for part in came],
        "pack", 0.5,
    )
    ring = [[own, to_core(other)]]
    for k in range(1, z.zz):
        ring.append([to_zz(part, 1) for part in ring[-1]])
        if k == 1:
            ring[1], picked = lax.optimization_barrier((ring[1], picked))

    held = [to_grp(picked[s], s) for s in range(z.grp)]
    (held,) = call(
        turn_kernel, [((width_in, rows), BF16)], [("v", part) for part in held], "turn", 0.5
    )
    held_b = to_core(held)

    (place,) = call(
        lambda *refs: place_kernel(z, *refs),
        [((z.dom, rows, rows), BF16)],
        [("s", me), ("v", domain)],
        "place", 1.5,
    )
    wide = 2 * z.grp * z.per_grp
    turned, plain = [], []
    for matrix in dense:
        got = arrange(z, place, matrix, wide)
        turned.append(got[:z.zz])
        plain.append(got[z.zz:])

    agg = []
    for k in range(z.zz):
        ins = [("v", plain[0][k]), ("v", plain[1][k])] + [("v", part) for part in ring[k]]
        ins += [("v", part) for part in agg]
        outs = [((rows, half), F32)] * 2
        last = k == z.zz - 1
        if last:
            ins += [("v", part) for part in (cot_a, cot_b, turned[0][k], turned[1][k])]
            outs = [((rows, half), BF16)] * 4 + [((wide // 2, half), BF16)] * 2
        agg = call(
            lambda *refs, k=k, last=last: forward_kernel(z, k == 0, last, *refs),
            outs, ins, "forward", 3 if last else 1,
        )
    hidden_a, hidden_b, grad_a, grad_b = agg[:4]
    came = agg[4:]

    for k in range(z.zz - 2, -1, -1):
        came = [to_zz(part, -1) for part in came]
        if k == z.zz - 2:
            came, hidden_b = lax.optimization_barrier((came, hidden_b))
            come = to_core(hidden_b)
        mine = call(
            back_kernel,
            [((wide // 2, half), F32)] * 2,
            [("v", part) for part in (turned[0][k], turned[1][k], grad_a, grad_b)],
            "back", 1,
        )
        if k:
            came = [
                call(
                    pass_kernel, [((wide // 2, half), BF16)], [("v", part), ("v", moved)],
                    "pass", 0.5,
                )[0]
                for part, moved in zip(mine, came)
            ]
    first = core == 0
    hidden = jnp.concatenate(
        [jnp.where(first, hidden_a, come), jnp.where(first, come, hidden_a)], axis=1
    )

    share = width_in // z.grp
    terms = call(
        lambda *refs: grad_kernel(z, *refs),
        [((share, half), BF16)] * z.grp,
        [("s", me), ("v", held), ("v", held_b)] + [("v", part) for part in (*mine, *came)],
        "grad", 1.5,
        (pltpu.VMEM((width_in, half), BF16),),
    )

    def total_of(parts):
        return call(
            sum_kernel, [((share, half), BF16)], [("v", part) for part in parts], "sum", 0.5
        )[0]

    mine = total_of([to_grp(terms[s], s) for s in range(z.grp)])
    step = 1
    while step < z.zz:
        mine = total_of(
            [mine, lax.ppermute(mine, "zz", [(i, i ^ step) for i in range(z.zz)])]
        )
        step *= 2
    mine = [to_grp(mine, s) for s in range(z.grp)]
    (grad_weight,) = call(
        lambda *refs: last_kernel(z, *refs),
        [((width_in, hidden_units), F32)],
        [("s", me)] + [("v", part) for part in mine + [to_core(part) for part in mine]],
        "last", 2,
    )
    return hidden, grad_weight


def solution(mesh):
    n_grp, n_dom = mesh.shape["grp"], mesh.shape["dom"]
    split = Mesh(mesh.devices.reshape(n_grp, n_dom // 2, 2), ("grp", "zz", "core"))
    by_rows = ("grp", "zz", "core")
    placed = (
        P(by_rows, None),
        P(by_rows),
        P(by_rows, None),
        P(by_rows),
        P(by_rows, None, None, None),
        P(),
        P(by_rows, None),
    )
    return jax.shard_map(
        shards,
        mesh=split,
        in_specs=placed,
        out_specs=(P(by_rows, None), P()),
        check_vma=False,
    )
```

```python
import jax
import jax.numpy as jnp
from jax import lax
from jax.experimental import pallas as pl
from jax.experimental.pallas import tpu as pltpu
from jax.sharding import Mesh, PartitionSpec as P

BF16 = jnp.bfloat16
F32 = jnp.float32
I32 = jnp.int32


def log2(n):
    assert n & (n - 1) == 0
    return n.bit_length() - 1


def iota(shape, dim):
    return lax.broadcasted_iota(I32, shape, dim)


def one_hot(mask):
    return jnp.where(mask, 1.0, 0.0).astype(BF16)


def dot(a, b):
    return jnp.dot(a, b, preferred_element_type=F32)


def dot_rows(a, b):
    return lax.dot_general(a, b, (((0,), (0,)), ((), ())), preferred_element_type=F32)


def call(body, outs, ins, name, us, scratch=()):
    smem = pl.BlockSpec(memory_space=pltpu.SMEM)
    vmem = pl.BlockSpec(memory_space=pltpu.VMEM)
    arrays = [jax.ShapeDtypeStruct(s, d) for s, d in outs] + [value for _, value in ins]
    size = sum(a.size * a.dtype.itemsize for a in arrays + [m.get_array_aval() for m in scratch])
    return pl.pallas_call(
        body,
        out_shape=tuple(jax.ShapeDtypeStruct(s, d) for s, d in outs),
        in_specs=[smem if where == "s" else vmem for where, _ in ins],
        out_specs=tuple(vmem for _ in outs),
        scratch_shapes=list(scratch),
        compiler_params=pltpu.CompilerParams(vmem_limit_bytes=size + (6 << 20)),
        cost_estimate=pl.CostEstimate(flops=int(us * 1e9), bytes_accessed=0, transcendentals=0),
        name=name,
    )(*(value for _, value in ins))


class Sizes:
    def __init__(self, rows, tiles):
        self.grp, self.zz = lax.axis_size("grp"), lax.axis_size("zz")
        self.dom = 2 * self.zz
        self.rows, self.tiles = rows, tiles
        self.pair = rows // (self.grp * self.dom)
        self.piece = self.grp * self.pair
        self.per_grp = self.dom * self.pair
        assert rows // 128 < 8 and self.pair <= 128


def column(row):
    n = row.shape[1]
    on = iota((n, n), 0) == iota((n, n), 1)
    return jnp.sum(jnp.where(on, row.astype(F32), 0.0), axis=1, keepdims=True).astype(I32)


def index_kernel(z, me_ref, order_ref, out_ref):
    rows = z.rows
    shift = log2(rows)
    order_r = order_ref[...]
    order_c = column(order_r)
    down, across = iota((rows, rows), 0), iota((rows, rows), 1)
    source_r, source_c = order_r >> shift, order_c >> shift
    row_c = order_c & (rows - 1)
    same = jnp.where(source_c == source_r, 1.0, 0.0)
    rank_c = jnp.sum(jnp.where(across < down, same, 0.0), axis=1, keepdims=True).astype(I32)
    rank_r = jnp.sum(jnp.where(down < across, same, 0.0), axis=0, keepdims=True).astype(I32)
    owner = one_hot(iota((z.grp * z.dom, rows), 0) == source_r)
    at_rank = iota((rows, z.pair), 1) == rank_c
    high = jnp.where(at_rank, (row_c >> 4).astype(F32), 0.0).astype(BF16)
    low = jnp.where(at_rank, (row_c & 15).astype(F32), 0.0).astype(BF16)
    want = (dot(owner, high) * 16.0 + dot(owner, low)).astype(I32)
    out_ref[...] = jnp.zeros_like(out_ref)
    for d in range(z.grp * z.dom):
        out_ref[d, 0:1, 0:z.pair] = want[d:d + 1, :]
    across_grp = (source_r >> log2(z.dom)) ^ me_ref[0]
    inner = source_r & (z.dom - 1)
    slot = (inner * z.grp + across_grp) * z.pair + rank_r
    for i in range(rows // 128):
        lanes = slot[:, i * 128:(i + 1) * 128]
        out_ref[:, 1 + i:2 + i, :] = jnp.broadcast_to(lanes[None], (z.grp * z.dom, 1, 128))


def product_kernel(z, me_ref, features_ref, weight_ref, *outs):
    half = outs[0].shape[1]
    for flip, out in enumerate(outs):
        at = pl.multiple_of((me_ref[2] ^ flip) * half, half)
        out[...] = dot(features_ref[...], weight_ref[:, pl.ds(at, half)]).astype(BF16)


def send_kernel(z, me_ref, message_ref, own_ref, other_ref, pick_ref, *outs):
    devices, height, width = message_ref.shape
    message = message_ref[...].reshape(devices * height, width)
    shape = (z.rows, devices * height)
    asker = (iota(shape, 0) >> log2(z.pair)) ^ (me_ref[0] * z.dom)
    spread = one_hot(iota(shape, 1) == asker * height)
    high = dot(spread, (message >> 4).astype(F32).astype(BF16))
    low = dot(spread, (message & 15).astype(F32).astype(BF16))
    mine = iota((z.rows, width), 1) == (iota((z.rows, width), 0) & (z.pair - 1))
    wanted = jnp.sum(jnp.where(mine, high * 16.0 + low, 0.0), axis=1, keepdims=True).astype(I32)
    pick_ref[...] = one_hot(iota((z.rows, z.rows), 1) == wanted)
    for flip, product in enumerate((own_ref, other_ref)):
        got = dot(pick_ref[...], product[...]).astype(BF16)
        for s in range(z.grp):
            outs[s][flip] = got[s * z.per_grp:(s + 1) * z.per_grp, :]


def rows_kernel(z, pick_ref, features_ref, *outs):
    for s, out in enumerate(outs):
        pick = pick_ref[s * z.per_grp:(s + 1) * z.per_grp, :]
        out[...] = dot(pick, features_ref[...]).astype(BF16)


def pack_kernel(z, *refs):
    ins, outs = refs[:z.grp], refs[z.grp:]
    for flip in range(2):
        for s in range(z.grp):
            outs[flip][s * z.per_grp:(s + 1) * z.per_grp, :] = ins[s][flip]


def place_kernel(z, me_ref, message_ref, out_ref):
    @pl.loop(0, z.dom)
    def _(n):
        message = message_ref[me_ref[0] * z.dom + n]
        slot = jnp.concatenate([message[1 + i:2 + i, :] for i in range(z.rows // 128)], axis=1)
        rank, at = slot & (z.pair - 1), slot >> log2(z.pair)
        s, at = at & (z.grp - 1), at >> log2(z.grp)
        k, rel = (me_ref[1] - (at >> 1)) & (z.zz - 1), (at & 1) ^ me_ref[2]
        slot = ((k * 2 + rel) * z.grp + s) * z.pair + rank
        out_ref[n] = one_hot(iota((z.rows, z.rows), 0) == slot)


def dense_kernel(cols_ref, vals_ref, out_ref, total):
    tiles, blocks, tile, _ = vals_ref.shape
    count = out_ref.shape[0]

    @pl.loop(0, tiles)
    def _(t):
        total[...] = jnp.zeros_like(total)
        for k in range(blocks):
            at = pl.multiple_of(cols_ref[t, k] * tile, tile)
            total[pl.ds(at, tile), :] += vals_ref[t, k].T.astype(F32)
        left = pl.multiple_of(t * tile, tile)
        out_ref[:, pl.ds(left, tile)] = total[pl.ds(0, count), :].astype(BF16)


def arrange_kernel(z, place_ref, dense_ref, *outs):
    turned, plain = outs[:z.zz], outs[z.zz:]

    @pl.loop(0, z.dom)
    def _(n):
        at = pl.multiple_of(n * z.rows, z.rows)
        part = dot(place_ref[n], dense_ref[pl.ds(at, z.rows), :]).astype(BF16)
        for k in range(z.zz):
            for p in range(2 * z.grp):
                first = (k * 2 * z.grp + p) * z.pair
                to = p * z.per_grp + n * z.pair
                if z.pair % 16 == 0:
                    to = pl.multiple_of(to, z.pair)
                    turned[k][pl.ds(to, z.pair), :] = part[first:first + z.pair, :]
                else:
                    turned[k][p, n] = part[first:first + z.pair, :]

    for out, source in zip(plain, turned):
        out[...] = source[...].reshape(out.shape[::-1]).T


def turn_kernel(*refs):
    out, height = refs[-1], refs[0].shape[0]
    for i, ref in enumerate(refs[:-1]):
        out[:, i * height:(i + 1) * height] = ref[...].T


def forward_kernel(z, first, last, *refs):
    plain, refs = refs[:2], refs[2:]
    pieces, refs = refs[:2], refs[2:]
    rows = jnp.concatenate([ref[...] for ref in pieces], axis=0)
    agg = [dot(ref[...], rows) for ref in plain]
    if not first:
        agg = [part + ref[...] for part, ref in zip(agg, refs)]
        refs = refs[2:]
    if not last:
        for ref, part in zip(refs, agg):
            ref[...] = part
        return
    cots, turned, hiddens, grads, parts = (refs[2 * i:2 * i + 2] for i in range(5))
    for part, cot, hidden, grad in zip(agg, cots, hiddens, grads):
        sig = jax.nn.sigmoid(part)
        hidden[...] = (part * sig).astype(BF16)
        grad[...] = (cot[...].astype(F32) * (sig * (1.0 + part * (1.0 - sig)))).astype(BF16)
    back_into(parts, turned, grads)


def back_into(outs, turned, grads):
    size = outs[0].shape[0]
    for i, out in enumerate(outs):
        rows = pl.ds(i * size, size)
        value = dot(turned[0][rows, :], grads[0][...]) + dot(turned[1][rows, :], grads[1][...])
        out[...] = value.astype(out.dtype)


def back_kernel(turned_a, turned_b, grad_a, grad_b, *outs):
    back_into(outs, (turned_a, turned_b), (grad_a, grad_b))


def pass_kernel(mine_ref, come_ref, out_ref):
    out_ref[...] = (mine_ref[...] + come_ref[...].astype(F32)).astype(BF16)


def grad_kernel(z, me_ref, left_a, left_b, mine_a, mine_b, come_a, come_b, *refs):
    outs, whole = refs[:-1], refs[-1]
    grads = [
        (mine[...] + come[...].astype(F32)).astype(BF16)
        for mine, come in ((mine_a, come_a), (mine_b, come_b))
    ]
    whole[...] = (dot(left_a[...], grads[0]) + dot(left_b[...], grads[1])).astype(BF16)
    share = whole.shape[0] // z.grp
    for s in range(z.grp):
        at = pl.multiple_of((me_ref[0] ^ s) * share, share)
        outs[s][...] = whole[pl.ds(at, share), :]


def sum_kernel(*refs):
    refs[-1][...] = sum(term[...].astype(F32) for term in refs[:-1]).astype(BF16)


def last_kernel(z, me_ref, *refs):
    pieces, out = refs[:-1], refs[-1]
    share, half = pieces[0].shape
    for rel in range(2):
        left = pl.multiple_of((me_ref[2] ^ rel) * half, half)
        for s in range(z.grp):
            at = pl.multiple_of((me_ref[0] ^ s) * share, share)
            out[pl.ds(at, share), pl.ds(left, half)] = pieces[rel * z.grp + s][...].astype(F32)


def arrange(z, place, dense, wide):
    inner = (wide, z.rows) if z.pair % 16 == 0 else (2 * z.grp, z.dom, z.pair, z.rows)
    got = call(
        lambda *refs: arrange_kernel(z, *refs),
        [(inner, BF16)] * z.zz + [((z.rows, wide), BF16)] * z.zz,
        [("v", place), ("v", dense)],
        "arrange", 4,
    )
    return [part.reshape(wide, z.rows) for part in got[:z.zz]] + list(got[z.zz:])


def shards(features, node_order, block_cols, block_count, block_vals, weight, cotangent):
    rows, width_in = features.shape
    hidden_units = weight.shape[1]
    half = hidden_units // 2
    tiles, blocks, tile = block_vals.shape[0], block_vals.shape[1], block_vals.shape[-1]
    z = Sizes(rows, tiles)
    at_grp, at_zz, core = lax.axis_index("grp"), lax.axis_index("zz"), lax.axis_index("core")
    me = jnp.stack([at_grp, at_zz, core]).astype(I32)

    def to_core(x):
        return lax.ppermute(x, "core", [(0, 1), (1, 0)])

    def to_grp(x, s):
        return lax.ppermute(x, "grp", [(i, i ^ s) for i in range(z.grp)]) if s else x

    def to_zz(x, k):
        return lax.ppermute(x, "zz", [(i, (i + k) % z.zz) for i in range(z.zz)]) if k else x

    (message,) = call(
        lambda *refs: index_kernel(z, *refs),
        [((z.grp * z.dom, 8, 128), I32)],
        [("s", me), ("v", node_order.reshape(1, rows))],
        "index", 1,
    )
    message = lax.all_to_all(
        message, ("grp", "zz", "core"), split_axis=0, concat_axis=0, tiled=True
    )
    vals_b = to_core(block_vals)

    products = call(
        lambda *refs: product_kernel(z, *refs),
        [((rows, half), BF16)] * 2,
        [("s", me), ("v", features), ("v", weight)],
        "product", 1.5,
    )
    pick, *got = call(
        lambda *refs: send_kernel(z, *refs),
        [((rows, rows), BF16)] + [((2, z.per_grp, half), BF16)] * z.grp,
        [("s", me), ("v", message)] + [("v", part) for part in products],
        "send", 1.5,
    )
    got, message, cotangent, block_cols = lax.optimization_barrier(
        (got, message, cotangent, block_cols)
    )
    came = [to_grp(got[s], s) for s in range(z.grp)]

    live = iota((tiles, blocks), 1) < block_count[:, None]
    cols_a = jnp.where(live, block_cols, z.dom * tiles)
    cols_b = to_core(cols_a)
    cot_a = lax.dynamic_slice_in_dim(cotangent, core * half, half, axis=1)
    cot_b = to_core(lax.dynamic_slice_in_dim(cotangent, (1 - core) * half, half, axis=1))

    (place,) = call(
        lambda *refs: place_kernel(z, *refs),
        [((z.dom, rows, rows), BF16)],
        [("s", me), ("v", message)],
        "place", 1.5,
    )
    wide = 2 * z.grp * z.per_grp

    def arranged(cols, vals):
        (dense,) = call(
            dense_kernel,
            [((z.dom * rows, rows), BF16)],
            [("s", cols), ("v", vals)],
            "dense", 2.5,
            (pltpu.VMEM((z.dom * rows + tile, tile), F32),),
        )
        got = arrange(z, place, dense, wide)
        return got[:z.zz], got[z.zz:]

    turned_a, plain_a = arranged(cols_a, block_vals)
    came, plain_a = lax.optimization_barrier((came, plain_a))

    own, other = call(
        lambda *refs: pack_kernel(z, *refs),
        [((rows, half), BF16)] * 2,
        [("v", part) for part in came],
        "pack", 0.5,
    )
    ring = [[own, to_core(other)]]
    turned_b, plain_b = arranged(cols_b, vals_b)
    turned, plain = (turned_a, turned_b), (plain_a, plain_b)
    for k in range(1, z.zz):
        ring.append([to_zz(part, 1) for part in ring[-1]])
        if k == 1:
            ring[1][0], plain_b = lax.optimization_barrier((ring[1][0], plain_b))
            plain = (plain_a, plain_b)
        if k == 2:
            ring[2][0], pick = lax.optimization_barrier((ring[2][0], pick))

    picked = call(
        lambda *refs: rows_kernel(z, *refs),
        [((z.per_grp, width_in), BF16)] * z.grp,
        [("v", pick), ("v", features)],
        "rows", 1,
    )
    held = [to_grp(picked[s], s) for s in range(z.grp)]
    (held,) = call(
        turn_kernel, [((width_in, rows), BF16)], [("v", part) for part in held], "turn", 0.5
    )
    held_b = to_core(held)

    agg = []
    for k in range(z.zz):
        ins = [("v", plain[0][k]), ("v", plain[1][k])] + [("v", part) for part in ring[k]]
        ins += [("v", part) for part in agg]
        outs = [((rows, half), F32)] * 2
        last = k == z.zz - 1
        if last:
            ins += [("v", part) for part in (cot_a, cot_b, turned[0][k], turned[1][k])]
            outs = [((rows, half), BF16)] * 4 + [((wide // 2, half), BF16)] * 2
        agg = call(
            lambda *refs, k=k, last=last: forward_kernel(z, k == 0, last, *refs),
            outs, ins, "forward", 3 if last else 1,
        )
    hidden_a, hidden_b, grad_a, grad_b, *came = agg

    for k in range(z.zz - 2, -1, -1):
        came = [to_zz(part, -1) for part in came]
        if k == 1:
            came[0], hidden_b = lax.optimization_barrier((came[0], hidden_b))
            come = to_core(hidden_b)
        if k == 0:
            came[1], come = lax.optimization_barrier((came[1], come))
        mine = call(
            back_kernel,
            [((wide // 2, half), F32)] * 2,
            [("v", part) for part in (turned[0][k], turned[1][k], grad_a, grad_b)],
            "back", 1,
        )
        if k:
            came = [
                call(
                    pass_kernel, [((wide // 2, half), BF16)], [("v", part), ("v", moved)],
                    "pass", 0.5,
                )[0]
                for part, moved in zip(mine, came)
            ]
    first = core == 0
    hidden = jnp.concatenate(
        [jnp.where(first, hidden_a, come), jnp.where(first, come, hidden_a)], axis=1
    )

    share = width_in // z.grp
    terms = call(
        lambda *refs: grad_kernel(z, *refs),
        [((share, half), BF16)] * z.grp,
        [("s", me), ("v", held), ("v", held_b)] + [("v", part) for part in (*mine, *came)],
        "grad", 1.5,
        (pltpu.VMEM((width_in, half), BF16),),
    )

    def total_of(parts):
        return call(
            sum_kernel, [((share, half), BF16)], [("v", part) for part in parts], "sum", 0.5
        )[0]

    mine = total_of([to_grp(terms[s], s) for s in range(z.grp)])
    step = 1
    while step < z.zz:
        mine = total_of(
            [mine, lax.ppermute(mine, "zz", [(i, i ^ step) for i in range(z.zz)])]
        )
        step *= 2
    mine = [to_grp(mine, s) for s in range(z.grp)]
    (grad_weight,) = call(
        lambda *refs: last_kernel(z, *refs),
        [((width_in, hidden_units), F32)],
        [("s", me)] + [("v", part) for part in mine + [to_core(part) for part in mine]],
        "last", 2,
    )
    return hidden, grad_weight


def solution(mesh):
    n_grp, n_dom = mesh.shape["grp"], mesh.shape["dom"]
    split = Mesh(mesh.devices.reshape(n_grp, n_dom // 2, 2), ("grp", "zz", "core"))
    by_rows = ("grp", "zz", "core")
    placed = (
        P(by_rows, None),
        P(by_rows),
        P(by_rows, None),
        P(by_rows),
        P(by_rows, None, None, None),
        P(),
        P(by_rows, None),
    )
    return jax.shard_map(
        shards,
        mesh=split,
        in_specs=placed,
        out_specs=(P(by_rows, None), P()),
        check_vma=False,
    )
```

```python
import jax
import jax.numpy as jnp
from jax import lax
from jax.experimental import pallas as pl
from jax.experimental.pallas import tpu as pltpu
from jax.sharding import Mesh, PartitionSpec as P

BF16 = jnp.bfloat16
F32 = jnp.float32
I32 = jnp.int32


def log2(n):
    assert n & (n - 1) == 0
    return n.bit_length() - 1


def iota(shape, dim):
    return lax.broadcasted_iota(I32, shape, dim)


def one_hot(mask):
    return jnp.where(mask, 1.0, 0.0).astype(BF16)


def dot(a, b):
    return jnp.dot(a, b, preferred_element_type=F32)


def dot_rows(a, b):
    return lax.dot_general(a, b, (((0,), (0,)), ((), ())), preferred_element_type=F32)


def call(body, outs, ins, name, us, scratch=()):
    smem = pl.BlockSpec(memory_space=pltpu.SMEM)
    vmem = pl.BlockSpec(memory_space=pltpu.VMEM)
    arrays = [jax.ShapeDtypeStruct(s, d) for s, d in outs] + [value for _, value in ins]
    size = sum(a.size * a.dtype.itemsize for a in arrays + [m.get_array_aval() for m in scratch])
    return pl.pallas_call(
        body,
        out_shape=tuple(jax.ShapeDtypeStruct(s, d) for s, d in outs),
        in_specs=[smem if where == "s" else vmem for where, _ in ins],
        out_specs=tuple(vmem for _ in outs),
        scratch_shapes=list(scratch),
        compiler_params=pltpu.CompilerParams(vmem_limit_bytes=size + (6 << 20)),
        cost_estimate=pl.CostEstimate(flops=int(us * 2.5e8), bytes_accessed=0, transcendentals=0),
        name=name,
    )(*(value for _, value in ins))


class Sizes:
    def __init__(self, rows, tiles):
        self.grp, self.zz = lax.axis_size("grp"), lax.axis_size("zz")
        self.dom = 2 * self.zz
        self.rows, self.tiles = rows, tiles
        self.pair = rows // (self.grp * self.dom)
        self.piece = self.grp * self.pair
        self.per_grp = self.dom * self.pair
        assert rows // 128 < 7 and self.pair <= 128

    def before(self, d):
        inner = d % self.dom
        return d - inner + (inner - 2) % self.dom


def column(row):
    n = row.shape[1]
    on = iota((n, n), 0) == iota((n, n), 1)
    return jnp.sum(jnp.where(on, row.astype(F32), 0.0), axis=1, keepdims=True).astype(I32)


def index_kernel(z, me_ref, order_ref, out_ref):
    rows = z.rows
    shift = log2(rows)
    order_r = order_ref[...]
    order_c = column(order_r)
    down, across = iota((rows, rows), 0), iota((rows, rows), 1)
    source_r, source_c = order_r >> shift, order_c >> shift
    row_c = order_c & (rows - 1)
    same = jnp.where(source_c == source_r, 1.0, 0.0)
    rank_c = jnp.sum(jnp.where(across < down, same, 0.0), axis=1, keepdims=True).astype(I32)
    rank_r = jnp.sum(jnp.where(down < across, same, 0.0), axis=0, keepdims=True).astype(I32)
    owner = one_hot(iota((z.grp * z.dom, rows), 0) == source_r)
    at_rank = iota((rows, z.pair), 1) == rank_c
    high = jnp.where(at_rank, (row_c >> 4).astype(F32), 0.0).astype(BF16)
    low = jnp.where(at_rank, (row_c & 15).astype(F32), 0.0).astype(BF16)
    want = (dot(owner, high) * 16.0 + dot(owner, low)).astype(I32)
    out_ref[...] = jnp.zeros_like(out_ref)
    for d in range(z.grp * z.dom):
        out_ref[d, 0:1, 0:z.pair] = want[d:d + 1, :]
        near = z.before(d)
        out_ref[d, 7:8, 0:z.pair] = want[near:near + 1, :]
    across_grp = (source_r >> log2(z.dom)) ^ me_ref[0]
    inner = source_r & (z.dom - 1)
    slot = (inner * z.grp + across_grp) * z.pair + rank_r
    for i in range(rows // 128):
        lanes = slot[:, i * 128:(i + 1) * 128]
        out_ref[:, 1 + i:2 + i, :] = jnp.broadcast_to(lanes[None], (z.grp * z.dom, 1, 128))


def product_kernel(z, me_ref, weight_ref, *refs):
    parts, outs = refs[:-2], refs[-2:]
    half, size = outs[0].shape[1], parts[0].shape[0]
    for flip, out in enumerate(outs):
        at = pl.multiple_of((me_ref[2] ^ flip) * half, half)
        for i, part in enumerate(parts):
            product = dot(part[...], weight_ref[:, pl.ds(at, half)])
            out[i * size:(i + 1) * size, :] = product.astype(BF16)


def send_kernel(z, line, me_ref, message_ref, own_ref, other_ref, pick_ref, *outs):
    devices, height, width = message_ref.shape
    message = message_ref[...].reshape(devices * height, width)
    shape = (z.rows, devices * height)
    asker = (iota(shape, 0) >> log2(z.pair)) ^ (me_ref[0] * z.dom)
    spread = one_hot(iota(shape, 1) == asker * height + line)
    high = dot(spread, (message >> 4).astype(F32).astype(BF16))
    low = dot(spread, (message & 15).astype(F32).astype(BF16))
    mine = iota((z.rows, width), 1) == (iota((z.rows, width), 0) & (z.pair - 1))
    wanted = jnp.sum(jnp.where(mine, high * 16.0 + low, 0.0), axis=1, keepdims=True).astype(I32)
    pick_ref[...] = one_hot(iota((z.rows, z.rows), 1) == wanted)
    for flip, product in enumerate((own_ref, other_ref)):
        got = dot(pick_ref[...], product[...]).astype(BF16)
        for s in range(z.grp):
            outs[s][flip] = got[s * z.per_grp:(s + 1) * z.per_grp, :]


def rows_kernel(z, pick_ref, *refs):
    parts, outs = refs[:-z.grp], refs[-z.grp:]
    size = parts[0].shape[0]
    for s, out in enumerate(outs):
        at = pl.ds(s * z.per_grp, z.per_grp)
        rows = sum(
            dot(pick_ref[at, i * size:(i + 1) * size], part[...]) for i, part in enumerate(parts)
        )
        out[...] = rows.astype(BF16)


def pack_kernel(z, *refs):
    ins, outs = refs[:z.grp], refs[z.grp:]
    for flip in range(2):
        for s in range(z.grp):
            outs[flip][s * z.per_grp:(s + 1) * z.per_grp, :] = ins[s][flip]


def place_kernel(z, me_ref, message_ref, out_ref):
    @pl.loop(0, z.dom)
    def _(n):
        message = message_ref[me_ref[0] * z.dom + n]
        slot = jnp.concatenate([message[1 + i:2 + i, :] for i in range(z.rows // 128)], axis=1)
        rank, at = slot & (z.pair - 1), slot >> log2(z.pair)
        s, at = at & (z.grp - 1), at >> log2(z.grp)
        k, rel = (me_ref[1] - (at >> 1)) & (z.zz - 1), (at & 1) ^ me_ref[2]
        slot = ((k * 2 + rel) * z.grp + s) * z.pair + rank
        out_ref[n] = one_hot(iota((z.rows, z.rows), 0) == slot)


def dense_kernel(cols_ref, vals_ref, out_ref, total):
    tiles, blocks, tile, _ = vals_ref.shape
    count = out_ref.shape[0]

    @pl.loop(0, tiles)
    def _(t):
        total[...] = jnp.zeros_like(total)
        for k in range(blocks):
            at = pl.multiple_of(cols_ref[t, k] * tile, tile)
            total[pl.ds(at, tile), :] += vals_ref[t, k].T.astype(F32)
        left = pl.multiple_of(t * tile, tile)
        out_ref[:, pl.ds(left, tile)] = total[pl.ds(0, count), :].astype(BF16)


def arrange_kernel(z, place_ref, dense_ref, *outs):
    @pl.loop(0, z.dom)
    def _(n):
        at = pl.multiple_of(n * z.rows, z.rows)
        part = dot(place_ref[n], dense_ref[pl.ds(at, z.rows), :]).astype(BF16)
        for k in range(z.zz):
            for p in range(2 * z.grp):
                first = (k * 2 * z.grp + p) * z.pair
                rows = part[first:first + z.pair, :]
                if z.pair % 16 == 0:
                    to = pl.multiple_of(p * z.per_grp + n * z.pair, z.pair)
                    outs[k][pl.ds(to, z.pair), :] = rows
                else:
                    outs[k][p, n] = rows


def turn_kernel(*refs):
    out, height = refs[-1], refs[0].shape[0]
    for s, part in enumerate(refs[:-1]):
        out[:, s * height:(s + 1) * height] = part[...].T


def forward_kernel(z, first, last, *refs):
    turned, refs = refs[:2], refs[2:]
    pieces, refs = refs[:2], refs[2:]
    rows = jnp.concatenate([ref[...] for ref in pieces], axis=0)
    agg = [dot_rows(ref[...], rows) for ref in turned]
    if not first:
        agg = [part + ref[...] for part, ref in zip(agg, refs)]
        refs = refs[2:]
    if not last:
        for ref, part in zip(refs, agg):
            ref[...] = part
        return
    cots, ahead, hiddens, grads, parts = (refs[2 * i:2 * i + 2] for i in range(5))
    for part, cot, hidden, grad in zip(agg, cots, hiddens, grads):
        sig = jax.nn.sigmoid(part)
        hidden[...] = (part * sig).astype(BF16)
        grad[...] = (cot[...].astype(F32) * (sig * (1.0 + part * (1.0 - sig)))).astype(BF16)
    back_into(parts, ahead, grads)


def back_into(outs, turned, grads):
    size = outs[0].shape[0]
    for i, out in enumerate(outs):
        rows = pl.ds(i * size, size)
        value = dot(turned[0][rows, :], grads[0][...]) + dot(turned[1][rows, :], grads[1][...])
        out[...] = value.astype(out.dtype)


def back_kernel(turned_a, turned_b, grad_a, grad_b, *outs):
    back_into(outs, (turned_a, turned_b), (grad_a, grad_b))


def pass_kernel(mine_ref, come_ref, out_ref):
    out_ref[...] = (mine_ref[...] + come_ref[...].astype(F32)).astype(BF16)


def grad_kernel(z, me_ref, *refs):
    own_left, near_left = refs[0:2], refs[2:4]
    own, mine, come, outs, whole = refs[4:6], refs[6:8], refs[8:10], refs[10:-1], refs[-1]
    total = 0.0
    for left, part in zip(own_left, own):
        total = total + dot(left[...], part[...].astype(BF16))
    for left, part, moved in zip(near_left, mine, come):
        total = total + dot(left[...], (part[...] + moved[...].astype(F32)).astype(BF16))
    whole[...] = total.astype(BF16)
    share = whole.shape[0] // z.grp
    for s in range(z.grp):
        at = pl.multiple_of((me_ref[0] ^ s) * share, share)
        outs[s][...] = whole[pl.ds(at, share), :]


def sum_kernel(*refs):
    refs[-1][...] = sum(term[...].astype(F32) for term in refs[:-1]).astype(BF16)


def last_kernel(z, me_ref, *refs):
    pieces, out = refs[:-1], refs[-1]
    share, half = pieces[0].shape
    for rel in range(2):
        left = pl.multiple_of((me_ref[2] ^ rel) * half, half)
        for s in range(z.grp):
            at = pl.multiple_of((me_ref[0] ^ s) * share, share)
            out[pl.ds(at, share), pl.ds(left, half)] = pieces[rel * z.grp + s][...].astype(F32)


def arrange(z, place, dense, wide):
    inner = (wide, z.rows) if z.pair % 16 == 0 else (2 * z.grp, z.dom, z.pair, z.rows)
    got = call(
        lambda *refs: arrange_kernel(z, *refs),
        [(inner, BF16)] * z.zz,
        [("v", place), ("v", dense)],
        "arrange", 4,
    )
    return [part.reshape(wide, z.rows) for part in got]


def shards(features, node_order, block_cols, block_count, block_vals, weight, cotangent):
    rows, width_in = features.shape
    hidden_units = weight.shape[1]
    half = hidden_units // 2
    tiles, blocks, tile = block_vals.shape[0], block_vals.shape[1], block_vals.shape[-1]
    z = Sizes(rows, tiles)
    at_grp, at_zz, core = lax.axis_index("grp"), lax.axis_index("zz"), lax.axis_index("core")
    me = jnp.stack([at_grp, at_zz, core]).astype(I32)

    def to_core(x):
        return lax.ppermute(x, "core", [(0, 1), (1, 0)])

    def to_grp(x, s):
        return lax.ppermute(x, "grp", [(i, i ^ s) for i in range(z.grp)]) if s else x

    def to_zz(x, k):
        return lax.ppermute(x, "zz", [(i, (i + k) % z.zz) for i in range(z.zz)]) if k else x

    first_half = features[:rows // 2]
    (message,) = call(
        lambda *refs: index_kernel(z, *refs),
        [((z.grp * z.dom, 8, 128), I32)],
        [("s", me), ("v", node_order.reshape(1, rows))],
        "index", 1,
    )
    message, features = lax.optimization_barrier((message, features))
    message = lax.all_to_all(
        message, ("grp", "zz", "core"), split_axis=0, concat_axis=0, tiled=True
    )
    vals_b = to_core(block_vals)

    def products_of(parts):
        return call(
            lambda *refs: product_kernel(z, *refs),
            [((rows, half), BF16)] * 2,
            [("s", me), ("v", weight)] + [("v", part) for part in parts],
            "product", 1.5,
        )

    def send_of(line, products):
        return call(
            lambda *refs: send_kernel(z, line, *refs),
            [((rows, rows), BF16)] + [((2, z.per_grp, half), BF16)] * z.grp,
            [("s", me), ("v", message)] + [("v", part) for part in products],
            "send", 1.5,
        )

    def pack(parts):
        own, other = call(
            lambda *refs: pack_kernel(z, *refs),
            [((rows, half), BF16)] * 2,
            [("v", part) for part in parts],
            "pack", 0.5,
        )
        return [own, to_core(other)]

    near = [to_zz(first_half, 1)]
    products = products_of([features])
    products, later = lax.optimization_barrier((products, features[rows // 2:]))
    near.append(to_zz(later, 1))
    message, vals_b, near[0] = lax.optimization_barrier((message, vals_b, near[0]))
    pick, *got = send_of(0, products)
    got, message, cotangent, block_cols = lax.optimization_barrier(
        (got, message, cotangent, block_cols)
    )
    came = [to_grp(got[s], s) for s in range(z.grp)]

    live = iota((tiles, blocks), 1) < block_count[:, None]
    cols_a = jnp.where(live, block_cols, z.dom * tiles)
    cols_b = to_core(cols_a)
    cot_a = lax.dynamic_slice_in_dim(cotangent, core * half, half, axis=1)
    cot_b = to_core(lax.dynamic_slice_in_dim(cotangent, (1 - core) * half, half, axis=1))

    wide = 2 * z.grp * z.per_grp

    def arranged(cols, vals):
        (dense,) = call(
            dense_kernel,
            [((z.dom * rows, rows), BF16)],
            [("s", cols), ("v", vals)],
            "dense", 2.5,
            (pltpu.VMEM((z.dom * rows + tile, tile), F32),),
        )
        return arrange(z, place, dense, wide)

    pick_near, *got = send_of(7, products_of(near))
    came, got = lax.optimization_barrier((came, got))

    def lefts_of(pick, parts):
        picked = call(
            lambda *refs: rows_kernel(z, *refs),
            [((z.per_grp, width_in), BF16)] * z.grp,
            [("v", pick)] + [("v", part) for part in parts],
            "rows", 1,
        )
        return [to_grp(picked[s], s) for s in range(z.grp)]

    def turned_of(parts):
        (left,) = call(
            turn_kernel, [((width_in, rows), BF16)], [("v", part) for part in parts], "turn", 0.5
        )
        return [left, to_core(left)]

    ring = {0: pack(came)}
    came = [to_grp(got[s], s) for s in range(z.grp)]
    ring[0][1], pick, message = lax.optimization_barrier((ring[0][1], pick, message))
    (place,) = call(
        lambda *refs: place_kernel(z, *refs),
        [((z.dom, rows, rows), BF16)],
        [("s", me), ("v", message)],
        "place", 1.5,
    )
    turned = [arranged(cols_a, block_vals)]
    order = list(range(z.zz - 1, 1, -1))
    for k in order:
        ring[k] = [to_zz(part, -1) for part in ring[(k + 1) % z.zz]]
        if k == order[0]:
            ring[k][0], vals_b = lax.optimization_barrier((ring[k][0], vals_b))
            turned.append(arranged(cols_b, vals_b))
    came, left = lax.optimization_barrier((came, lefts_of(pick, [features])))
    ring[1] = pack(came)
    lefts = turned_of(left)

    agg = []
    order = [0, 1] + order
    for k in order:
        ins = [("v", turned[0][k]), ("v", turned[1][k])] + [("v", part) for part in ring[k]]
        ins += [("v", part) for part in agg]
        outs = [((rows, half), F32)] * 2
        last = k == order[-1]
        if last:
            ahead = (turned[0][z.zz - 1], turned[1][z.zz - 1])
            ins += [("v", part) for part in (cot_a, cot_b, *ahead)]
            outs = [((rows, half), BF16)] * 4 + [((wide // 2, half), BF16)] * 2
        agg = call(
            lambda *refs, k=k, last=last: forward_kernel(z, k == 0, last, *refs),
            outs, ins, "forward", 3 if last else 1,
        )
    hidden_a, hidden_b, grad_a, grad_b, *came = agg

    def back(k):
        return call(
            back_kernel,
            [((wide // 2, half), F32)] * 2,
            [("v", part) for part in (turned[0][k], turned[1][k], grad_a, grad_b)],
            "back", 1,
        )

    for k in range(z.zz - 2, 0, -1):
        came = [to_zz(part, -1) for part in came]
        if k == z.zz - 2:
            came[0], pick_near = lax.optimization_barrier((came[0], pick_near))
            lefts += turned_of(lefts_of(pick_near, near))
        mine = back(k)
        if k == 1:
            came[1], come = lax.optimization_barrier((came[1], come))
            break
        came = [
            call(
                pass_kernel, [((wide // 2, half), BF16)], [("v", part), ("v", moved)],
                "pass", 0.5,
            )[0]
            for part, moved in zip(mine, came)
        ]
        if k == z.zz - 2:
            came[1], hidden_b = lax.optimization_barrier((came[1], hidden_b))
            come = to_core(hidden_b)
    first = core == 0
    hidden = jnp.concatenate(
        [jnp.where(first, hidden_a, come), jnp.where(first, come, hidden_a)], axis=1
    )

    share = width_in // z.grp
    terms = call(
        lambda *refs: grad_kernel(z, *refs),
        [((share, half), BF16)] * z.grp,
        [("s", me)] + [("v", part) for part in (*lefts, *back(0), *mine, *came)],
        "grad", 1.5,
        (pltpu.VMEM((width_in, half), BF16),),
    )

    def total_of(parts):
        return call(
            sum_kernel, [((share, half), BF16)], [("v", part) for part in parts], "sum", 0.5
        )[0]

    mine = total_of([to_grp(terms[s], s) for s in range(z.grp)])
    step = 1
    while step < z.zz:
        mine = total_of(
            [mine, lax.ppermute(mine, "zz", [(i, i ^ step) for i in range(z.zz)])]
        )
        step *= 2
    mine = [to_grp(mine, s) for s in range(z.grp)]
    (grad_weight,) = call(
        lambda *refs: last_kernel(z, *refs),
        [((width_in, hidden_units), F32)],
        [("s", me)] + [("v", part) for part in mine + [to_core(part) for part in mine]],
        "last", 2,
    )
    return hidden, grad_weight


def solution(mesh):
    n_grp, n_dom = mesh.shape["grp"], mesh.shape["dom"]
    split = Mesh(mesh.devices.reshape(n_grp, n_dom // 2, 2), ("grp", "zz", "core"))
    by_rows = ("grp", "zz", "core")
    placed = (
        P(by_rows, None),
        P(by_rows),
        P(by_rows, None),
        P(by_rows),
        P(by_rows, None, None, None),
        P(),
        P(by_rows, None),
    )
    return jax.shard_map(
        shards,
        mesh=split,
        in_specs=placed,
        out_specs=(P(by_rows, None), P()),
        check_vma=False,
    )
```

```python
import jax
import jax.numpy as jnp
from jax import lax
from jax.experimental import pallas as pl
from jax.experimental.pallas import tpu as pltpu
from jax.sharding import Mesh, PartitionSpec as P

BF16 = jnp.bfloat16
F32 = jnp.float32
I32 = jnp.int32


def log2(n):
    assert n & (n - 1) == 0
    return n.bit_length() - 1


def iota(shape, dim):
    return lax.broadcasted_iota(I32, shape, dim)


def one_hot(mask):
    return jnp.where(mask, 1.0, 0.0).astype(BF16)


def dot(a, b):
    return jnp.dot(a, b, preferred_element_type=F32)


def dot_rows(a, b):
    return lax.dot_general(a, b, (((0,), (0,)), ((), ())), preferred_element_type=F32)


def call(body, outs, ins, name, us, scratch=()):
    smem = pl.BlockSpec(memory_space=pltpu.SMEM)
    vmem = pl.BlockSpec(memory_space=pltpu.VMEM)
    arrays = [jax.ShapeDtypeStruct(s, d) for s, d in outs] + [value for _, value in ins]
    size = sum(a.size * a.dtype.itemsize for a in arrays + [m.get_array_aval() for m in scratch])
    return pl.pallas_call(
        body,
        out_shape=tuple(jax.ShapeDtypeStruct(s, d) for s, d in outs),
        in_specs=[smem if where == "s" else vmem for where, _ in ins],
        out_specs=tuple(vmem for _ in outs),
        scratch_shapes=list(scratch),
        compiler_params=pltpu.CompilerParams(vmem_limit_bytes=size + (6 << 20)),
        cost_estimate=pl.CostEstimate(flops=int(us * 2e7), bytes_accessed=0, transcendentals=0),
        name=name,
    )(*(value for _, value in ins))


class Sizes:
    def __init__(self, rows, tiles):
        self.grp, self.zz = lax.axis_size("grp"), lax.axis_size("zz")
        self.dom = 2 * self.zz
        self.rows, self.tiles = rows, tiles
        self.pair = rows // (self.grp * self.dom)
        self.piece = self.grp * self.pair
        self.per_grp = self.dom * self.pair
        assert rows // 128 < 5 and self.pair <= 128

    def before(self, d):
        inner = d % self.dom
        return d - inner + (inner - 2) % self.dom


def column(row):
    n = row.shape[1]
    on = iota((n, n), 0) == iota((n, n), 1)
    return jnp.sum(jnp.where(on, row.astype(F32), 0.0), axis=1, keepdims=True).astype(I32)


def index_kernel(z, me_ref, order_ref, out_ref):
    rows = z.rows
    shift = log2(rows)
    order_r = order_ref[...]
    order_c = column(order_r)
    down, across = iota((rows, rows), 0), iota((rows, rows), 1)
    source_r, source_c = order_r >> shift, order_c >> shift
    row_c = order_c & (rows - 1)
    same = jnp.where(source_c == source_r, 1.0, 0.0)
    rank_c = jnp.sum(jnp.where(across < down, same, 0.0), axis=1, keepdims=True).astype(I32)
    rank_r = jnp.sum(jnp.where(down < across, same, 0.0), axis=0, keepdims=True).astype(I32)
    owner = one_hot(iota((z.grp * z.dom, rows), 0) == source_r)
    at_rank = iota((rows, z.pair), 1) == rank_c
    high = jnp.where(at_rank, (row_c >> 4).astype(F32), 0.0).astype(BF16)
    low = jnp.where(at_rank, (row_c & 15).astype(F32), 0.0).astype(BF16)
    want = (dot(owner, high) * 16.0 + dot(owner, low)).astype(I32)
    out_ref[...] = jnp.zeros_like(out_ref)
    for d in range(z.grp * z.dom):
        near = z.before(d)
        for line, source in ((0, d), (5, d ^ 1), (6, near), (7, near ^ 1)):
            out_ref[d, line:line + 1, 0:z.pair] = want[source:source + 1, :]
    across_grp = (source_r >> log2(z.dom)) ^ me_ref[0]
    inner = source_r & (z.dom - 1)
    slot = (inner * z.grp + across_grp) * z.pair + rank_r
    for i in range(rows // 128):
        lanes = slot[:, i * 128:(i + 1) * 128]
        out_ref[:, 1 + i:2 + i, :] = jnp.broadcast_to(lanes[None], (z.grp * z.dom, 1, 128))


def product_kernel(z, me_ref, features_ref, weight_ref, *outs):
    half = outs[0].shape[1]
    for flip, out in enumerate(outs):
        at = pl.multiple_of((me_ref[2] ^ flip) * half, half)
        out[...] = dot(features_ref[...], weight_ref[:, pl.ds(at, half)]).astype(BF16)


def send_kernel(z, lines, me_ref, message_ref, own_ref, other_ref, pick_ref, *outs):
    devices, height, width = message_ref.shape
    message = message_ref[...].reshape(devices * height, width)
    high_bits = (message >> 4).astype(F32).astype(BF16)
    low_bits = (message & 15).astype(F32).astype(BF16)
    shape = (z.rows, devices * height)
    asker = (iota(shape, 0) >> log2(z.pair)) ^ (me_ref[0] * z.dom)
    mine = iota((z.rows, width), 1) == (iota((z.rows, width), 0) & (z.pair - 1))
    for rel, (line, product) in enumerate(zip(lines, (own_ref, other_ref))):
        spread = one_hot(iota(shape, 1) == asker * height + line)
        asked = dot(spread, high_bits) * 16.0 + dot(spread, low_bits)
        wanted = jnp.sum(jnp.where(mine, asked, 0.0), axis=1, keepdims=True).astype(I32)
        pick = one_hot(iota((z.rows, z.rows), 1) == wanted)
        if rel == 0:
            pick_ref[...] = pick
        got = dot(pick, product[...]).astype(BF16)
        for s in range(z.grp):
            outs[s][rel] = got[s * z.per_grp:(s + 1) * z.per_grp, :]


def rows_kernel(z, pick_ref, features_ref, *outs):
    for s, out in enumerate(outs):
        pick = pick_ref[s * z.per_grp:(s + 1) * z.per_grp, :]
        out[...] = dot(pick, features_ref[...]).astype(BF16)


def pack_kernel(z, *refs):
    ins, out = refs[:-1], refs[-1]
    for rel in range(2):
        for s in range(z.grp):
            at = (rel * z.grp + s) * z.per_grp
            out[at:at + z.per_grp, :] = ins[s][rel]


def place_kernel(z, me_ref, message_ref, out_ref):
    @pl.loop(0, z.dom)
    def _(n):
        message = message_ref[me_ref[0] * z.dom + n]
        slot = jnp.concatenate([message[1 + i:2 + i, :] for i in range(z.rows // 128)], axis=1)
        rank, at = slot & (z.pair - 1), slot >> log2(z.pair)
        s, at = at & (z.grp - 1), at >> log2(z.grp)
        k, rel = (me_ref[1] - (at >> 1)) & (z.zz - 1), (at & 1) ^ me_ref[2]
        slot = ((k * 2 + rel) * z.grp + s) * z.pair + rank
        out_ref[n] = one_hot(iota((z.rows, z.rows), 0) == slot)


def dense_kernel(cols_ref, vals_ref, out_ref, total):
    tiles, blocks, tile, _ = vals_ref.shape
    count = out_ref.shape[0]

    @pl.loop(0, tiles)
    def _(t):
        total[...] = jnp.zeros_like(total)
        for k in range(blocks):
            at = pl.multiple_of(cols_ref[t, k] * tile, tile)
            total[pl.ds(at, tile), :] += vals_ref[t, k].T.astype(F32)
        left = pl.multiple_of(t * tile, tile)
        out_ref[:, pl.ds(left, tile)] = total[pl.ds(0, count), :].astype(BF16)


def arrange_kernel(z, place_ref, dense_ref, *outs):
    @pl.loop(0, z.dom)
    def _(n):
        at = pl.multiple_of(n * z.rows, z.rows)
        part = dot(place_ref[n], dense_ref[pl.ds(at, z.rows), :]).astype(BF16)
        for k in range(z.zz):
            for p in range(2 * z.grp):
                first = (k * 2 * z.grp + p) * z.pair
                rows = part[first:first + z.pair, :]
                if z.pair % 16 == 0:
                    to = pl.multiple_of(p * z.per_grp + n * z.pair, z.pair)
                    outs[k][pl.ds(to, z.pair), :] = rows
                else:
                    outs[k][p, n] = rows


def turn_kernel(*refs):
    out, height = refs[-1], refs[0].shape[0]
    for s, part in enumerate(refs[:-1]):
        out[:, s * height:(s + 1) * height] = part[...].T


def forward_kernel(z, first, last, *refs):
    turned, refs = refs[:2], refs[2:]
    rows, refs = refs[0][...], refs[1:]
    agg = [dot_rows(ref[...], rows) for ref in turned]
    if not first:
        agg = [part + ref[...] for part, ref in zip(agg, refs)]
        refs = refs[2:]
    if not last:
        for ref, part in zip(refs, agg):
            ref[...] = part
        return
    cots, ahead, hiddens, grads = (refs[2 * i:2 * i + 2] for i in range(4))
    for part, cot, hidden, grad in zip(agg, cots, hiddens, grads):
        sig = jax.nn.sigmoid(part)
        hidden[...] = (part * sig).astype(BF16)
        grad[...] = (cot[...].astype(F32) * (sig * (1.0 + part * (1.0 - sig)))).astype(BF16)
    back_kernel(*ahead, *grads, refs[-1])


def back_kernel(turned_a, turned_b, grad_a, grad_b, out):
    value = dot(turned_a[...], grad_a[...]) + dot(turned_b[...], grad_b[...])
    out[...] = value.astype(out.dtype)


def pass_kernel(mine_ref, come_ref, out_ref):
    out_ref[...] = (mine_ref[...] + come_ref[...].astype(F32)).astype(BF16)


def grad_kernel(z, me_ref, own_a, own_b, near_a, near_b, own_ref, mine_ref, come_ref, *refs):
    outs, whole = refs[:-1], refs[-1]
    own = own_ref[...].astype(BF16)
    near = (mine_ref[...] + come_ref[...].astype(F32)).astype(BF16)
    total = dot(own_a[...], own[:z.rows]) + dot(own_b[...], own[z.rows:])
    total = total + dot(near_a[...], near[:z.rows]) + dot(near_b[...], near[z.rows:])
    whole[...] = total.astype(BF16)
    share = whole.shape[0] // z.grp
    for s in range(z.grp):
        at = pl.multiple_of((me_ref[0] ^ s) * share, share)
        outs[s][...] = whole[pl.ds(at, share), :]


def sum_kernel(*refs):
    refs[-1][...] = sum(term[...].astype(F32) for term in refs[:-1]).astype(BF16)


def last_kernel(z, me_ref, *refs):
    pieces, out = refs[:-1], refs[-1]
    share, half = pieces[0].shape
    for rel in range(2):
        left = pl.multiple_of((me_ref[2] ^ rel) * half, half)
        for s in range(z.grp):
            at = pl.multiple_of((me_ref[0] ^ s) * share, share)
            out[pl.ds(at, share), pl.ds(left, half)] = pieces[rel * z.grp + s][...].astype(F32)


def arrange(z, place, dense, wide):
    inner = (wide, z.rows) if z.pair % 16 == 0 else (2 * z.grp, z.dom, z.pair, z.rows)
    got = call(
        lambda *refs: arrange_kernel(z, *refs),
        [(inner, BF16)] * z.zz,
        [("v", place), ("v", dense)],
        "arrange", 4,
    )
    return [part.reshape(wide, z.rows) for part in got]


def shards(features, node_order, block_cols, block_count, block_vals, weight, cotangent):
    rows, width_in = features.shape
    hidden_units = weight.shape[1]
    half = hidden_units // 2
    tiles, blocks, tile = block_vals.shape[0], block_vals.shape[1], block_vals.shape[-1]
    z = Sizes(rows, tiles)
    at_grp, at_zz, core = lax.axis_index("grp"), lax.axis_index("zz"), lax.axis_index("core")
    me = jnp.stack([at_grp, at_zz, core]).astype(I32)

    def to_core(x):
        return lax.ppermute(x, "core", [(0, 1), (1, 0)])

    def to_grp(x, s):
        return lax.ppermute(x, "grp", [(i, i ^ s) for i in range(z.grp)]) if s else x

    def to_zz(x, k):
        return lax.ppermute(x, "zz", [(i, (i + k) % z.zz) for i in range(z.zz)]) if k else x

    first_half = features[:rows // 2]
    (message,) = call(
        lambda *refs: index_kernel(z, *refs),
        [((z.grp * z.dom, 8, 128), I32)],
        [("s", me), ("v", node_order.reshape(1, rows))],
        "index", 1,
    )
    message, features = lax.optimization_barrier((message, features))
    message = lax.all_to_all(
        message, ("grp", "zz", "core"), split_axis=0, concat_axis=0, tiled=True
    )
    vals_b = to_core(block_vals)

    def products_of(part):
        own, other = call(
            lambda *refs: product_kernel(z, *refs),
            [((rows, half), BF16)] * 2,
            [("s", me), ("v", part), ("v", weight)],
            "product", 1.5,
        )
        return own, to_core(other)

    def send_of(lines, products):
        return call(
            lambda *refs: send_kernel(z, lines, *refs),
            [((rows, rows), BF16)] + [((2, z.per_grp, half), BF16)] * z.grp,
            [("s", me), ("v", message)] + [("v", part) for part in products],
            "send", 1.5,
        )

    def across(parts):
        return [to_grp(part, s) for s, part in enumerate(parts)]

    def pack(parts):
        return call(
            lambda *refs: pack_kernel(z, *refs),
            [((2 * rows, half), BF16)],
            [("v", part) for part in parts],
            "pack", 0.5,
        )[0]

    def rows_of(pick, part):
        return call(
            lambda *refs: rows_kernel(z, *refs),
            [((z.per_grp, width_in), BF16)] * z.grp,
            [("v", pick), ("v", part)],
            "rows", 1,
        )

    def turned_of(parts):
        (left,) = call(
            turn_kernel, [((width_in, rows), BF16)], [("v", part) for part in parts], "turn", 0.5
        )
        return [left, to_core(left)]

    products = products_of(features)
    pick, *got = send_of((0, 5), products)
    got, message, cotangent, block_cols, vals_b, late = lax.optimization_barrier(
        (got, message, cotangent, block_cols, vals_b, features)
    )
    came = across(got)

    near = to_zz(late, 1)

    live = iota((tiles, blocks), 1) < block_count[:, None]
    cols_a = jnp.where(live, block_cols, z.dom * tiles)
    cols_b = to_core(cols_a)
    cot_a = lax.dynamic_slice_in_dim(cotangent, core * half, half, axis=1)
    cot_b = to_core(lax.dynamic_slice_in_dim(cotangent, (1 - core) * half, half, axis=1))

    (place,) = call(
        lambda *refs: place_kernel(z, *refs),
        [((z.dom, rows, rows), BF16)],
        [("s", me), ("v", message)],
        "place", 1.5,
    )

    def dense_of(cols, vals):
        return call(
            dense_kernel,
            [((z.dom * rows, rows), BF16)],
            [("s", cols), ("v", vals)],
            "dense", 2.5,
            (pltpu.VMEM((z.dom * rows + tile, tile), F32),),
        )[0]

    dense_a = dense_of(cols_a, block_vals)
    came, dense_a, place, cols_b = lax.optimization_barrier((came, dense_a, place, cols_b))

    wide = 2 * z.grp * z.per_grp
    turned = [arrange(z, place, dense_a, wide), arrange(z, place, dense_of(cols_b, vals_b), wide)]
    ring = {0: pack(came)}
    lefts = turned_of(across(rows_of(pick, features)))
    near, turned[0][0] = lax.optimization_barrier((near, turned[0][0]))
    order = list(range(z.zz - 1, 1, -1))
    for k in order:
        ring[k] = to_zz(ring[(k + 1) % z.zz], -1)
        if k == order[0]:
            pick_near, *got = send_of((6, 7), products_of(near))
            ring[k], turned, got, cot_a, cot_b, lefts = lax.optimization_barrier(
                (ring[k], turned, got, cot_a, cot_b, lefts)
            )
            came = across(got)
    came, pick_near = lax.optimization_barrier((came, pick_near))
    ring[1] = pack(came)
    held_near = rows_of(pick_near, near)

    agg = []
    order = [0] + order[:-1] + [1] + order[-1:]
    for k in order:
        last = k == order[-1]
        if last:
            agg, held_near = lax.optimization_barrier((agg, held_near))
        ins = [("v", part) for part in (turned[0][k], turned[1][k], ring[k], *agg)]
        outs = [((rows, half), F32)] * 2
        if last:
            ahead = (turned[0][z.zz - 1], turned[1][z.zz - 1])
            ins += [("v", part) for part in (cot_a, cot_b, *ahead)]
            outs = [((rows, half), BF16)] * 4 + [((wide, half), BF16)]
        agg = call(
            lambda *refs, k=k, last=last: forward_kernel(z, k == 0, last, *refs),
            outs, ins, "forward", 3 if last else 1,
        )
    hidden_a, hidden_b, grad_a, grad_b, came = agg

    def back(k):
        return call(
            back_kernel,
            [((wide, half), F32)],
            [("v", part) for part in (turned[0][k], turned[1][k], grad_a, grad_b)],
            "back", 1,
        )[0]

    held_near = across(held_near)
    come = to_core(hidden_b)
    for k in range(z.zz - 2, 0, -1):
        came = to_zz(came, -1)
        mine = back(k)
        if k == 1:
            break
        (came,) = call(
            pass_kernel, [((wide, half), BF16)], [("v", mine), ("v", came)], "pass", 0.5
        )
        if k == z.zz - 2:
            came, come, held_near = lax.optimization_barrier((came, come, held_near))
    lefts += turned_of(held_near)
    first = core == 0
    hidden = jnp.concatenate(
        [jnp.where(first, hidden_a, come), jnp.where(first, come, hidden_a)], axis=1
    )

    share = width_in // z.grp
    terms = call(
        lambda *refs: grad_kernel(z, *refs),
        [((share, half), BF16)] * z.grp,
        [("s", me)] + [("v", part) for part in (*lefts, back(0), mine, came)],
        "grad", 1.5,
        (pltpu.VMEM((width_in, half), BF16),),
    )

    def total_of(parts):
        return call(
            sum_kernel, [((share, half), BF16)], [("v", part) for part in parts], "sum", 0.5
        )[0]

    mine = total_of([to_grp(terms[s], s) for s in range(z.grp)])
    step = 1
    while step < z.zz:
        mine = total_of(
            [mine, lax.ppermute(mine, "zz", [(i, i ^ step) for i in range(z.zz)])]
        )
        step *= 2
    mine = [to_grp(mine, s) for s in range(z.grp)]
    (grad_weight,) = call(
        lambda *refs: last_kernel(z, *refs),
        [((width_in, hidden_units), F32)],
        [("s", me)] + [("v", part) for part in mine + [to_core(part) for part in mine]],
        "last", 2,
    )
    return hidden, grad_weight


def solution(mesh):
    n_grp, n_dom = mesh.shape["grp"], mesh.shape["dom"]
    split = Mesh(mesh.devices.reshape(n_grp, n_dom // 2, 2), ("grp", "zz", "core"))
    by_rows = ("grp", "zz", "core")
    placed = (
        P(by_rows, None),
        P(by_rows),
        P(by_rows, None),
        P(by_rows),
        P(by_rows, None, None, None),
        P(),
        P(by_rows, None),
    )
    return jax.shard_map(
        shards,
        mesh=split,
        in_specs=placed,
        out_specs=(P(by_rows, None), P()),
        check_vma=False,
    )
```

```python
import jax
import jax.numpy as jnp
from jax import lax
from jax.experimental import pallas as pl
from jax.experimental.pallas import tpu as pltpu
from jax.sharding import Mesh, PartitionSpec as P

BF16 = jnp.bfloat16
F32 = jnp.float32
I32 = jnp.int32


def log2(n):
    assert n & (n - 1) == 0
    return n.bit_length() - 1


def iota(shape, dim):
    return lax.broadcasted_iota(I32, shape, dim)


def one_hot(mask):
    return jnp.where(mask, 1.0, 0.0).astype(BF16)


def dot(a, b):
    return jnp.dot(a, b, preferred_element_type=F32)


def dot_rows(a, b):
    return lax.dot_general(a, b, (((0,), (0,)), ((), ())), preferred_element_type=F32)


def call(body, outs, ins, name, us, scratch=(), after=(), token=False):
    smem = pl.BlockSpec(memory_space=pltpu.SMEM)
    vmem = pl.BlockSpec(memory_space=pltpu.VMEM)
    count = len(ins)
    ties = len(after)
    if token:
        outs = [*outs, ((8, 128), F32)]

    def kernel(*refs):
        refs = refs[:count] + refs[count + ties:]
        if token:
            at = count + len(outs) - 1
            refs[at][...] = jnp.zeros((8, 128), F32)
            refs = refs[:at] + refs[at + 1:]
        body(*refs)

    arrays = [jax.ShapeDtypeStruct(s, d) for s, d in outs] + [value for _, value in ins]
    size = sum(a.size * a.dtype.itemsize for a in arrays + [m.get_array_aval() for m in scratch])
    return pl.pallas_call(
        kernel,
        out_shape=tuple(jax.ShapeDtypeStruct(s, d) for s, d in outs),
        in_specs=[smem if where == "s" else vmem for where, _ in ins]
        + [pl.BlockSpec(memory_space=pl.ANY)] * ties,
        out_specs=tuple(vmem for _ in outs),
        scratch_shapes=list(scratch),
        compiler_params=pltpu.CompilerParams(vmem_limit_bytes=size + (6 << 20)),
        cost_estimate=pl.CostEstimate(flops=int(us * 2e7), bytes_accessed=0, transcendentals=0),
        name=name,
    )(*(value for _, value in ins), *after)


class Sizes:
    def __init__(self, rows, tiles):
        self.grp, self.zz = lax.axis_size("grp"), lax.axis_size("zz")
        self.dom = 2 * self.zz
        self.rows, self.tiles = rows, tiles
        self.pair = rows // (self.grp * self.dom)
        self.piece = self.grp * self.pair
        self.per_grp = self.dom * self.pair
        assert rows // 128 < 5 and self.pair <= 128

    def before(self, d):
        inner = d % self.dom
        return d - inner + (inner - 2) % self.dom


def column(row):
    n = row.shape[1]
    on = iota((n, n), 0) == iota((n, n), 1)
    return jnp.sum(jnp.where(on, row.astype(F32), 0.0), axis=1, keepdims=True).astype(I32)


def index_kernel(z, me_ref, order_ref, out_ref):
    rows = z.rows
    shift = log2(rows)
    order_r = order_ref[...]
    order_c = column(order_r)
    down, across = iota((rows, rows), 0), iota((rows, rows), 1)
    source_r, source_c = order_r >> shift, order_c >> shift
    row_c = order_c & (rows - 1)
    same = jnp.where(source_c == source_r, 1.0, 0.0)
    rank_c = jnp.sum(jnp.where(across < down, same, 0.0), axis=1, keepdims=True).astype(I32)
    rank_r = jnp.sum(jnp.where(down < across, same, 0.0), axis=0, keepdims=True).astype(I32)
    owner = one_hot(iota((z.grp * z.dom, rows), 0) == source_r)
    at_rank = iota((rows, z.pair), 1) == rank_c
    high = jnp.where(at_rank, (row_c >> 4).astype(F32), 0.0).astype(BF16)
    low = jnp.where(at_rank, (row_c & 15).astype(F32), 0.0).astype(BF16)
    want = (dot(owner, high) * 16.0 + dot(owner, low)).astype(I32)
    out_ref[...] = jnp.zeros_like(out_ref)
    for d in range(z.grp * z.dom):
        near = z.before(d)
        for line, source in ((0, d), (5, d ^ 1), (6, near), (7, near ^ 1)):
            out_ref[d, line:line + 1, 0:z.pair] = want[source:source + 1, :]
    across_grp = (source_r >> log2(z.dom)) ^ me_ref[0]
    inner = source_r & (z.dom - 1)
    slot = (inner * z.grp + across_grp) * z.pair + rank_r
    for i in range(rows // 128):
        lanes = slot[:, i * 128:(i + 1) * 128]
        out_ref[:, 1 + i:2 + i, :] = jnp.broadcast_to(lanes[None], (z.grp * z.dom, 1, 128))


def product_kernel(z, me_ref, features_ref, weight_ref, *outs):
    half = outs[0].shape[1]
    for flip, out in enumerate(outs):
        at = pl.multiple_of((me_ref[2] ^ flip) * half, half)
        out[...] = dot(features_ref[...], weight_ref[:, pl.ds(at, half)]).astype(BF16)


def send_kernel(z, lines, me_ref, message_ref, own_ref, other_ref, pick_ref, *outs):
    devices, height, width = message_ref.shape
    message = message_ref[...].reshape(devices * height, width)
    high_bits = (message >> 4).astype(F32).astype(BF16)
    low_bits = (message & 15).astype(F32).astype(BF16)
    shape = (z.rows, devices * height)
    asker = (iota(shape, 0) >> log2(z.pair)) ^ (me_ref[0] * z.dom)
    mine = iota((z.rows, width), 1) == (iota((z.rows, width), 0) & (z.pair - 1))
    for rel, (line, product) in enumerate(zip(lines, (own_ref, other_ref))):
        spread = one_hot(iota(shape, 1) == asker * height + line)
        asked = dot(spread, high_bits) * 16.0 + dot(spread, low_bits)
        wanted = jnp.sum(jnp.where(mine, asked, 0.0), axis=1, keepdims=True).astype(I32)
        pick = one_hot(iota((z.rows, z.rows), 1) == wanted)
        if rel == 0:
            pick_ref[...] = pick
        got = dot(pick, product[...]).astype(BF16)
        for s in range(z.grp):
            outs[s][rel] = got[s * z.per_grp:(s + 1) * z.per_grp, :]


def rows_kernel(z, pick_ref, features_ref, *outs):
    for s, out in enumerate(outs):
        pick = pick_ref[s * z.per_grp:(s + 1) * z.per_grp, :]
        out[...] = dot(pick, features_ref[...]).astype(BF16)


def pack_kernel(z, *refs):
    ins, out = refs[:-1], refs[-1]
    for rel in range(2):
        for s in range(z.grp):
            at = (rel * z.grp + s) * z.per_grp
            out[at:at + z.per_grp, :] = ins[s][rel]


def place_kernel(z, me_ref, message_ref, out_ref):
    @pl.loop(0, z.dom)
    def _(n):
        message = message_ref[me_ref[0] * z.dom + n]
        slot = jnp.concatenate([message[1 + i:2 + i, :] for i in range(z.rows // 128)], axis=1)
        rank, at = slot & (z.pair - 1), slot >> log2(z.pair)
        s, at = at & (z.grp - 1), at >> log2(z.grp)
        k, rel = (me_ref[1] - (at >> 1)) & (z.zz - 1), (at & 1) ^ me_ref[2]
        slot = ((k * 2 + rel) * z.grp + s) * z.pair + rank
        out_ref[n] = one_hot(iota((z.rows, z.rows), 0) == slot)


def dense_kernel(cols_ref, vals_ref, out_ref, total):
    tiles, blocks, tile, _ = vals_ref.shape
    count = out_ref.shape[0]

    @pl.loop(0, tiles)
    def _(t):
        total[...] = jnp.zeros_like(total)
        for k in range(blocks):
            at = pl.multiple_of(cols_ref[t, k] * tile, tile)
            total[pl.ds(at, tile), :] += vals_ref[t, k].T.astype(F32)
        left = pl.multiple_of(t * tile, tile)
        out_ref[:, pl.ds(left, tile)] = total[pl.ds(0, count), :].astype(BF16)


def arrange_kernel(z, place_ref, dense_ref, *outs):
    @pl.loop(0, z.dom)
    def _(n):
        at = pl.multiple_of(n * z.rows, z.rows)
        part = dot(place_ref[n], dense_ref[pl.ds(at, z.rows), :]).astype(BF16)
        for k in range(z.zz):
            for p in range(2 * z.grp):
                first = (k * 2 * z.grp + p) * z.pair
                rows = part[first:first + z.pair, :]
                if z.pair % 16 == 0:
                    to = pl.multiple_of(p * z.per_grp + n * z.pair, z.pair)
                    outs[k][pl.ds(to, z.pair), :] = rows
                else:
                    outs[k][p, n] = rows


def turn_kernel(*refs):
    out, height = refs[-1], refs[0].shape[0]
    for s, part in enumerate(refs[:-1]):
        out[:, s * height:(s + 1) * height] = part[...].T


def forward_kernel(z, first, last, *refs):
    turned, refs = refs[:2], refs[2:]
    rows, refs = refs[0][...], refs[1:]
    agg = [dot_rows(ref[...], rows) for ref in turned]
    if not first:
        agg = [part + ref[...] for part, ref in zip(agg, refs)]
        refs = refs[2:]
    if not last:
        for ref, part in zip(refs, agg):
            ref[...] = part
        return
    cots, ahead, hiddens, grads = (refs[2 * i:2 * i + 2] for i in range(4))
    for part, cot, hidden, grad in zip(agg, cots, hiddens, grads):
        sig = jax.nn.sigmoid(part)
        hidden[...] = (part * sig).astype(BF16)
        grad[...] = (cot[...].astype(F32) * (sig * (1.0 + part * (1.0 - sig)))).astype(BF16)
    back_kernel(*ahead, *grads, refs[-1])


def back_kernel(turned_a, turned_b, grad_a, grad_b, out):
    value = dot(turned_a[...], grad_a[...]) + dot(turned_b[...], grad_b[...])
    out[...] = value.astype(out.dtype)


def pass_kernel(mine_ref, come_ref, out_ref):
    out_ref[...] = (mine_ref[...] + come_ref[...].astype(F32)).astype(BF16)


def grad_kernel(z, me_ref, own_a, own_b, near_a, near_b, own_ref, mine_ref, come_ref, *refs):
    outs, whole = refs[:-1], refs[-1]
    own = own_ref[...].astype(BF16)
    near = (mine_ref[...] + come_ref[...].astype(F32)).astype(BF16)
    total = dot(own_a[...], own[:z.rows]) + dot(own_b[...], own[z.rows:])
    total = total + dot(near_a[...], near[:z.rows]) + dot(near_b[...], near[z.rows:])
    whole[...] = total.astype(BF16)
    share = whole.shape[0] // z.grp
    for s in range(z.grp):
        at = pl.multiple_of((me_ref[0] ^ s) * share, share)
        outs[s][...] = whole[pl.ds(at, share), :]


def sum_kernel(*refs):
    refs[-1][...] = sum(term[...].astype(F32) for term in refs[:-1]).astype(BF16)


def last_kernel(z, me_ref, *refs):
    pieces, out = refs[:-1], refs[-1]
    share, half = pieces[0].shape
    for rel in range(2):
        left = pl.multiple_of((me_ref[2] ^ rel) * half, half)
        for s in range(z.grp):
            at = pl.multiple_of((me_ref[0] ^ s) * share, share)
            out[pl.ds(at, share), pl.ds(left, half)] = pieces[rel * z.grp + s][...].astype(F32)


def arrange(z, place, dense, wide, after=()):
    inner = (wide, z.rows) if z.pair % 16 == 0 else (2 * z.grp, z.dom, z.pair, z.rows)
    *got, token = call(
        lambda *refs: arrange_kernel(z, *refs),
        [(inner, BF16)] * z.zz,
        [("v", place), ("v", dense)],
        "arrange", 4, after=after, token=True,
    )
    return [part.reshape(wide, z.rows) for part in got], token


def shards(features, node_order, block_cols, block_count, block_vals, weight, cotangent):
    rows, width_in = features.shape
    hidden_units = weight.shape[1]
    half = hidden_units // 2
    tiles, blocks, tile = block_vals.shape[0], block_vals.shape[1], block_vals.shape[-1]
    z = Sizes(rows, tiles)
    at_grp, at_zz, core = lax.axis_index("grp"), lax.axis_index("zz"), lax.axis_index("core")
    me = jnp.stack([at_grp, at_zz, core]).astype(I32)

    def to_core(x):
        return lax.ppermute(x, "core", [(0, 1), (1, 0)])

    def to_grp(x, s):
        return lax.ppermute(x, "grp", [(i, i ^ s) for i in range(z.grp)]) if s else x

    def to_zz(x, k):
        return lax.ppermute(x, "zz", [(i, (i + k) % z.zz) for i in range(z.zz)]) if k else x

    first_half = features[:rows // 2]
    (message,) = call(
        lambda *refs: index_kernel(z, *refs),
        [((z.grp * z.dom, 8, 128), I32)],
        [("s", me), ("v", node_order.reshape(1, rows))],
        "index", 1,
    )
    message, features = lax.optimization_barrier((message, features))
    message = lax.all_to_all(
        message, ("grp", "zz", "core"), split_axis=0, concat_axis=0, tiled=True
    )
    vals_b = to_core(block_vals)

    def products_of(part, after=()):
        own, other = call(
            lambda *refs: product_kernel(z, *refs),
            [((rows, half), BF16)] * 2,
            [("s", me), ("v", part), ("v", weight)],
            "product", 75, after=after,
        )
        return own, to_core(other)

    def send_of(lines, products):
        return call(
            lambda *refs: send_kernel(z, lines, *refs),
            [((rows, rows), BF16)] + [((2, z.per_grp, half), BF16)] * z.grp,
            [("s", me), ("v", message)] + [("v", part) for part in products],
            "send", 1.5, token=True,
        )

    def across(parts):
        return [to_grp(part, s) for s, part in enumerate(parts)]

    def pack(parts, after=()):
        return call(
            lambda *refs: pack_kernel(z, *refs),
            [((2 * rows, half), BF16)],
            [("v", part) for part in parts],
            "pack", 0.5, after=after,
        )[0]

    def rows_of(pick, part, after):
        return call(
            lambda *refs: rows_kernel(z, *refs),
            [((z.per_grp, width_in), BF16)] * z.grp,
            [("v", pick), ("v", part)],
            "rows", 1, after=after,
        )

    def turned_of(parts):
        left, token = call(
            turn_kernel, [((width_in, rows), BF16)], [("v", part) for part in parts],
            "turn", 0.5, token=True,
        )
        return [left, to_core(left)], token

    products = products_of(features)
    pick, *got, token = send_of((0, 5), products)
    token, cotangent, block_cols, late = lax.optimization_barrier(
        (token, cotangent, block_cols, features)
    )
    came = across(got)

    near = to_zz(late, 1)

    live = iota((tiles, blocks), 1) < block_count[:, None]
    cols_a = jnp.where(live, block_cols, z.dom * tiles)
    cols_b = to_core(cols_a)
    cot_a = lax.dynamic_slice_in_dim(cotangent, core * half, half, axis=1)
    cot_b = to_core(lax.dynamic_slice_in_dim(cotangent, (1 - core) * half, half, axis=1))

    (place,) = call(
        lambda *refs: place_kernel(z, *refs),
        [((z.dom, rows, rows), BF16)],
        [("s", me), ("v", message)],
        "place", 1.5, after=[token],
    )

    def dense_of(cols, vals, after=()):
        return call(
            dense_kernel,
            [((z.dom * rows, rows), BF16)],
            [("s", cols), ("v", vals)],
            "dense", 2.5,
            (pltpu.VMEM((z.dom * rows + tile, tile), F32),), after=after,
        )[0]

    dense_a = dense_of(cols_a, block_vals, [vals_b])

    wide = 2 * z.grp * z.per_grp
    ring = {0: pack(came, [place, dense_a, cols_b])}
    turned_a, _ = arrange(z, place, dense_a, wide, [ring[0]])
    turned_b, token_b = arrange(z, place, dense_of(cols_b, vals_b, [ring[0]]), wide)
    turned = (turned_a, turned_b)
    lefts, token_l = turned_of(across(rows_of(pick, features, [ring[0]])))
    pick_near, *got, token_n = send_of((6, 7), products_of(near, [turned_a[0]]))
    order = list(range(z.zz - 1, 1, -1))
    for k in order:
        ring[k] = to_zz(ring[(k + 1) % z.zz], -1)
        if k == order[0]:
            ring[k], *tokens = lax.optimization_barrier((ring[k], token_b, token_l, token_n))
    came = across(got)
    ring[1] = pack(came)
    held_near = rows_of(pick_near, near, came[1:])

    agg = []
    order = [0] + order[:-1] + [1] + order[-1:]
    for k in order:
        last = k == order[-1]
        ins = [("v", part) for part in (turned[0][k], turned[1][k], ring[k], *agg)]
        outs = [((rows, half), F32)] * 2
        if last:
            ahead = (turned[0][z.zz - 1], turned[1][z.zz - 1])
            ins += [("v", part) for part in (cot_a, cot_b, *ahead)]
            outs = [((rows, half), BF16)] * 4 + [((wide, half), BF16)]
        agg = call(
            lambda *refs, k=k, last=last: forward_kernel(z, k == 0, last, *refs),
            outs, ins, "forward", 3 if last else 1,
            after=held_near if last else [cot_a, cot_b, *tokens] if k == order[1] else (),
        )
    hidden_a, hidden_b, grad_a, grad_b, came = agg

    def back(k):
        return call(
            back_kernel,
            [((wide, half), F32)],
            [("v", part) for part in (turned[0][k], turned[1][k], grad_a, grad_b)],
            "back", 1,
        )[0]

    held_near = across(held_near)
    come = to_core(hidden_b)
    for k in range(z.zz - 2, 0, -1):
        came = to_zz(came, -1)
        mine = back(k)
        if k == 1:
            break
        (came,) = call(
            pass_kernel, [((wide, half), BF16)], [("v", mine), ("v", came)], "pass", 0.5,
            after=[come, *held_near],
        )
    lefts += turned_of(held_near)[0]
    first = core == 0
    hidden = jnp.concatenate(
        [jnp.where(first, hidden_a, come), jnp.where(first, come, hidden_a)], axis=1
    )

    share = width_in // z.grp
    terms = call(
        lambda *refs: grad_kernel(z, *refs),
        [((share, half), BF16)] * z.grp,
        [("s", me)] + [("v", part) for part in (*lefts, back(0), mine, came)],
        "grad", 1.5,
        (pltpu.VMEM((width_in, half), BF16),),
    )

    def total_of(parts):
        return call(
            sum_kernel, [((share, half), BF16)], [("v", part) for part in parts], "sum", 0.5
        )[0]

    mine = total_of([to_grp(terms[s], s) for s in range(z.grp)])
    step = 1
    while step < z.zz:
        mine = total_of(
            [mine, lax.ppermute(mine, "zz", [(i, i ^ step) for i in range(z.zz)])]
        )
        step *= 2
    mine = [to_grp(mine, s) for s in range(z.grp)]
    (grad_weight,) = call(
        lambda *refs: last_kernel(z, *refs),
        [((width_in, hidden_units), F32)],
        [("s", me)] + [("v", part) for part in mine + [to_core(part) for part in mine]],
        "last", 2,
    )
    return hidden, grad_weight


def solution(mesh):
    n_grp, n_dom = mesh.shape["grp"], mesh.shape["dom"]
    split = Mesh(mesh.devices.reshape(n_grp, n_dom // 2, 2), ("grp", "zz", "core"))
    by_rows = ("grp", "zz", "core")
    placed = (
        P(by_rows, None),
        P(by_rows),
        P(by_rows, None),
        P(by_rows),
        P(by_rows, None, None, None),
        P(),
        P(by_rows, None),
    )
    return jax.shard_map(
        shards,
        mesh=split,
        in_specs=placed,
        out_specs=(P(by_rows, None), P()),
        check_vma=False,
    )
```

```python
import jax
import jax.numpy as jnp
from jax import lax
from jax.experimental import pallas as pl
from jax.experimental.pallas import tpu as pltpu
from jax.sharding import Mesh, PartitionSpec as P

BF16 = jnp.bfloat16
F32 = jnp.float32
I32 = jnp.int32


def log2(n):
    assert n & (n - 1) == 0
    return n.bit_length() - 1


def iota(shape, dim):
    return lax.broadcasted_iota(I32, shape, dim)


def one_hot(mask):
    return jnp.where(mask, 1.0, 0.0).astype(BF16)


def dot(a, b):
    return jnp.dot(a, b, preferred_element_type=F32)


def dot_rows(a, b):
    return lax.dot_general(a, b, (((0,), (0,)), ((), ())), preferred_element_type=F32)


def call(body, outs, ins, name, us, scratch=(), after=(), token=False):
    smem = pl.BlockSpec(memory_space=pltpu.SMEM)
    vmem = pl.BlockSpec(memory_space=pltpu.VMEM)
    count = len(ins)
    ties = len(after)
    if token:
        outs = [*outs, ((8, 128), F32)]

    def kernel(*refs):
        refs = refs[:count] + refs[count + ties:]
        if token:
            at = count + len(outs) - 1
            refs[at][...] = jnp.zeros((8, 128), F32)
            refs = refs[:at] + refs[at + 1:]
        body(*refs)

    arrays = [jax.ShapeDtypeStruct(s, d) for s, d in outs] + [value for _, value in ins]
    size = sum(a.size * a.dtype.itemsize for a in arrays + [m.get_array_aval() for m in scratch])
    return pl.pallas_call(
        kernel,
        out_shape=tuple(jax.ShapeDtypeStruct(s, d) for s, d in outs),
        in_specs=[smem if where == "s" else vmem for where, _ in ins]
        + [vmem] * ties,
        out_specs=tuple(vmem for _ in outs),
        scratch_shapes=list(scratch),
        compiler_params=pltpu.CompilerParams(vmem_limit_bytes=size + (5 << 20)),
        cost_estimate=pl.CostEstimate(flops=int(us * 2e7), bytes_accessed=0, transcendentals=0),
        name=name,
    )(*(value for _, value in ins), *after)


class Sizes:
    def __init__(self, rows, tiles):
        self.grp, self.zz = lax.axis_size("grp"), lax.axis_size("zz")
        self.dom = 2 * self.zz
        self.rows, self.tiles = rows, tiles
        self.pair = rows // (self.grp * self.dom)
        self.piece = self.grp * self.pair
        self.per_grp = self.dom * self.pair
        assert rows // 128 < 5 and self.pair <= 128

    def before(self, d):
        inner = d % self.dom
        return d - inner + (inner - 2) % self.dom


def column(row):
    n = row.shape[1]
    on = iota((n, n), 0) == iota((n, n), 1)
    return jnp.sum(jnp.where(on, row.astype(F32), 0.0), axis=1, keepdims=True).astype(I32)


def index_kernel(z, me_ref, order_ref, out_ref):
    rows = z.rows
    shift = log2(rows)
    order_r = order_ref[...]
    order_c = column(order_r)
    down, across = iota((rows, rows), 0), iota((rows, rows), 1)
    source_r, source_c = order_r >> shift, order_c >> shift
    row_c = order_c & (rows - 1)
    same = jnp.where(source_c == source_r, 1.0, 0.0)
    rank_c = jnp.sum(jnp.where(across < down, same, 0.0), axis=1, keepdims=True).astype(I32)
    rank_r = jnp.sum(jnp.where(down < across, same, 0.0), axis=0, keepdims=True).astype(I32)
    owner = one_hot(iota((z.grp * z.dom, rows), 0) == source_r)
    at_rank = iota((rows, z.pair), 1) == rank_c
    high = jnp.where(at_rank, (row_c >> 4).astype(F32), 0.0).astype(BF16)
    low = jnp.where(at_rank, (row_c & 15).astype(F32), 0.0).astype(BF16)
    want = (dot(owner, high) * 16.0 + dot(owner, low)).astype(I32)
    out_ref[...] = jnp.zeros_like(out_ref)
    for d in range(z.grp * z.dom):
        near = z.before(d)
        for line, source in ((0, d), (5, d ^ 1), (6, near), (7, near ^ 1)):
            out_ref[d, line:line + 1, 0:z.pair] = want[source:source + 1, :]
    across_grp = (source_r >> log2(z.dom)) ^ me_ref[0]
    inner = source_r & (z.dom - 1)
    slot = (inner * z.grp + across_grp) * z.pair + rank_r
    for i in range(rows // 128):
        lanes = slot[:, i * 128:(i + 1) * 128]
        out_ref[:, 1 + i:2 + i, :] = jnp.broadcast_to(lanes[None], (z.grp * z.dom, 1, 128))


def product_kernel(z, me_ref, features_ref, weight_ref, *outs):
    half = outs[0].shape[1]
    for flip, out in enumerate(outs):
        at = pl.multiple_of((me_ref[2] ^ flip) * half, half)
        out[...] = dot(features_ref[...], weight_ref[:, pl.ds(at, half)]).astype(BF16)


def send_kernel(z, lines, me_ref, message_ref, own_ref, other_ref, pick_ref, *outs):
    devices, height, width = message_ref.shape
    message = message_ref[...].reshape(devices * height, width)
    high_bits = (message >> 4).astype(F32).astype(BF16)
    low_bits = (message & 15).astype(F32).astype(BF16)
    shape = (z.rows, devices * height)
    asker = (iota(shape, 0) >> log2(z.pair)) ^ (me_ref[0] * z.dom)
    mine = iota((z.rows, width), 1) == (iota((z.rows, width), 0) & (z.pair - 1))
    for rel, (line, product) in enumerate(zip(lines, (own_ref, other_ref))):
        spread = one_hot(iota(shape, 1) == asker * height + line)
        asked = dot(spread, high_bits) * 16.0 + dot(spread, low_bits)
        wanted = jnp.sum(jnp.where(mine, asked, 0.0), axis=1, keepdims=True).astype(I32)
        pick = one_hot(iota((z.rows, z.rows), 1) == wanted)
        if rel == 0:
            pick_ref[...] = pick
        got = dot(pick, product[...]).astype(BF16)
        for s in range(z.grp):
            outs[s][rel] = got[s * z.per_grp:(s + 1) * z.per_grp, :]


def rows_kernel(z, pick_ref, features_ref, *outs):
    for s, out in enumerate(outs):
        pick = pick_ref[s * z.per_grp:(s + 1) * z.per_grp, :]
        out[...] = dot(pick, features_ref[...]).astype(BF16)


def pack_kernel(z, *refs):
    ins, out = refs[:-1], refs[-1]
    for rel in range(2):
        for s in range(z.grp):
            at = (rel * z.grp + s) * z.per_grp
            out[at:at + z.per_grp, :] = ins[s][rel]


def place_kernel(z, me_ref, message_ref, out_ref):
    @pl.loop(0, z.dom)
    def _(n):
        message = message_ref[me_ref[0] * z.dom + n]
        slot = jnp.concatenate([message[1 + i:2 + i, :] for i in range(z.rows // 128)], axis=1)
        rank, at = slot & (z.pair - 1), slot >> log2(z.pair)
        s, at = at & (z.grp - 1), at >> log2(z.grp)
        k, rel = (me_ref[1] - (at >> 1)) & (z.zz - 1), (at & 1) ^ me_ref[2]
        slot = ((k * 2 + rel) * z.grp + s) * z.pair + rank
        out_ref[n] = one_hot(iota((z.rows, z.rows), 0) == slot)


def dense_kernel(cols_ref, vals_ref, out_ref, total):
    tiles, blocks, tile, _ = vals_ref.shape
    count = out_ref.shape[0]

    @pl.loop(0, tiles)
    def _(t):
        total[...] = jnp.zeros_like(total)
        for k in range(blocks):
            at = pl.multiple_of(cols_ref[t, k] * tile, tile)
            total[pl.ds(at, tile), :] += vals_ref[t, k].T.astype(F32)
        left = pl.multiple_of(t * tile, tile)
        out_ref[:, pl.ds(left, tile)] = total[pl.ds(0, count), :].astype(BF16)


def arrange_kernel(z, place_ref, dense_ref, *outs):
    @pl.loop(0, z.dom)
    def _(n):
        at = pl.multiple_of(n * z.rows, z.rows)
        part = dot(place_ref[n], dense_ref[pl.ds(at, z.rows), :]).astype(BF16)
        for k in range(z.zz):
            for p in range(2 * z.grp):
                first = (k * 2 * z.grp + p) * z.pair
                rows = part[first:first + z.pair, :]
                if z.pair % 16 == 0:
                    to = pl.multiple_of(p * z.per_grp + n * z.pair, z.pair)
                    outs[k][pl.ds(to, z.pair), :] = rows
                else:
                    outs[k][p, n] = rows


def turn_kernel(*refs):
    out, height = refs[-1], refs[0].shape[0]
    for s, part in enumerate(refs[:-1]):
        out[:, s * height:(s + 1) * height] = part[...].T


def forward_kernel(z, first, last, *refs):
    turned, refs = refs[:2], refs[2:]
    rows, refs = refs[0][...], refs[1:]
    agg = [dot_rows(ref[...], rows) for ref in turned]
    if not first:
        agg = [part + ref[...] for part, ref in zip(agg, refs)]
        refs = refs[2:]
    if not last:
        for ref, part in zip(refs, agg):
            ref[...] = part
        return
    cots, ahead, hiddens, grads = (refs[2 * i:2 * i + 2] for i in range(4))
    for part, cot, hidden, grad in zip(agg, cots, hiddens, grads):
        sig = jax.nn.sigmoid(part)
        hidden[...] = (part * sig).astype(BF16)
        grad[...] = (cot[...].astype(F32) * (sig * (1.0 + part * (1.0 - sig)))).astype(BF16)
    back_kernel(*ahead, *grads, refs[-1])


def back_kernel(turned_a, turned_b, grad_a, grad_b, out):
    value = dot(turned_a[...], grad_a[...]) + dot(turned_b[...], grad_b[...])
    out[...] = value.astype(out.dtype)


def pass_kernel(mine_ref, come_ref, out_ref):
    out_ref[...] = (mine_ref[...] + come_ref[...].astype(F32)).astype(BF16)


def grad_kernel(z, me_ref, own_a, own_b, near_a, near_b, own_ref, mine_ref, come_ref, *refs):
    outs, whole = refs[:-1], refs[-1]
    own = own_ref[...].astype(BF16)
    near = (mine_ref[...] + come_ref[...].astype(F32)).astype(BF16)
    total = dot(own_a[...], own[:z.rows]) + dot(own_b[...], own[z.rows:])
    total = total + dot(near_a[...], near[:z.rows]) + dot(near_b[...], near[z.rows:])
    whole[...] = total.astype(BF16)
    share = whole.shape[0] // z.grp
    for s in range(z.grp):
        at = pl.multiple_of((me_ref[0] ^ s) * share, share)
        outs[s][...] = whole[pl.ds(at, share), :]


def sum_kernel(*refs):
    refs[-1][...] = sum(term[...].astype(F32) for term in refs[:-1]).astype(BF16)


def last_kernel(z, me_ref, *refs):
    pieces, out = refs[:-1], refs[-1]
    share, half = pieces[0].shape
    for rel in range(2):
        left = pl.multiple_of((me_ref[2] ^ rel) * half, half)
        for s in range(z.grp):
            at = pl.multiple_of((me_ref[0] ^ s) * share, share)
            out[pl.ds(at, share), pl.ds(left, half)] = pieces[rel * z.grp + s][...].astype(F32)


def arrange(z, place, dense, wide, after=()):
    inner = (wide, z.rows) if z.pair % 16 == 0 else (2 * z.grp, z.dom, z.pair, z.rows)
    *got, token = call(
        lambda *refs: arrange_kernel(z, *refs),
        [(inner, BF16)] * z.zz,
        [("v", place), ("v", dense)],
        "arrange", 4, after=after, token=True,
    )
    return [part.reshape(wide, z.rows) for part in got], token


def shards(features, node_order, block_cols, block_count, block_vals, weight, cotangent):
    rows, width_in = features.shape
    hidden_units = weight.shape[1]
    half = hidden_units // 2
    tiles, blocks, tile = block_vals.shape[0], block_vals.shape[1], block_vals.shape[-1]
    z = Sizes(rows, tiles)
    at_grp, at_zz, core = lax.axis_index("grp"), lax.axis_index("zz"), lax.axis_index("core")
    me = jnp.stack([at_grp, at_zz, core]).astype(I32)

    def to_core(x):
        return lax.ppermute(x, "core", [(0, 1), (1, 0)])

    def to_grp(x, s):
        return lax.ppermute(x, "grp", [(i, i ^ s) for i in range(z.grp)]) if s else x

    def to_zz(x, k):
        return lax.ppermute(x, "zz", [(i, (i + k) % z.zz) for i in range(z.zz)]) if k else x

    first_half = features[:rows // 2]
    (message,) = call(
        lambda *refs: index_kernel(z, *refs),
        [((z.grp * z.dom, 8, 128), I32)],
        [("s", me), ("v", node_order.reshape(1, rows))],
        "index", 1,
    )
    message, features = lax.optimization_barrier((message, features))
    message = lax.all_to_all(
        message, ("grp", "zz", "core"), split_axis=0, concat_axis=0, tiled=True
    )
    vals_b = to_core(block_vals)

    def products_of(part, after=()):
        own, other = call(
            lambda *refs: product_kernel(z, *refs),
            [((rows, half), BF16)] * 2,
            [("s", me), ("v", part), ("v", weight)],
            "product", 75, after=after,
        )
        return own, to_core(other)

    def send_of(lines, products, after=()):
        return call(
            lambda *refs: send_kernel(z, lines, *refs),
            [((rows, rows), BF16)] + [((2, z.per_grp, half), BF16)] * z.grp,
            [("s", me), ("v", message)] + [("v", part) for part in products],
            "send", 1.5, after=after, token=True,
        )

    def across(parts):
        return [to_grp(part, s) for s, part in enumerate(parts)]

    def pack(parts, after=()):
        return call(
            lambda *refs: pack_kernel(z, *refs),
            [((2 * rows, half), BF16)],
            [("v", part) for part in parts],
            "pack", 0.5, after=after, token=True,
        )

    def rows_of(pick, part, after):
        return call(
            lambda *refs: rows_kernel(z, *refs),
            [((z.per_grp, width_in), BF16)] * z.grp,
            [("v", pick), ("v", part)],
            "rows", 1, after=after, token=True,
        )

    def turned_of(parts):
        left, token = call(
            turn_kernel, [((width_in, rows), BF16)], [("v", part) for part in parts],
            "turn", 0.5, token=True,
        )
        return [left, to_core(left)], token

    products = products_of(features)
    pick, *got, token = send_of((0, 5), products)
    token, cotangent, block_cols, late = lax.optimization_barrier(
        (token, cotangent, block_cols, features)
    )
    came = across(got)

    near = to_zz(late, 1)

    live = iota((tiles, blocks), 1) < block_count[:, None]
    cols_a = jnp.where(live, block_cols, z.dom * tiles)
    cols_b = to_core(cols_a)
    cot_a = lax.dynamic_slice_in_dim(cotangent, core * half, half, axis=1)
    cot_b = to_core(lax.dynamic_slice_in_dim(cotangent, (1 - core) * half, half, axis=1))

    place, token_p = call(
        lambda *refs: place_kernel(z, *refs),
        [((z.dom, rows, rows), BF16)],
        [("s", me), ("v", message)],
        "place", 1.5, after=[token], token=True,
    )

    def dense_of(cols, vals, after=()):
        return call(
            dense_kernel,
            [((z.dom * rows, rows), BF16)],
            [("s", cols), ("v", vals)],
            "dense", 2.5,
            (pltpu.VMEM((z.dom * rows + tile, tile), F32),), after=after, token=True,
        )

    dense_a, token_a = dense_of(cols_a, block_vals)

    wide = 2 * z.grp * z.per_grp
    first, token = pack(came, [token_p, token_a])
    ring = {0: first}
    *picked, token_r = rows_of(pick, features, [token])
    held = across(picked)
    turned_a, token = arrange(z, place, dense_a, wide, [token_r])
    dense_b, token = dense_of(cols_b, vals_b, [token])
    turned_b, token = arrange(z, place, dense_b, wide)
    turned = (turned_a, turned_b)
    lefts, token_l = turned_of(held)
    products = products_of(near, [token, token_l])
    order = list(range(z.zz - 1, 1, -1))
    for k in order:
        ring[k] = to_zz(ring[(k + 1) % z.zz], -1)
        if k == order[0]:
            ring[k], token = lax.optimization_barrier((ring[k], token))
            pick_near, *got, _ = send_of((6, 7), products, [token])
    ring[1], token_k = pack(across(got))
    *picked, token_r = rows_of(pick_near, near, [token_k])
    held_near = across(picked)

    agg = []
    order = [0] + order[:-1] + [1] + order[-1:]
    for k in order:
        last = k == order[-1]
        ins = [("v", part) for part in (turned[0][k], turned[1][k], ring[k], *agg)]
        outs = [((rows, half), F32)] * 2
        if last:
            ahead = (turned[0][z.zz - 1], turned[1][z.zz - 1])
            ins += [("v", part) for part in (cot_a, cot_b, *ahead)]
            outs = [((rows, half), BF16)] * 4 + [((wide, half), BF16)]
        agg = call(
            lambda *refs, k=k, last=last: forward_kernel(z, k == 0, last, *refs),
            outs, ins, "forward", 3 if last else 1,
            after=[token_r] if last else [cot_a, cot_b] if k == order[1] else (),
        )
    hidden_a, hidden_b, grad_a, grad_b, came = agg

    def back(k):
        return call(
            back_kernel,
            [((wide, half), F32)],
            [("v", part) for part in (turned[0][k], turned[1][k], grad_a, grad_b)],
            "back", 1,
        )[0]

    come = to_core(hidden_b)
    for k in range(z.zz - 2, 0, -1):
        came = to_zz(came, -1)
        mine = back(k)
        if k == 1:
            break
        (came,) = call(
            pass_kernel, [((wide, half), BF16)], [("v", mine), ("v", came)], "pass", 0.5,
            after=[come],
        )
    lefts += turned_of(held_near)[0]
    first = core == 0
    hidden = jnp.concatenate(
        [jnp.where(first, hidden_a, come), jnp.where(first, come, hidden_a)], axis=1
    )

    share = width_in // z.grp
    terms = call(
        lambda *refs: grad_kernel(z, *refs),
        [((share, half), BF16)] * z.grp,
        [("s", me)] + [("v", part) for part in (*lefts, back(0), mine, came)],
        "grad", 1.5,
        (pltpu.VMEM((width_in, half), BF16),),
    )

    def total_of(parts):
        return call(
            sum_kernel, [((share, half), BF16)], [("v", part) for part in parts], "sum", 0.5
        )[0]

    mine = total_of([to_grp(terms[s], s) for s in range(z.grp)])
    step = 1
    while step < z.zz:
        mine = total_of(
            [mine, lax.ppermute(mine, "zz", [(i, i ^ step) for i in range(z.zz)])]
        )
        step *= 2
    mine = [to_grp(mine, s) for s in range(z.grp)]
    (grad_weight,) = call(
        lambda *refs: last_kernel(z, *refs),
        [((width_in, hidden_units), F32)],
        [("s", me)] + [("v", part) for part in mine + [to_core(part) for part in mine]],
        "last", 2,
    )
    return hidden, grad_weight


def solution(mesh):
    n_grp, n_dom = mesh.shape["grp"], mesh.shape["dom"]
    split = Mesh(mesh.devices.reshape(n_grp, n_dom // 2, 2), ("grp", "zz", "core"))
    by_rows = ("grp", "zz", "core")
    placed = (
        P(by_rows, None),
        P(by_rows),
        P(by_rows, None),
        P(by_rows),
        P(by_rows, None, None, None),
        P(),
        P(by_rows, None),
    )
    return jax.shard_map(
        shards,
        mesh=split,
        in_specs=placed,
        out_specs=(P(by_rows, None), P()),
        check_vma=False,
    )
```

```python
import jax
import jax.numpy as jnp
from jax import lax
from jax.experimental import pallas as pl
from jax.experimental.pallas import tpu as pltpu
from jax.sharding import Mesh, PartitionSpec as P

BF16 = jnp.bfloat16
F32 = jnp.float32
I32 = jnp.int32


def log2(n):
    assert n & (n - 1) == 0
    return n.bit_length() - 1


def iota(shape, dim):
    return lax.broadcasted_iota(I32, shape, dim)


def one_hot(mask):
    return jnp.where(mask, 1.0, 0.0).astype(BF16)


def dot(a, b):
    return jnp.dot(a, b, preferred_element_type=F32)


def dot_rows(a, b):
    return lax.dot_general(a, b, (((0,), (0,)), ((), ())), preferred_element_type=F32)


def call(body, outs, ins, name, us, scratch=(), after=(), token=False):
    smem = pl.BlockSpec(memory_space=pltpu.SMEM)
    vmem = pl.BlockSpec(memory_space=pltpu.VMEM)
    count = len(ins)
    ties = len(after)
    if token:
        outs = [*outs, ((8, 128), F32)]

    def kernel(*refs):
        refs = refs[:count] + refs[count + ties:]
        if token:
            at = count + len(outs) - 1
            refs[at][...] = jnp.zeros((8, 128), F32)
            refs = refs[:at] + refs[at + 1:]
        body(*refs)

    arrays = [jax.ShapeDtypeStruct(s, d) for s, d in outs] + [value for _, value in ins]
    size = sum(a.size * a.dtype.itemsize for a in arrays + [m.get_array_aval() for m in scratch])
    return pl.pallas_call(
        kernel,
        out_shape=tuple(jax.ShapeDtypeStruct(s, d) for s, d in outs),
        in_specs=[smem if where == "s" else vmem for where, _ in ins]
        + [vmem] * ties,
        out_specs=tuple(vmem for _ in outs),
        scratch_shapes=list(scratch),
        compiler_params=pltpu.CompilerParams(vmem_limit_bytes=size + (5 << 20)),
        cost_estimate=pl.CostEstimate(flops=int(us * 1e8), bytes_accessed=0, transcendentals=0),
        name=name,
    )(*(value for _, value in ins), *after)


class Sizes:
    def __init__(self, rows, tiles):
        self.grp, self.zz = lax.axis_size("grp"), lax.axis_size("zz")
        self.dom = 2 * self.zz
        self.rows, self.tiles = rows, tiles
        self.pair = rows // (self.grp * self.dom)
        self.piece = self.grp * self.pair
        self.per_grp = self.dom * self.pair
        assert rows // 128 < 5 and self.pair <= 128


def column(row):
    n = row.shape[1]
    on = iota((n, n), 0) == iota((n, n), 1)
    return jnp.sum(jnp.where(on, row.astype(F32), 0.0), axis=1, keepdims=True).astype(I32)


def index_kernel(z, me_ref, order_ref, out_ref):
    rows = z.rows
    shift = log2(rows)
    order_r = order_ref[...]
    order_c = column(order_r)
    down, across = iota((rows, rows), 0), iota((rows, rows), 1)
    source_r, source_c = order_r >> shift, order_c >> shift
    row_c = order_c & (rows - 1)
    same = jnp.where(source_c == source_r, 1.0, 0.0)
    rank_c = jnp.sum(jnp.where(across < down, same, 0.0), axis=1, keepdims=True).astype(I32)
    rank_r = jnp.sum(jnp.where(down < across, same, 0.0), axis=0, keepdims=True).astype(I32)
    owner = one_hot(iota((z.grp * z.dom, rows), 0) == source_r)
    at_rank = iota((rows, z.pair), 1) == rank_c
    high = jnp.where(at_rank, (row_c >> 4).astype(F32), 0.0).astype(BF16)
    low = jnp.where(at_rank, (row_c & 15).astype(F32), 0.0).astype(BF16)
    want = (dot(owner, high) * 16.0 + dot(owner, low)).astype(I32)
    out_ref[...] = jnp.zeros_like(out_ref)
    for d in range(z.grp * z.dom):
        for line, source in ((0, d), (5, d ^ 1)):
            out_ref[d, line:line + 1, 0:z.pair] = want[source:source + 1, :]
    across_grp = (source_r >> log2(z.dom)) ^ me_ref[0]
    inner = source_r & (z.dom - 1)
    slot = (inner * z.grp + across_grp) * z.pair + rank_r
    for i in range(rows // 128):
        lanes = slot[:, i * 128:(i + 1) * 128]
        out_ref[:, 1 + i:2 + i, :] = jnp.broadcast_to(lanes[None], (z.grp * z.dom, 1, 128))


def product_kernel(z, me_ref, features_ref, weight_ref, *outs):
    half = outs[0].shape[1]
    for flip, out in enumerate(outs):
        at = pl.multiple_of((me_ref[2] ^ flip) * half, half)
        out[...] = dot(features_ref[...], weight_ref[:, pl.ds(at, half)]).astype(BF16)


def send_kernel(z, lines, me_ref, message_ref, own_ref, other_ref, pick_ref, *outs):
    devices, height, width = message_ref.shape
    message = message_ref[...].reshape(devices * height, width)
    high_bits = (message >> 4).astype(F32).astype(BF16)
    low_bits = (message & 15).astype(F32).astype(BF16)
    shape = (z.rows, devices * height)
    asker = (iota(shape, 0) >> log2(z.pair)) ^ (me_ref[0] * z.dom)
    mine = iota((z.rows, width), 1) == (iota((z.rows, width), 0) & (z.pair - 1))
    for rel, (line, product) in enumerate(zip(lines, (own_ref, other_ref))):
        spread = one_hot(iota(shape, 1) == asker * height + line)
        asked = dot(spread, high_bits) * 16.0 + dot(spread, low_bits)
        wanted = jnp.sum(jnp.where(mine, asked, 0.0), axis=1, keepdims=True).astype(I32)
        pick = one_hot(iota((z.rows, z.rows), 1) == wanted)
        if rel == 0:
            pick_ref[...] = pick
        got = dot(pick, product[...]).astype(BF16)
        for s in range(z.grp):
            outs[s][rel] = got[s * z.per_grp:(s + 1) * z.per_grp, :]


def rows_kernel(z, pick_ref, features_ref, *outs):
    for s, out in enumerate(outs):
        pick = pick_ref[s * z.per_grp:(s + 1) * z.per_grp, :]
        out[...] = dot(pick, features_ref[...]).astype(BF16)


def pack_kernel(z, *refs):
    ins, outs = refs[:z.grp], refs[z.grp:]
    for rel, out in enumerate(outs):
        for s in range(z.grp):
            out[s * z.per_grp:(s + 1) * z.per_grp, :] = ins[s][rel]


def prepare_kernel(z, me_ref, cols_ref, message_ref, vals_ref, *refs):
    outs, (total, dense) = refs[:z.zz], refs[z.zz:]
    tiles, blocks, tile, _ = vals_ref.shape

    @pl.loop(0, tiles)
    def _(t):
        total[...] = jnp.zeros_like(total)
        for k in range(blocks):
            at = pl.multiple_of(cols_ref[t, k] * tile, tile)
            total[pl.ds(at, tile), :] += vals_ref[t, k].T.astype(F32)
        left = pl.multiple_of(t * tile, tile)
        dense[:, pl.ds(left, tile)] = total[pl.ds(0, z.dom * z.rows), :].astype(BF16)

    @pl.loop(0, z.dom)
    def _(n):
        message = message_ref[me_ref[0] * z.dom + n]
        slot = jnp.concatenate([message[1 + i:2 + i, :] for i in range(z.rows // 128)], axis=1)
        rank, at = slot & (z.pair - 1), slot >> log2(z.pair)
        s, at = at & (z.grp - 1), at >> log2(z.grp)
        k, rel = (me_ref[1] - (at >> 1)) & (z.zz - 1), (at & 1) ^ me_ref[2]
        slot = ((k * 2 + rel) * z.grp + s) * z.pair + rank
        place = one_hot(iota((z.rows, z.rows), 0) == slot)
        at = pl.multiple_of(n * z.rows, z.rows)
        part = dot(place, dense[pl.ds(at, z.rows), :]).astype(BF16)
        for k in range(z.zz):
            for p in range(2 * z.grp):
                first = (k * 2 * z.grp + p) * z.pair
                rows = part[first:first + z.pair, :]
                if z.pair % 16 == 0:
                    to = pl.multiple_of(p * z.per_grp + n * z.pair, z.pair)
                    outs[k][pl.ds(to, z.pair), :] = rows
                else:
                    outs[k][p, n] = rows


def turn_kernel(*refs):
    out, height = refs[-1], refs[0].shape[0]
    for s, part in enumerate(refs[:-1]):
        out[:, s * height:(s + 1) * height] = part[...].T


def forward_kernel(z, first, last, *refs):
    turned, refs = refs[:2], refs[2:]
    rows, refs = jnp.concatenate([ref[...] for ref in refs[:2]], axis=0), refs[2:]
    agg = [dot_rows(ref[...], rows) for ref in turned]
    if not first:
        agg = [part + ref[...] for part, ref in zip(agg, refs)]
        refs = refs[2:]
    if not last:
        for ref, part in zip(refs, agg):
            ref[...] = part
        return
    cots, ahead, hiddens, grads = (refs[2 * i:2 * i + 2] for i in range(4))
    for part, cot, hidden, grad in zip(agg, cots, hiddens, grads):
        sig = jax.nn.sigmoid(part)
        hidden[...] = (part * sig).astype(BF16)
        grad[...] = (cot[...].astype(F32) * (sig * (1.0 + part * (1.0 - sig)))).astype(BF16)
    back_kernel(*ahead, *grads, *refs[-2:])


def back_kernel(turned_a, turned_b, grad_a, grad_b, *outs):
    size = outs[0].shape[0]
    for i, out in enumerate(outs):
        rows = pl.ds(i * size, size)
        value = dot(turned_a[rows, :], grad_a[...]) + dot(turned_b[rows, :], grad_b[...])
        out[...] = value.astype(out.dtype)


def pass_kernel(mine_ref, come_ref, out_ref):
    out_ref[...] = (mine_ref[...] + come_ref[...].astype(F32)).astype(BF16)


def grad_kernel(z, me_ref, left_a, left_b, mine_a, mine_b, come_a, come_b, *refs):
    outs, whole = refs[:-1], refs[-1]
    grads = [
        (mine[...] + come[...].astype(F32)).astype(BF16)
        for mine, come in ((mine_a, come_a), (mine_b, come_b))
    ]
    whole[...] = (dot(left_a[...], grads[0]) + dot(left_b[...], grads[1])).astype(BF16)
    share = whole.shape[0] // z.grp
    for s in range(z.grp):
        at = pl.multiple_of((me_ref[0] ^ s) * share, share)
        outs[s][...] = whole[pl.ds(at, share), :]


def sum_kernel(*refs):
    refs[-1][...] = sum(term[...].astype(F32) for term in refs[:-1]).astype(BF16)


def last_kernel(z, me_ref, *refs):
    pieces, out = refs[:-1], refs[-1]
    share, half = pieces[0].shape
    for rel in range(2):
        left = pl.multiple_of((me_ref[2] ^ rel) * half, half)
        for s in range(z.grp):
            at = pl.multiple_of((me_ref[0] ^ s) * share, share)
            out[pl.ds(at, share), pl.ds(left, half)] = pieces[rel * z.grp + s][...].astype(F32)


def shards(features, node_order, block_cols, block_count, block_vals, weight, cotangent):
    rows, width_in = features.shape
    hidden_units = weight.shape[1]
    half = hidden_units // 2
    tiles, blocks, tile = block_vals.shape[0], block_vals.shape[1], block_vals.shape[-1]
    z = Sizes(rows, tiles)
    at_grp, at_zz, core = lax.axis_index("grp"), lax.axis_index("zz"), lax.axis_index("core")
    me = jnp.stack([at_grp, at_zz, core]).astype(I32)

    def to_core(x):
        return lax.ppermute(x, "core", [(0, 1), (1, 0)])

    def to_grp(x, s):
        return lax.ppermute(x, "grp", [(i, i ^ s) for i in range(z.grp)]) if s else x

    def to_zz(x, k):
        return lax.ppermute(x, "zz", [(i, (i + k) % z.zz) for i in range(z.zz)]) if k else x

    first_half = features[:rows // 2]
    (message,) = call(
        lambda *refs: index_kernel(z, *refs),
        [((z.grp * z.dom, 8, 128), I32)],
        [("s", me), ("v", node_order.reshape(1, rows))],
        "index", 1,
    )
    message, features = lax.optimization_barrier((message, features))
    message = lax.all_to_all(
        message, ("grp", "zz", "core"), split_axis=0, concat_axis=0, tiled=True
    )
    vals_b = to_core(block_vals)

    def products_of(part, after=()):
        own, other = call(
            lambda *refs: product_kernel(z, *refs),
            [((rows, half), BF16)] * 2,
            [("s", me), ("v", part), ("v", weight)],
            "product", 15, after=after,
        )
        return own, to_core(other)

    def send_of(lines, products, after=()):
        return call(
            lambda *refs: send_kernel(z, lines, *refs),
            [((rows, rows), BF16)] + [((2, z.per_grp, half), BF16)] * z.grp,
            [("s", me), ("v", message)] + [("v", part) for part in products],
            "send", 1.5, after=after, token=True,
        )

    def across(parts):
        return [to_grp(part, s) for s, part in enumerate(parts)]

    def pack(parts, after=()):
        return call(
            lambda *refs: pack_kernel(z, *refs),
            [((rows, half), BF16)] * 2,
            [("v", part) for part in parts],
            "pack", 0.5, after=after, token=True,
        )

    def rows_of(pick, part, after):
        return call(
            lambda *refs: rows_kernel(z, *refs),
            [((z.per_grp, width_in), BF16)] * z.grp,
            [("v", pick), ("v", part)],
            "rows", 1, after=after, token=True,
        )

    def turned_of(parts):
        left, token = call(
            turn_kernel, [((width_in, rows), BF16)], [("v", part) for part in parts],
            "turn", 0.5, token=True,
        )
        return [left, to_core(left)], token

    products = products_of(features)
    pick, *got, token = send_of((0, 5), products)
    token, cotangent = lax.optimization_barrier((token, cotangent))
    *ring, token = pack(across(got), [token])
    ring = [ring]

    live = iota((tiles, blocks), 1) < block_count[:, None]
    cols_a = jnp.where(live, block_cols, z.dom * tiles)
    cols_b = to_core(cols_a)
    cot_a = lax.dynamic_slice_in_dim(cotangent, core * half, half, axis=1)
    cot_b = to_core(lax.dynamic_slice_in_dim(cotangent, (1 - core) * half, half, axis=1))

    wide = 2 * z.grp * z.per_grp
    inner = (wide, rows) if z.pair % 16 == 0 else (2 * z.grp, z.dom, z.pair, rows)

    def prepared(cols, vals, token):
        *got, token = call(
            lambda *refs: prepare_kernel(z, *refs),
            [(inner, BF16)] * z.zz,
            [("s", me), ("s", cols), ("v", message), ("v", vals)],
            "prepare", 7,
            (
                pltpu.VMEM((z.dom * rows + tile, tile), F32),
                pltpu.VMEM((z.dom * rows, rows), BF16),
            ),
            after=[token], token=True,
        )
        return [part.reshape(wide, rows) for part in got], token

    turned = []
    for k in range(1, z.zz):
        ring.append([to_zz(part, 1) for part in ring[-1]])
        if k < 3:
            got, token = prepared(*((cols_a, block_vals), (cols_b, vals_b))[k - 1], token)
            turned.append(got)
            ring[k][0], token = lax.optimization_barrier((ring[k][0], token))

    agg = []
    for k in range(z.zz):
        last = k == z.zz - 1
        ins = [("v", part) for part in (turned[0][k], turned[1][k], *ring[k], *agg)]
        outs = [((rows, half), F32)] * 2
        if last:
            ahead = (turned[0][k], turned[1][k])
            ins += [("v", part) for part in (cot_a, cot_b, *ahead)]
            outs = [((rows, half), BF16)] * 6
        agg = call(
            lambda *refs, k=k, last=last: forward_kernel(z, k == 0, last, *refs),
            outs, ins, "forward", 3 if last else 1,
            after=[cot_a, cot_b] if k == z.zz - 2 else (),
        )
    hidden_a, hidden_b, grad_a, grad_b, *came = agg

    def back(k):
        return call(
            back_kernel,
            [((rows, half), F32)] * 2,
            [("v", part) for part in (turned[0][k], turned[1][k], grad_a, grad_b)],
            "back", 1,
        )

    come = to_core(hidden_b)
    for k in range(z.zz - 2, -1, -1):
        came = [to_zz(part, -1) for part in came]
        mine = back(k)
        if k:
            passed = [
                call(
                    pass_kernel, [((rows, half), BF16)], [("v", part), ("v", moved)], "pass", 0.5,
                    after=[come] if i == 1 and k == 1 else (), token=True,
                )
                for i, (part, moved) in enumerate(zip(mine, came))
            ]
            came = [part for part, _ in passed]
            if k == z.zz - 2:
                *picked, _ = rows_of(pick, features, [passed[1][1]])
                lefts, _ = turned_of(across(picked))
    first = core == 0
    hidden = jnp.concatenate(
        [jnp.where(first, hidden_a, come), jnp.where(first, come, hidden_a)], axis=1
    )

    share = width_in // z.grp
    terms = call(
        lambda *refs: grad_kernel(z, *refs),
        [((share, half), BF16)] * z.grp,
        [("s", me)] + [("v", part) for part in (*lefts, *mine, *came)],
        "grad", 1.5,
        (pltpu.VMEM((width_in, half), BF16),),
    )

    def total_of(parts):
        return call(
            sum_kernel, [((share, half), BF16)], [("v", part) for part in parts], "sum", 0.5
        )[0]

    mine = total_of([to_grp(terms[s], s) for s in range(z.grp)])
    step = 1
    while step < z.zz:
        mine = total_of(
            [mine, lax.ppermute(mine, "zz", [(i, i ^ step) for i in range(z.zz)])]
        )
        step *= 2
    mine = [to_grp(mine, s) for s in range(z.grp)]
    (grad_weight,) = call(
        lambda *refs: last_kernel(z, *refs),
        [((width_in, hidden_units), F32)],
        [("s", me)] + [("v", part) for part in mine + [to_core(part) for part in mine]],
        "last", 2,
    )
    return hidden, grad_weight


def solution(mesh):
    n_grp, n_dom = mesh.shape["grp"], mesh.shape["dom"]
    split = Mesh(mesh.devices.reshape(n_grp, n_dom // 2, 2), ("grp", "zz", "core"))
    by_rows = ("grp", "zz", "core")
    placed = (
        P(by_rows, None),
        P(by_rows),
        P(by_rows, None),
        P(by_rows),
        P(by_rows, None, None, None),
        P(),
        P(by_rows, None),
    )
    return jax.shard_map(
        shards,
        mesh=split,
        in_specs=placed,
        out_specs=(P(by_rows, None), P()),
        check_vma=False,
    )
```

```python
import jax
import jax.numpy as jnp
from jax import lax
from jax.experimental import pallas as pl
from jax.experimental.pallas import tpu as pltpu
from jax.sharding import Mesh, PartitionSpec as P

BF16 = jnp.bfloat16
F32 = jnp.float32
I32 = jnp.int32


def log2(n):
    assert n & (n - 1) == 0
    return n.bit_length() - 1


def iota(shape, dim):
    return lax.broadcasted_iota(I32, shape, dim)


def one_hot(mask):
    return jnp.where(mask, 1.0, 0.0).astype(BF16)


def dot(a, b):
    return jnp.dot(a, b, preferred_element_type=F32)


def dot_rows(a, b):
    return lax.dot_general(a, b, (((0,), (0,)), ((), ())), preferred_element_type=F32)


def call(body, outs, ins, name, us, scratch=(), after=(), token=False):
    smem = pl.BlockSpec(memory_space=pltpu.SMEM)
    vmem = pl.BlockSpec(memory_space=pltpu.VMEM)
    count = len(ins)
    ties = len(after)
    if token:
        outs = [*outs, ((8, 128), F32)]

    def kernel(*refs):
        refs = refs[:count] + refs[count + ties:]
        if token:
            at = count + len(outs) - 1
            refs[at][...] = jnp.zeros((8, 128), F32)
            refs = refs[:at] + refs[at + 1:]
        body(*refs)

    arrays = [jax.ShapeDtypeStruct(s, d) for s, d in outs] + [value for _, value in ins]
    size = sum(a.size * a.dtype.itemsize for a in arrays + [m.get_array_aval() for m in scratch])
    return pl.pallas_call(
        kernel,
        out_shape=tuple(jax.ShapeDtypeStruct(s, d) for s, d in outs),
        in_specs=[smem if where == "s" else vmem for where, _ in ins]
        + [vmem] * ties,
        out_specs=tuple(vmem for _ in outs),
        scratch_shapes=list(scratch),
        compiler_params=pltpu.CompilerParams(vmem_limit_bytes=size + (5 << 20)),
        cost_estimate=pl.CostEstimate(flops=int(us * 1e8), bytes_accessed=0, transcendentals=0),
        name=name,
    )(*(value for _, value in ins), *after)


class Sizes:
    def __init__(self, rows, tiles):
        self.grp, self.zz = lax.axis_size("grp"), lax.axis_size("zz")
        self.dom = 2 * self.zz
        self.rows, self.tiles = rows, tiles
        self.pair = rows // (self.grp * self.dom)
        self.piece = self.grp * self.pair
        self.per_grp = self.dom * self.pair
        assert rows // 128 < 5 and self.pair <= 128


def column(row):
    n = row.shape[1]
    on = iota((n, n), 0) == iota((n, n), 1)
    return jnp.sum(jnp.where(on, row.astype(F32), 0.0), axis=1, keepdims=True).astype(I32)


def index_kernel(z, me_ref, order_ref, out_ref):
    rows = z.rows
    shift = log2(rows)
    order_r = order_ref[...]
    order_c = column(order_r)
    down, across = iota((rows, rows), 0), iota((rows, rows), 1)
    source_r, source_c = order_r >> shift, order_c >> shift
    row_c = order_c & (rows - 1)
    same = jnp.where(source_c == source_r, 1.0, 0.0)
    rank_c = jnp.sum(jnp.where(across < down, same, 0.0), axis=1, keepdims=True).astype(I32)
    rank_r = jnp.sum(jnp.where(down < across, same, 0.0), axis=0, keepdims=True).astype(I32)
    owner = one_hot(iota((z.grp * z.dom, rows), 0) == source_r)
    at_rank = iota((rows, z.pair), 1) == rank_c
    high = jnp.where(at_rank, (row_c >> 4).astype(F32), 0.0).astype(BF16)
    low = jnp.where(at_rank, (row_c & 15).astype(F32), 0.0).astype(BF16)
    want = (dot(owner, high) * 16.0 + dot(owner, low)).astype(I32)
    out_ref[...] = jnp.zeros_like(out_ref)
    for d in range(z.grp * z.dom):
        for line, source in ((0, d), (5, d ^ 1)):
            out_ref[d, line:line + 1, 0:z.pair] = want[source:source + 1, :]
    across_grp = (source_r >> log2(z.dom)) ^ me_ref[0]
    inner = source_r & (z.dom - 1)
    slot = (inner * z.grp + across_grp) * z.pair + rank_r
    for i in range(rows // 128):
        lanes = slot[:, i * 128:(i + 1) * 128]
        out_ref[:, 1 + i:2 + i, :] = jnp.broadcast_to(lanes[None], (z.grp * z.dom, 1, 128))


def product_kernel(z, me_ref, features_ref, weight_ref, *outs):
    half = outs[0].shape[1]
    for flip, out in enumerate(outs):
        at = pl.multiple_of((me_ref[2] ^ flip) * half, half)
        out[...] = dot(features_ref[...], weight_ref[:, pl.ds(at, half)]).astype(BF16)


def send_kernel(z, lines, me_ref, message_ref, own_ref, other_ref, pick_ref, *outs):
    devices, height, width = message_ref.shape
    message = message_ref[...].reshape(devices * height, width)
    high_bits = (message >> 4).astype(F32).astype(BF16)
    low_bits = (message & 15).astype(F32).astype(BF16)
    shape = (z.rows, devices * height)
    asker = (iota(shape, 0) >> log2(z.pair)) ^ (me_ref[0] * z.dom)
    mine = iota((z.rows, width), 1) == (iota((z.rows, width), 0) & (z.pair - 1))
    for rel, (line, product) in enumerate(zip(lines, (own_ref, other_ref))):
        spread = one_hot(iota(shape, 1) == asker * height + line)
        asked = dot(spread, high_bits) * 16.0 + dot(spread, low_bits)
        wanted = jnp.sum(jnp.where(mine, asked, 0.0), axis=1, keepdims=True).astype(I32)
        pick = one_hot(iota((z.rows, z.rows), 1) == wanted)
        if rel == 0:
            pick_ref[...] = pick
        got = dot(pick, product[...]).astype(BF16)
        for s in range(z.grp):
            outs[s][rel] = got[s * z.per_grp:(s + 1) * z.per_grp, :]


def rows_kernel(z, pick_ref, features_ref, *outs):
    for s, out in enumerate(outs):
        pick = pick_ref[s * z.per_grp:(s + 1) * z.per_grp, :]
        out[...] = dot(pick, features_ref[...]).astype(BF16)


def pack_kernel(z, *refs):
    ins, outs = refs[:z.grp], refs[z.grp:]
    for rel, out in enumerate(outs):
        for s in range(z.grp):
            out[s * z.per_grp:(s + 1) * z.per_grp, :] = ins[s][rel]


def prepare_kernel(z, me_ref, cols_ref, message_ref, vals_ref, *refs):
    outs, (total, dense) = refs[:z.zz], refs[z.zz:]
    tiles, blocks, tile, _ = vals_ref.shape

    @pl.loop(0, tiles)
    def _(t):
        total[...] = jnp.zeros_like(total)
        for k in range(blocks):
            at = pl.multiple_of(cols_ref[t, k] * tile, tile)
            total[pl.ds(at, tile), :] += vals_ref[t, k].T.astype(F32)
        left = pl.multiple_of(t * tile, tile)
        dense[:, pl.ds(left, tile)] = total[pl.ds(0, z.dom * z.rows), :].astype(BF16)

    @pl.loop(0, z.dom)
    def _(n):
        message = message_ref[me_ref[0] * z.dom + n]
        slot = jnp.concatenate([message[1 + i:2 + i, :] for i in range(z.rows // 128)], axis=1)
        rank, at = slot & (z.pair - 1), slot >> log2(z.pair)
        s, at = at & (z.grp - 1), at >> log2(z.grp)
        k, rel = (me_ref[1] - (at >> 1)) & (z.zz - 1), (at & 1) ^ me_ref[2]
        slot = ((k * 2 + rel) * z.grp + s) * z.pair + rank
        place = one_hot(iota((z.rows, z.rows), 0) == slot)
        at = pl.multiple_of(n * z.rows, z.rows)
        part = dot(place, dense[pl.ds(at, z.rows), :]).astype(BF16)
        for k in range(z.zz):
            for p in range(2 * z.grp):
                first = (k * 2 * z.grp + p) * z.pair
                rows = part[first:first + z.pair, :]
                if z.pair % 16 == 0:
                    to = pl.multiple_of(p * z.per_grp + n * z.pair, z.pair)
                    outs[k][pl.ds(to, z.pair), :] = rows
                else:
                    outs[k][p, n] = rows


def turn_kernel(*refs):
    out, height = refs[-1], refs[0].shape[0]
    for s, part in enumerate(refs[:-1]):
        out[:, s * height:(s + 1) * height] = part[...].T


def forward_kernel(z, first, last, *refs):
    turned, refs = refs[:2], refs[2:]
    rows, refs = jnp.concatenate([ref[...] for ref in refs[:2]], axis=0), refs[2:]
    agg = [dot_rows(ref[...], rows) for ref in turned]
    if not first:
        agg = [part + ref[...] for part, ref in zip(agg, refs)]
        refs = refs[2:]
    if not last:
        for ref, part in zip(refs, agg):
            ref[...] = part
        return
    cots, ahead, hiddens, grads = (refs[2 * i:2 * i + 2] for i in range(4))
    for part, cot, hidden, grad in zip(agg, cots, hiddens, grads):
        sig = jax.nn.sigmoid(part)
        hidden[...] = (part * sig).astype(BF16)
        grad[...] = (cot[...].astype(F32) * (sig * (1.0 + part * (1.0 - sig)))).astype(BF16)
    back_kernel(*ahead, *grads, *refs[-2:])


def back_kernel(turned_a, turned_b, grad_a, grad_b, *outs):
    size = outs[0].shape[0]
    for i, out in enumerate(outs):
        rows = pl.ds(i * size, size)
        value = dot(turned_a[rows, :], grad_a[...]) + dot(turned_b[rows, :], grad_b[...])
        out[...] = value.astype(out.dtype)


def pass_kernel(mine_ref, come_ref, out_ref):
    out_ref[...] = (mine_ref[...] + come_ref[...].astype(F32)).astype(BF16)


def grad_kernel(z, me_ref, left_a, left_b, mine_a, mine_b, come_a, come_b, *refs):
    outs, whole = refs[:-1], refs[-1]
    grads = [
        (mine[...] + come[...].astype(F32)).astype(BF16)
        for mine, come in ((mine_a, come_a), (mine_b, come_b))
    ]
    whole[...] = (dot(left_a[...], grads[0]) + dot(left_b[...], grads[1])).astype(BF16)
    share = whole.shape[0] // z.grp
    for s in range(z.grp):
        at = pl.multiple_of((me_ref[0] ^ s) * share, share)
        outs[s][...] = whole[pl.ds(at, share), :]


def sum_kernel(*refs):
    refs[-1][...] = sum(term[...].astype(F32) for term in refs[:-1]).astype(BF16)


def last_kernel(z, me_ref, *refs):
    pieces, out = refs[:-1], refs[-1]
    share, half = pieces[0].shape
    for rel in range(2):
        left = pl.multiple_of((me_ref[2] ^ rel) * half, half)
        for s in range(z.grp):
            at = pl.multiple_of((me_ref[0] ^ s) * share, share)
            out[pl.ds(at, share), pl.ds(left, half)] = pieces[rel * z.grp + s][...].astype(F32)


def shards(features, node_order, block_cols, block_count, block_vals, weight, cotangent):
    rows, width_in = features.shape
    hidden_units = weight.shape[1]
    half = hidden_units // 2
    tiles, blocks, tile = block_vals.shape[0], block_vals.shape[1], block_vals.shape[-1]
    z = Sizes(rows, tiles)
    at_grp, at_zz, core = lax.axis_index("grp"), lax.axis_index("zz"), lax.axis_index("core")
    me = jnp.stack([at_grp, at_zz, core]).astype(I32)

    def to_core(x):
        return lax.ppermute(x, "core", [(0, 1), (1, 0)])

    def to_grp(x, s):
        return lax.ppermute(x, "grp", [(i, i ^ s) for i in range(z.grp)]) if s else x

    def to_zz(x, k):
        return lax.ppermute(x, "zz", [(i, (i + k) % z.zz) for i in range(z.zz)]) if k else x

    first_half = features[:rows // 2]
    (message,) = call(
        lambda *refs: index_kernel(z, *refs),
        [((z.grp * z.dom, 8, 128), I32)],
        [("s", me), ("v", node_order.reshape(1, rows))],
        "index", 1,
    )
    message, features = lax.optimization_barrier((message, features))
    message = lax.all_to_all(
        message, ("grp", "zz", "core"), split_axis=0, concat_axis=0, tiled=True
    )
    vals_b = to_core(block_vals)

    def products_of(part, after=()):
        own, other = call(
            lambda *refs: product_kernel(z, *refs),
            [((rows, half), BF16)] * 2,
            [("s", me), ("v", part), ("v", weight)],
            "product", 15, after=after,
        )
        return own, to_core(other)

    def send_of(lines, products, after=()):
        return call(
            lambda *refs: send_kernel(z, lines, *refs),
            [((rows, rows), BF16)] + [((2, z.per_grp, half), BF16)] * z.grp,
            [("s", me), ("v", message)] + [("v", part) for part in products],
            "send", 1.5, after=after, token=True,
        )

    def across(parts):
        return [to_grp(part, s) for s, part in enumerate(parts)]

    def pack(parts, after=()):
        return call(
            lambda *refs: pack_kernel(z, *refs),
            [((rows, half), BF16)] * 2,
            [("v", part) for part in parts],
            "pack", 0.5, after=after, token=True,
        )

    def rows_of(pick, part, after):
        return call(
            lambda *refs: rows_kernel(z, *refs),
            [((z.per_grp, width_in), BF16)] * z.grp,
            [("v", pick), ("v", part)],
            "rows", 1, after=after, token=True,
        )

    def turned_of(parts):
        left, token = call(
            turn_kernel, [((width_in, rows), BF16)], [("v", part) for part in parts],
            "turn", 0.5, token=True,
        )
        return [left, to_core(left)], token

    products = products_of(features)
    pick, *got, token = send_of((0, 5), products)
    token, cotangent = lax.optimization_barrier((token, cotangent))
    *ring, token = pack(across(got), [token])
    ring = [ring]

    live = iota((tiles, blocks), 1) < block_count[:, None]
    cols_a = jnp.where(live, block_cols, z.dom * tiles)
    cols_b = to_core(cols_a)
    cot_a = lax.dynamic_slice_in_dim(cotangent, core * half, half, axis=1)
    cot_b = to_core(lax.dynamic_slice_in_dim(cotangent, (1 - core) * half, half, axis=1))

    wide = 2 * z.grp * z.per_grp
    inner = (wide, rows) if z.pair % 16 == 0 else (2 * z.grp, z.dom, z.pair, rows)

    def prepared(cols, vals, token):
        *got, token = call(
            lambda *refs: prepare_kernel(z, *refs),
            [(inner, BF16)] * z.zz,
            [("s", me), ("s", cols), ("v", message), ("v", vals)],
            "prepare", 7,
            (
                pltpu.VMEM((z.dom * rows + tile, tile), F32),
                pltpu.VMEM((z.dom * rows, rows), BF16),
            ),
            after=[token], token=True,
        )
        return [part.reshape(wide, rows) for part in got], token

    for k in range(1, z.zz):
        ring.append([to_zz(part, 1) for part in ring[-1]])
        if k == 1:
            turned_a, token = prepared(cols_a, block_vals, token)
            ring[1][0], token = lax.optimization_barrier((ring[1][0], token))
            *picked, token = rows_of(pick, features, [token])
            lefts, token_l = turned_of(across(picked))
        if k == 2:
            turned_b, token = prepared(cols_b, vals_b, token)
            ring[2][0], token = lax.optimization_barrier((ring[2][0], token))
    turned = (turned_a, turned_b)

    agg = []
    for k in range(z.zz):
        last = k == z.zz - 1
        ins = [("v", part) for part in (turned[0][k], turned[1][k], *ring[k], *agg)]
        outs = [((rows, half), F32)] * 2
        if last:
            ahead = (turned[0][k], turned[1][k])
            ins += [("v", part) for part in (cot_a, cot_b, *ahead)]
            outs = [((rows, half), BF16)] * 6
        agg = call(
            lambda *refs, k=k, last=last: forward_kernel(z, k == 0, last, *refs),
            outs, ins, "forward", 3 if last else 1,
            after=[cot_a, cot_b, token_l] if k == z.zz - 2 else [token] if k == 0 else (),
        )
    hidden_a, hidden_b, grad_a, grad_b, *came = agg

    def back(k):
        return call(
            back_kernel,
            [((rows, half), F32)] * 2,
            [("v", part) for part in (turned[0][k], turned[1][k], grad_a, grad_b)],
            "back", 1,
        )

    come = to_core(hidden_b)
    for k in range(z.zz - 2, -1, -1):
        came = [to_zz(part, -1) for part in came]
        mine = back(k)
        if k:
            passed = [
                call(
                    pass_kernel, [((rows, half), BF16)], [("v", part), ("v", moved)], "pass", 0.5,
                    after=[come] if i == 1 and k == 1 else (), token=True,
                )
                for i, (part, moved) in enumerate(zip(mine, came))
            ]
            came = [part for part, _ in passed]
    first = core == 0
    hidden = jnp.concatenate(
        [jnp.where(first, hidden_a, come), jnp.where(first, come, hidden_a)], axis=1
    )

    share = width_in // z.grp
    terms = call(
        lambda *refs: grad_kernel(z, *refs),
        [((share, half), BF16)] * z.grp,
        [("s", me)] + [("v", part) for part in (*lefts, *mine, *came)],
        "grad", 1.5,
        (pltpu.VMEM((width_in, half), BF16),),
    )

    def total_of(parts):
        return call(
            sum_kernel, [((share, half), BF16)], [("v", part) for part in parts], "sum", 0.5
        )[0]

    mine = total_of([to_grp(terms[s], s) for s in range(z.grp)])
    step = 1
    while step < z.zz:
        mine = total_of(
            [mine, lax.ppermute(mine, "zz", [(i, i ^ step) for i in range(z.zz)])]
        )
        step *= 2
    mine = [to_grp(mine, s) for s in range(z.grp)]
    (grad_weight,) = call(
        lambda *refs: last_kernel(z, *refs),
        [((width_in, hidden_units), F32)],
        [("s", me)] + [("v", part) for part in mine + [to_core(part) for part in mine]],
        "last", 2,
    )
    return hidden, grad_weight


def solution(mesh):
    n_grp, n_dom = mesh.shape["grp"], mesh.shape["dom"]
    split = Mesh(mesh.devices.reshape(n_grp, n_dom // 2, 2), ("grp", "zz", "core"))
    by_rows = ("grp", "zz", "core")
    placed = (
        P(by_rows, None),
        P(by_rows),
        P(by_rows, None),
        P(by_rows),
        P(by_rows, None, None, None),
        P(),
        P(by_rows, None),
    )
    return jax.shard_map(
        shards,
        mesh=split,
        in_specs=placed,
        out_specs=(P(by_rows, None), P()),
        check_vma=False,
    )
```

```python
import jax
import jax.numpy as jnp
from jax import lax
from jax.experimental import pallas as pl
from jax.experimental.pallas import tpu as pltpu
from jax.sharding import Mesh, PartitionSpec as P

BF16 = jnp.bfloat16
F32 = jnp.float32
I32 = jnp.int32


def log2(n):
    assert n & (n - 1) == 0
    return n.bit_length() - 1


def iota(shape, dim):
    return lax.broadcasted_iota(I32, shape, dim)


def one_hot(mask):
    return jnp.where(mask, 1.0, 0.0).astype(BF16)


def dot(a, b):
    return jnp.dot(a, b, preferred_element_type=F32)


def dot_rows(a, b):
    return lax.dot_general(a, b, (((0,), (0,)), ((), ())), preferred_element_type=F32)


def call(body, outs, ins, name, us, scratch=(), after=(), token=False):
    smem = pl.BlockSpec(memory_space=pltpu.SMEM)
    vmem = pl.BlockSpec(memory_space=pltpu.VMEM)
    count = len(ins)
    ties = len(after)
    if token:
        outs = [*outs, ((8, 128), F32)]

    def kernel(*refs):
        refs = refs[:count] + refs[count + ties:]
        if token:
            at = count + len(outs) - 1
            refs[at][...] = jnp.zeros((8, 128), F32)
            refs = refs[:at] + refs[at + 1:]
        body(*refs)

    arrays = [jax.ShapeDtypeStruct(s, d) for s, d in outs] + [value for _, value in ins]
    size = sum(a.size * a.dtype.itemsize for a in arrays + [m.get_array_aval() for m in scratch])
    return pl.pallas_call(
        kernel,
        out_shape=tuple(jax.ShapeDtypeStruct(s, d) for s, d in outs),
        in_specs=[smem if where == "s" else vmem for where, _ in ins]
        + [vmem] * ties,
        out_specs=tuple(vmem for _ in outs),
        scratch_shapes=list(scratch),
        compiler_params=pltpu.CompilerParams(vmem_limit_bytes=size + (5 << 20)),
        cost_estimate=pl.CostEstimate(flops=int(us * 1e8), bytes_accessed=0, transcendentals=0),
        name=name,
    )(*(value for _, value in ins), *after)


class Sizes:
    def __init__(self, rows, tiles):
        self.grp, self.zz = lax.axis_size("grp"), lax.axis_size("zz")
        self.dom = 2 * self.zz
        self.rows, self.tiles = rows, tiles
        self.pair = rows // (self.grp * self.dom)
        self.piece = self.grp * self.pair
        self.per_grp = self.dom * self.pair
        assert rows // 128 < 5 and self.pair <= 128


def column(row):
    n = row.shape[1]
    on = iota((n, n), 0) == iota((n, n), 1)
    return jnp.sum(jnp.where(on, row.astype(F32), 0.0), axis=1, keepdims=True).astype(I32)


def index_kernel(z, me_ref, order_ref, out_ref):
    rows = z.rows
    shift = log2(rows)
    order_r = order_ref[...]
    order_c = column(order_r)
    down, across = iota((rows, rows), 0), iota((rows, rows), 1)
    source_r, source_c = order_r >> shift, order_c >> shift
    row_c = order_c & (rows - 1)
    same = jnp.where(source_c == source_r, 1.0, 0.0)
    rank_c = jnp.sum(jnp.where(across < down, same, 0.0), axis=1, keepdims=True).astype(I32)
    rank_r = jnp.sum(jnp.where(down < across, same, 0.0), axis=0, keepdims=True).astype(I32)
    owner = one_hot(iota((z.grp * z.dom, rows), 0) == source_r)
    at_rank = iota((rows, z.pair), 1) == rank_c
    high = jnp.where(at_rank, (row_c >> 4).astype(F32), 0.0).astype(BF16)
    low = jnp.where(at_rank, (row_c & 15).astype(F32), 0.0).astype(BF16)
    want = (dot(owner, high) * 16.0 + dot(owner, low)).astype(I32)
    out_ref[...] = jnp.zeros_like(out_ref)
    for d in range(z.grp * z.dom):
        out_ref[d, 0:1, 0:z.pair] = want[d:d + 1, :]
    across_grp = (source_r >> log2(z.dom)) ^ me_ref[0]
    inner = source_r & (z.dom - 1)
    slot = (inner * z.grp + across_grp) * z.pair + rank_r
    for i in range(rows // 128):
        lanes = slot[:, i * 128:(i + 1) * 128]
        out_ref[:, 1 + i:2 + i, :] = jnp.broadcast_to(lanes[None], (z.grp * z.dom, 1, 128))


def product_kernel(z, me_ref, features_ref, weight_ref, *outs):
    half = outs[0].shape[1]
    for flip, out in enumerate(outs):
        at = pl.multiple_of((me_ref[2] ^ flip) * half, half)
        out[...] = dot(features_ref[...], weight_ref[:, pl.ds(at, half)]).astype(BF16)


def send_kernel(z, me_ref, message_ref, own_ref, other_ref, pick_ref, *outs):
    devices, height, width = message_ref.shape
    message = message_ref[...].reshape(devices * height, width)
    shape = (z.rows, devices * height)
    asker = (iota(shape, 0) >> log2(z.pair)) ^ (me_ref[0] * z.dom)
    spread = one_hot(iota(shape, 1) == asker * height)
    high = dot(spread, (message >> 4).astype(F32).astype(BF16))
    low = dot(spread, (message & 15).astype(F32).astype(BF16))
    mine = iota((z.rows, width), 1) == (iota((z.rows, width), 0) & (z.pair - 1))
    wanted = jnp.sum(jnp.where(mine, high * 16.0 + low, 0.0), axis=1, keepdims=True).astype(I32)
    pick_ref[...] = one_hot(iota((z.rows, z.rows), 1) == wanted)
    for flip, product in enumerate((own_ref, other_ref)):
        got = dot(pick_ref[...], product[...]).astype(BF16)
        for s in range(z.grp):
            outs[s][flip] = got[s * z.per_grp:(s + 1) * z.per_grp, :]


def rows_kernel(z, pick_ref, features_ref, *outs):
    for s, out in enumerate(outs):
        pick = pick_ref[s * z.per_grp:(s + 1) * z.per_grp, :]
        out[...] = dot(pick, features_ref[...]).astype(BF16)


def pack_kernel(z, *refs):
    ins, outs = refs[:z.grp], refs[z.grp:]
    for rel, out in enumerate(outs):
        for s in range(z.grp):
            out[s * z.per_grp:(s + 1) * z.per_grp, :] = ins[s][rel]


def prepare_kernel(z, me_ref, cols_ref, message_ref, vals_ref, *refs):
    outs, (total, dense) = refs[:z.zz], refs[z.zz:]
    tiles, blocks, tile, _ = vals_ref.shape

    @pl.loop(0, tiles)
    def _(t):
        total[...] = jnp.zeros_like(total)
        for k in range(blocks):
            at = pl.multiple_of(cols_ref[t, k] * tile, tile)
            total[pl.ds(at, tile), :] += vals_ref[t, k].T.astype(F32)
        left = pl.multiple_of(t * tile, tile)
        dense[:, pl.ds(left, tile)] = total[pl.ds(0, z.dom * z.rows), :].astype(BF16)

    @pl.loop(0, z.dom)
    def _(n):
        message = message_ref[me_ref[0] * z.dom + n]
        slot = jnp.concatenate([message[1 + i:2 + i, :] for i in range(z.rows // 128)], axis=1)
        rank, at = slot & (z.pair - 1), slot >> log2(z.pair)
        s, at = at & (z.grp - 1), at >> log2(z.grp)
        k, rel = (me_ref[1] - (at >> 1)) & (z.zz - 1), (at & 1) ^ me_ref[2]
        slot = ((k * 2 + rel) * z.grp + s) * z.pair + rank
        place = one_hot(iota((z.rows, z.rows), 0) == slot)
        at = pl.multiple_of(n * z.rows, z.rows)
        part = dot(place, dense[pl.ds(at, z.rows), :]).astype(BF16)
        for k in range(z.zz):
            for p in range(2 * z.grp):
                first = (k * 2 * z.grp + p) * z.pair
                rows = part[first:first + z.pair, :]
                if z.pair % 16 == 0:
                    to = pl.multiple_of(p * z.per_grp + n * z.pair, z.pair)
                    outs[k][pl.ds(to, z.pair), :] = rows
                else:
                    outs[k][p, n] = rows


def turn_kernel(*refs):
    out, height = refs[-1], refs[0].shape[0]
    for s, part in enumerate(refs[:-1]):
        out[:, s * height:(s + 1) * height] = part[...].T


def forward_kernel(z, first, last, *refs):
    turned, refs = refs[:2], refs[2:]
    rows, refs = jnp.concatenate([ref[...] for ref in refs[:2]], axis=0), refs[2:]
    agg = [dot_rows(ref[...], rows) for ref in turned]
    if not first:
        agg = [part + ref[...] for part, ref in zip(agg, refs)]
        refs = refs[2:]
    if not last:
        for ref, part in zip(refs, agg):
            ref[...] = part
        return
    cots, ahead, hiddens, grads = (refs[2 * i:2 * i + 2] for i in range(4))
    for part, cot, hidden, grad in zip(agg, cots, hiddens, grads):
        sig = jax.nn.sigmoid(part)
        hidden[...] = (part * sig).astype(BF16)
        grad[...] = (cot[...].astype(F32) * (sig * (1.0 + part * (1.0 - sig)))).astype(BF16)
    back_kernel(*ahead, *grads, *refs[-2:])


def back_kernel(turned_a, turned_b, grad_a, grad_b, *outs):
    size = outs[0].shape[0]
    for i, out in enumerate(outs):
        rows = pl.ds(i * size, size)
        value = dot(turned_a[rows, :], grad_a[...]) + dot(turned_b[rows, :], grad_b[...])
        out[...] = value.astype(out.dtype)


def pass_kernel(mine_ref, come_ref, out_ref):
    out_ref[...] = (mine_ref[...] + come_ref[...].astype(F32)).astype(BF16)


def grad_kernel(z, me_ref, left_a, left_b, mine_a, mine_b, come_a, come_b, *refs):
    outs, whole = refs[:-1], refs[-1]
    grads = [
        (mine[...] + come[...].astype(F32)).astype(BF16)
        for mine, come in ((mine_a, come_a), (mine_b, come_b))
    ]
    whole[...] = (dot(left_a[...], grads[0]) + dot(left_b[...], grads[1])).astype(BF16)
    share = whole.shape[0] // z.grp
    for s in range(z.grp):
        at = pl.multiple_of((me_ref[0] ^ s) * share, share)
        outs[s][...] = whole[pl.ds(at, share), :]


def sum_kernel(*refs):
    refs[-1][...] = sum(term[...].astype(F32) for term in refs[:-1]).astype(BF16)


def last_kernel(z, me_ref, *refs):
    pieces, out = refs[:-1], refs[-1]
    share, half = pieces[0].shape
    for rel in range(2):
        left = pl.multiple_of((me_ref[2] ^ rel) * half, half)
        for s in range(z.grp):
            at = pl.multiple_of((me_ref[0] ^ s) * share, share)
            out[pl.ds(at, share), pl.ds(left, half)] = pieces[rel * z.grp + s][...].astype(F32)


def shards(features, node_order, block_cols, block_count, block_vals, weight, cotangent):
    rows, width_in = features.shape
    hidden_units = weight.shape[1]
    half = hidden_units // 2
    tiles, blocks, tile = block_vals.shape[0], block_vals.shape[1], block_vals.shape[-1]
    z = Sizes(rows, tiles)
    at_grp, at_zz, core = lax.axis_index("grp"), lax.axis_index("zz"), lax.axis_index("core")
    me = jnp.stack([at_grp, at_zz, core]).astype(I32)

    def to_core(x):
        return lax.ppermute(x, "core", [(0, 1), (1, 0)])

    def to_grp(x, s):
        return lax.ppermute(x, "grp", [(i, i ^ s) for i in range(z.grp)]) if s else x

    def to_zz(x, k):
        return lax.ppermute(x, "zz", [(i, (i + k) % z.zz) for i in range(z.zz)]) if k else x

    first_half = features[:rows // 2]
    (message,) = call(
        lambda *refs: index_kernel(z, *refs),
        [((z.grp * z.dom, 8, 128), I32)],
        [("s", me), ("v", node_order.reshape(1, rows))],
        "index", 1,
    )
    message, features = lax.optimization_barrier((message, features))
    message = lax.all_to_all(
        message, ("grp", "zz", "core"), split_axis=0, concat_axis=0, tiled=True
    )
    vals_b = to_core(block_vals)

    def across(parts):
        return [to_grp(part, s) for s, part in enumerate(parts)]

    def pack(parts, after=()):
        return call(
            lambda *refs: pack_kernel(z, *refs),
            [((rows, half), BF16)] * 2,
            [("v", part) for part in parts],
            "pack", 0.5, after=after, token=True,
        )

    def rows_of(pick, part, after):
        return call(
            lambda *refs: rows_kernel(z, *refs),
            [((z.per_grp, width_in), BF16)] * z.grp,
            [("v", pick), ("v", part)],
            "rows", 1, after=after, token=True,
        )

    def turned_of(parts):
        left, token = call(
            turn_kernel, [((width_in, rows), BF16)], [("v", part) for part in parts],
            "turn", 0.5, token=True,
        )
        return [left, to_core(left)], token

    products = call(
        lambda *refs: product_kernel(z, *refs),
        [((rows, half), BF16)] * 2,
        [("s", me), ("v", features), ("v", weight)],
        "product", 15,
    )
    pick, *got, token = call(
        lambda *refs: send_kernel(z, *refs),
        [((rows, rows), BF16)] + [((2, z.per_grp, half), BF16)] * z.grp,
        [("s", me), ("v", message)] + [("v", part) for part in products],
        "send", 1.5, token=True,
    )
    token, cotangent, block_cols = lax.optimization_barrier((token, cotangent, block_cols))
    own, other, token = pack(across(got), [token])
    ring = [[own, to_core(other)]]

    live = iota((tiles, blocks), 1) < block_count[:, None]
    cols_a = jnp.where(live, block_cols, z.dom * tiles)
    cols_b = to_core(cols_a)
    cot_a = lax.dynamic_slice_in_dim(cotangent, core * half, half, axis=1)
    cot_b = to_core(lax.dynamic_slice_in_dim(cotangent, (1 - core) * half, half, axis=1))

    wide = 2 * z.grp * z.per_grp
    inner = (wide, rows) if z.pair % 16 == 0 else (2 * z.grp, z.dom, z.pair, rows)

    def prepared(cols, vals, token):
        *got, token = call(
            lambda *refs: prepare_kernel(z, *refs),
            [(inner, BF16)] * z.zz,
            [("s", me), ("s", cols), ("v", message), ("v", vals)],
            "prepare", 7,
            (
                pltpu.VMEM((z.dom * rows + tile, tile), F32),
                pltpu.VMEM((z.dom * rows, rows), BF16),
            ),
            after=[token, cols_b], token=True,
        )
        return [part.reshape(wide, rows) for part in got], token

    for k in range(1, z.zz):
        ring.append([to_zz(part, 1) for part in ring[-1]])
        if k == 1:
            *picked, token = rows_of(pick, features, [token, cot_a, cot_b])
            lefts, token_l = turned_of(across(picked))
            turned_a, token = prepared(cols_a, block_vals, token)
            ring[1][0], token = lax.optimization_barrier((ring[1][0], token))
        if k == 2:
            turned_b, token = prepared(cols_b, vals_b, token)
            ring[2][0], token = lax.optimization_barrier((ring[2][0], token))
    turned = (turned_a, turned_b)

    agg = []
    for k in range(z.zz):
        last = k == z.zz - 1
        ins = [("v", part) for part in (turned[0][k], turned[1][k], *ring[k], *agg)]
        outs = [((rows, half), F32)] * 2
        if last:
            ahead = (turned[0][k], turned[1][k])
            ins += [("v", part) for part in (cot_a, cot_b, *ahead)]
            outs = [((rows, half), BF16)] * 6
        agg = call(
            lambda *refs, k=k, last=last: forward_kernel(z, k == 0, last, *refs),
            outs, ins, "forward", 3 if last else 1,
            after=[token_l] if k == z.zz - 2 else [token] if k == 0 else (),
        )
    hidden_a, hidden_b, grad_a, grad_b, *came = agg

    def back(k):
        return call(
            back_kernel,
            [((rows, half), F32)] * 2,
            [("v", part) for part in (turned[0][k], turned[1][k], grad_a, grad_b)],
            "back", 1,
        )

    come = to_core(hidden_b)
    for k in range(z.zz - 2, -1, -1):
        came = [to_zz(part, -1) for part in came]
        mine = back(k)
        if k:
            passed = [
                call(
                    pass_kernel, [((rows, half), BF16)], [("v", part), ("v", moved)], "pass", 0.5,
                    after=[come] if i == 1 and k == 1 else (), token=True,
                )
                for i, (part, moved) in enumerate(zip(mine, came))
            ]
            came = [part for part, _ in passed]
    first = core == 0
    hidden = jnp.concatenate(
        [jnp.where(first, hidden_a, come), jnp.where(first, come, hidden_a)], axis=1
    )

    share = width_in // z.grp
    terms = call(
        lambda *refs: grad_kernel(z, *refs),
        [((share, half), BF16)] * z.grp,
        [("s", me)] + [("v", part) for part in (*lefts, *mine, *came)],
        "grad", 1.5,
        (pltpu.VMEM((width_in, half), BF16),),
    )

    def total_of(parts):
        return call(
            sum_kernel, [((share, half), BF16)], [("v", part) for part in parts], "sum", 0.5
        )[0]

    mine = total_of([to_grp(terms[s], s) for s in range(z.grp)])
    step = 1
    while step < z.zz:
        mine = total_of(
            [mine, lax.ppermute(mine, "zz", [(i, i ^ step) for i in range(z.zz)])]
        )
        step *= 2
    mine = [to_grp(mine, s) for s in range(z.grp)]
    (grad_weight,) = call(
        lambda *refs: last_kernel(z, *refs),
        [((width_in, hidden_units), F32)],
        [("s", me)] + [("v", part) for part in mine + [to_core(part) for part in mine]],
        "last", 2,
    )
    return hidden, grad_weight


def solution(mesh):
    n_grp, n_dom = mesh.shape["grp"], mesh.shape["dom"]
    split = Mesh(mesh.devices.reshape(n_grp, n_dom // 2, 2), ("grp", "zz", "core"))
    by_rows = ("grp", "zz", "core")
    placed = (
        P(by_rows, None),
        P(by_rows),
        P(by_rows, None),
        P(by_rows),
        P(by_rows, None, None, None),
        P(),
        P(by_rows, None),
    )
    return jax.shard_map(
        shards,
        mesh=split,
        in_specs=placed,
        out_specs=(P(by_rows, None), P()),
        check_vma=False,
    )
```

```python
import jax
import jax.numpy as jnp
from jax import lax
from jax.experimental import pallas as pl
from jax.experimental.pallas import tpu as pltpu
from jax.sharding import Mesh, PartitionSpec as P

BF16 = jnp.bfloat16
F32 = jnp.float32
I32 = jnp.int32


def log2(n):
    assert n & (n - 1) == 0
    return n.bit_length() - 1


def iota(shape, dim):
    return lax.broadcasted_iota(I32, shape, dim)


def one_hot(mask):
    return jnp.where(mask, 1.0, 0.0).astype(BF16)


def dot(a, b):
    return jnp.dot(a, b, preferred_element_type=F32)


def dot_rows(a, b):
    return lax.dot_general(a, b, (((0,), (0,)), ((), ())), preferred_element_type=F32)


def call(body, outs, ins, name, us, scratch=(), after=(), token=False):
    smem = pl.BlockSpec(memory_space=pltpu.SMEM)
    vmem = pl.BlockSpec(memory_space=pltpu.VMEM)
    count = len(ins)
    ties = len(after)
    if token:
        outs = [*outs, ((8, 128), F32)]

    def kernel(*refs):
        refs = refs[:count] + refs[count + ties:]
        if token:
            at = count + len(outs) - 1
            refs[at][...] = jnp.zeros((8, 128), F32)
            refs = refs[:at] + refs[at + 1:]
        body(*refs)

    arrays = [jax.ShapeDtypeStruct(s, d) for s, d in outs] + [value for _, value in ins]
    size = sum(a.size * a.dtype.itemsize for a in arrays + [m.get_array_aval() for m in scratch])
    return pl.pallas_call(
        kernel,
        out_shape=tuple(jax.ShapeDtypeStruct(s, d) for s, d in outs),
        in_specs=[smem if where == "s" else vmem for where, _ in ins]
        + [vmem] * ties,
        out_specs=tuple(vmem for _ in outs),
        scratch_shapes=list(scratch),
        compiler_params=pltpu.CompilerParams(vmem_limit_bytes=size + (5 << 20)),
        cost_estimate=pl.CostEstimate(flops=int(us * 1e8), bytes_accessed=0, transcendentals=0),
        name=name,
    )(*(value for _, value in ins), *after)


class Sizes:
    def __init__(self, rows, tiles):
        self.grp, self.zz = lax.axis_size("grp"), lax.axis_size("zz")
        self.dom = 2 * self.zz
        self.rows, self.tiles = rows, tiles
        self.pair = rows // (self.grp * self.dom)
        self.piece = self.grp * self.pair
        self.per_grp = self.dom * self.pair
        assert rows // 128 < 5 and self.pair <= 128


def column(row):
    n = row.shape[1]
    on = iota((n, n), 0) == iota((n, n), 1)
    return jnp.sum(jnp.where(on, row.astype(F32), 0.0), axis=1, keepdims=True).astype(I32)


def index_kernel(z, me_ref, order_ref, out_ref):
    rows = z.rows
    shift = log2(rows)
    order_r = order_ref[...]
    order_c = column(order_r)
    down, across = iota((rows, rows), 0), iota((rows, rows), 1)
    source_r, source_c = order_r >> shift, order_c >> shift
    row_c = order_c & (rows - 1)
    same = jnp.where(source_c == source_r, 1.0, 0.0)
    rank_c = jnp.sum(jnp.where(across < down, same, 0.0), axis=1, keepdims=True).astype(I32)
    rank_r = jnp.sum(jnp.where(down < across, same, 0.0), axis=0, keepdims=True).astype(I32)
    owner = one_hot(iota((z.grp * z.dom, rows), 0) == source_r)
    at_rank = iota((rows, z.pair), 1) == rank_c
    high = jnp.where(at_rank, (row_c >> 4).astype(F32), 0.0).astype(BF16)
    low = jnp.where(at_rank, (row_c & 15).astype(F32), 0.0).astype(BF16)
    want = (dot(owner, high) * 16.0 + dot(owner, low)).astype(I32)
    out_ref[...] = jnp.zeros_like(out_ref)
    for d in range(z.grp * z.dom):
        out_ref[d, 0:1, 0:z.pair] = want[d:d + 1, :]
    across_grp = (source_r >> log2(z.dom)) ^ me_ref[0]
    inner = source_r & (z.dom - 1)
    slot = (inner * z.grp + across_grp) * z.pair + rank_r
    for i in range(rows // 128):
        lanes = slot[:, i * 128:(i + 1) * 128]
        out_ref[:, 1 + i:2 + i, :] = jnp.broadcast_to(lanes[None], (z.grp * z.dom, 1, 128))


def product_kernel(z, me_ref, features_ref, weight_ref, *outs):
    half = outs[0].shape[1]
    for flip, out in enumerate(outs):
        at = pl.multiple_of((me_ref[2] ^ flip) * half, half)
        out[...] = dot(features_ref[...], weight_ref[:, pl.ds(at, half)]).astype(BF16)


def send_kernel(z, me_ref, message_ref, own_ref, other_ref, pick_ref, *outs):
    devices, height, width = message_ref.shape
    message = message_ref[...].reshape(devices * height, width)
    shape = (z.rows, devices * height)
    asker = (iota(shape, 0) >> log2(z.pair)) ^ (me_ref[0] * z.dom)
    spread = one_hot(iota(shape, 1) == asker * height)
    high = dot(spread, (message >> 4).astype(F32).astype(BF16))
    low = dot(spread, (message & 15).astype(F32).astype(BF16))
    mine = iota((z.rows, width), 1) == (iota((z.rows, width), 0) & (z.pair - 1))
    wanted = jnp.sum(jnp.where(mine, high * 16.0 + low, 0.0), axis=1, keepdims=True).astype(I32)
    pick_ref[...] = one_hot(iota((z.rows, z.rows), 1) == wanted)
    for flip, product in enumerate((own_ref, other_ref)):
        got = dot(pick_ref[...], product[...]).astype(BF16)
        for s in range(z.grp):
            outs[s][flip] = got[s * z.per_grp:(s + 1) * z.per_grp, :]


def rows_kernel(z, pick_ref, features_ref, *outs):
    for s, out in enumerate(outs):
        pick = pick_ref[s * z.per_grp:(s + 1) * z.per_grp, :]
        out[...] = dot(pick, features_ref[...]).astype(BF16)


def pack_kernel(z, *refs):
    ins, outs = refs[:z.grp], refs[z.grp:]
    for rel, out in enumerate(outs):
        for s in range(z.grp):
            out[s * z.per_grp:(s + 1) * z.per_grp, :] = ins[s][rel]


def prepare_kernel(z, me_ref, cols_ref, message_ref, vals_ref, *refs):
    outs, (total, dense) = refs[:z.zz], refs[z.zz:]
    tiles, blocks, tile, _ = vals_ref.shape

    @pl.loop(0, tiles)
    def _(t):
        total[...] = jnp.zeros_like(total)
        for k in range(blocks):
            at = pl.multiple_of(cols_ref[t, k] * tile, tile)
            total[pl.ds(at, tile), :] += vals_ref[t, k].T.astype(F32)
        left = pl.multiple_of(t * tile, tile)
        dense[:, pl.ds(left, tile)] = total[pl.ds(0, z.dom * z.rows), :].astype(BF16)

    @pl.loop(0, z.dom)
    def _(n):
        message = message_ref[me_ref[0] * z.dom + n]
        slot = jnp.concatenate([message[1 + i:2 + i, :] for i in range(z.rows // 128)], axis=1)
        rank, at = slot & (z.pair - 1), slot >> log2(z.pair)
        s, at = at & (z.grp - 1), at >> log2(z.grp)
        k, rel = (me_ref[1] - (at >> 1)) & (z.zz - 1), (at & 1) ^ me_ref[2]
        slot = ((k * 2 + rel) * z.grp + s) * z.pair + rank
        place = one_hot(iota((z.rows, z.rows), 0) == slot)
        at = pl.multiple_of(n * z.rows, z.rows)
        part = dot(place, dense[pl.ds(at, z.rows), :]).astype(BF16)
        for k in range(z.zz):
            for p in range(2 * z.grp):
                first = (k * 2 * z.grp + p) * z.pair
                rows = part[first:first + z.pair, :]
                if z.pair % 16 == 0:
                    to = pl.multiple_of(p * z.per_grp + n * z.pair, z.pair)
                    outs[k][pl.ds(to, z.pair), :] = rows
                else:
                    outs[k][p, n] = rows


def turn_kernel(*refs):
    out, height = refs[-1], refs[0].shape[0]
    for s, part in enumerate(refs[:-1]):
        out[:, s * height:(s + 1) * height] = part[...].T


def forward_kernel(z, first, last, *refs):
    turned, refs = refs[:2], refs[2:]
    rows, refs = jnp.concatenate([ref[...] for ref in refs[:2]], axis=0), refs[2:]
    agg = [dot_rows(ref[...], rows) for ref in turned]
    if not first:
        agg = [part + ref[...] for part, ref in zip(agg, refs)]
        refs = refs[2:]
    if not last:
        for ref, part in zip(refs, agg):
            ref[...] = part
        return
    cots, ahead, hiddens, grads = (refs[2 * i:2 * i + 2] for i in range(4))
    for part, cot, hidden, grad in zip(agg, cots, hiddens, grads):
        sig = jax.nn.sigmoid(part)
        hidden[...] = (part * sig).astype(BF16)
        grad[...] = (cot[...].astype(F32) * (sig * (1.0 + part * (1.0 - sig)))).astype(BF16)
    back_kernel(*ahead, *grads, *refs[-2:])


def back_kernel(turned_a, turned_b, grad_a, grad_b, *outs):
    size = outs[0].shape[0]
    for i, out in enumerate(outs):
        rows = pl.ds(i * size, size)
        value = dot(turned_a[rows, :], grad_a[...]) + dot(turned_b[rows, :], grad_b[...])
        out[...] = value.astype(out.dtype)


def pass_kernel(mine_ref, come_ref, out_ref):
    out_ref[...] = (mine_ref[...] + come_ref[...].astype(F32)).astype(BF16)


def grad_kernel(z, me_ref, left_a, left_b, mine_a, mine_b, come_a, come_b, *refs):
    outs, whole = refs[:-1], refs[-1]
    grads = [
        (mine[...] + come[...].astype(F32)).astype(BF16)
        for mine, come in ((mine_a, come_a), (mine_b, come_b))
    ]
    whole[...] = (dot(left_a[...], grads[0]) + dot(left_b[...], grads[1])).astype(BF16)
    share = whole.shape[0] // z.grp
    for s in range(z.grp):
        at = pl.multiple_of((me_ref[0] ^ s) * share, share)
        outs[s][...] = whole[pl.ds(at, share), :]


def sum_kernel(*refs):
    refs[-1][...] = sum(term[...].astype(F32) for term in refs[:-1]).astype(BF16)


def last_kernel(z, me_ref, *refs):
    pieces, out = refs[:-1], refs[-1]
    share, half = pieces[0].shape
    for rel in range(2):
        left = pl.multiple_of((me_ref[2] ^ rel) * half, half)
        for s in range(z.grp):
            at = pl.multiple_of((me_ref[0] ^ s) * share, share)
            out[pl.ds(at, share), pl.ds(left, half)] = pieces[rel * z.grp + s][...].astype(F32)


def shards(features, node_order, block_cols, block_count, block_vals, weight, cotangent):
    rows, width_in = features.shape
    hidden_units = weight.shape[1]
    half = hidden_units // 2
    tiles, blocks, tile = block_vals.shape[0], block_vals.shape[1], block_vals.shape[-1]
    z = Sizes(rows, tiles)
    at_grp, at_zz, core = lax.axis_index("grp"), lax.axis_index("zz"), lax.axis_index("core")
    me = jnp.stack([at_grp, at_zz, core]).astype(I32)

    def to_core(x):
        return lax.ppermute(x, "core", [(0, 1), (1, 0)])

    def to_grp(x, s):
        return lax.ppermute(x, "grp", [(i, i ^ s) for i in range(z.grp)]) if s else x

    def to_zz(x, k):
        return lax.ppermute(x, "zz", [(i, (i + k) % z.zz) for i in range(z.zz)]) if k else x

    first_half = features[:rows // 2]
    (message,) = call(
        lambda *refs: index_kernel(z, *refs),
        [((z.grp * z.dom, 8, 128), I32)],
        [("s", me), ("v", node_order.reshape(1, rows))],
        "index", 1,
    )
    message, features = lax.optimization_barrier((message, features))
    message = lax.all_to_all(
        message, ("grp", "zz", "core"), split_axis=0, concat_axis=0, tiled=True
    )
    vals_b = to_core(block_vals)

    def across(parts):
        return [to_grp(part, s) for s, part in enumerate(parts)]

    def pack(parts, after=()):
        return call(
            lambda *refs: pack_kernel(z, *refs),
            [((rows, half), BF16)] * 2,
            [("v", part) for part in parts],
            "pack", 0.5, after=after, token=True,
        )

    def rows_of(pick, part, after):
        return call(
            lambda *refs: rows_kernel(z, *refs),
            [((z.per_grp, width_in), BF16)] * z.grp,
            [("v", pick), ("v", part)],
            "rows", 1, after=after, token=True,
        )

    def turned_of(parts):
        left, token = call(
            turn_kernel, [((width_in, rows), BF16)], [("v", part) for part in parts],
            "turn", 0.5, token=True,
        )
        return [left, to_core(left)], token

    products = call(
        lambda *refs: product_kernel(z, *refs),
        [((rows, half), BF16)] * 2,
        [("s", me), ("v", features), ("v", weight)],
        "product", 15,
    )
    pick, *got, token = call(
        lambda *refs: send_kernel(z, *refs),
        [((rows, rows), BF16)] + [((2, z.per_grp, half), BF16)] * z.grp,
        [("s", me), ("v", message)] + [("v", part) for part in products],
        "send", 1.5, token=True,
    )
    token, cotangent, block_cols = lax.optimization_barrier((token, cotangent, block_cols))
    own, other, token = pack(across(got), [token])
    ring = [[own, to_core(other)]]

    live = iota((tiles, blocks), 1) < block_count[:, None]
    cols_a = jnp.where(live, block_cols, z.dom * tiles)
    cols_b = to_core(cols_a)
    cot_a = lax.dynamic_slice_in_dim(cotangent, core * half, half, axis=1)
    cot_b = to_core(lax.dynamic_slice_in_dim(cotangent, (1 - core) * half, half, axis=1))

    wide = 2 * z.grp * z.per_grp
    inner = (wide, rows) if z.pair % 16 == 0 else (2 * z.grp, z.dom, z.pair, rows)

    def prepared(cols, vals, token):
        *got, token = call(
            lambda *refs: prepare_kernel(z, *refs),
            [(inner, BF16)] * z.zz,
            [("s", me), ("s", cols), ("v", message), ("v", vals)],
            "prepare", 7,
            (
                pltpu.VMEM((z.dom * rows + tile, tile), F32),
                pltpu.VMEM((z.dom * rows, rows), BF16),
            ),
            after=[token, cols_b], token=True,
        )
        return [part.reshape(wide, rows) for part in got], token

    for k in range(1, z.zz):
        ring.append([to_zz(part, 1) for part in ring[-1]])
        if k == 1:
            *picked, token = rows_of(pick, features, [token, cot_a, cot_b])
            lefts, token_l = turned_of(across(picked))
            turned_a, token = prepared(cols_a, block_vals, token)
            for part in range(2):
                ring[1][part], token = lax.optimization_barrier((ring[1][part], token))
        if k == 2:
            turned_b, token = prepared(cols_b, vals_b, token)
            ring[2][1], token = lax.optimization_barrier((ring[2][1], token))
    turned = (turned_a, turned_b)

    agg = []
    for k in range(z.zz):
        last = k == z.zz - 1
        ins = [("v", part) for part in (turned[0][k], turned[1][k], *ring[k], *agg)]
        outs = [((rows, half), F32)] * 2
        if last:
            ahead = (turned[0][k], turned[1][k])
            ins += [("v", part) for part in (cot_a, cot_b, *ahead)]
            outs = [((rows, half), BF16)] * 6
        agg = call(
            lambda *refs, k=k, last=last: forward_kernel(z, k == 0, last, *refs),
            outs, ins, "forward", 3 if last else 1,
            after=[token_l] if k == z.zz - 2 else [token] if k == 0 else (),
        )
    hidden_a, hidden_b, grad_a, grad_b, *came = agg

    def back(k):
        return call(
            back_kernel,
            [((rows, half), F32)] * 2,
            [("v", part) for part in (turned[0][k], turned[1][k], grad_a, grad_b)],
            "back", 1,
        )

    come = to_core(hidden_b)
    for k in range(z.zz - 2, -1, -1):
        came = [to_zz(part, -1) for part in came]
        mine = back(k)
        if k:
            passed = [
                call(
                    pass_kernel, [((rows, half), BF16)], [("v", part), ("v", moved)], "pass", 0.5,
                    after=[come] if i == 1 and k == 1 else (), token=True,
                )
                for i, (part, moved) in enumerate(zip(mine, came))
            ]
            came = [part for part, _ in passed]
    first = core == 0
    hidden = jnp.concatenate(
        [jnp.where(first, hidden_a, come), jnp.where(first, come, hidden_a)], axis=1
    )

    share = width_in // z.grp
    terms = call(
        lambda *refs: grad_kernel(z, *refs),
        [((share, half), BF16)] * z.grp,
        [("s", me)] + [("v", part) for part in (*lefts, *mine, *came)],
        "grad", 1.5,
        (pltpu.VMEM((width_in, half), BF16),),
    )

    def total_of(parts):
        return call(
            sum_kernel, [((share, half), BF16)], [("v", part) for part in parts], "sum", 0.5
        )[0]

    mine = total_of([to_grp(terms[s], s) for s in range(z.grp)])
    step = 1
    while step < z.zz:
        mine = total_of(
            [mine, lax.ppermute(mine, "zz", [(i, i ^ step) for i in range(z.zz)])]
        )
        step *= 2
    mine = [to_grp(mine, s) for s in range(z.grp)]
    (grad_weight,) = call(
        lambda *refs: last_kernel(z, *refs),
        [((width_in, hidden_units), F32)],
        [("s", me)] + [("v", part) for part in mine + [to_core(part) for part in mine]],
        "last", 2,
    )
    return hidden, grad_weight


def solution(mesh):
    n_grp, n_dom = mesh.shape["grp"], mesh.shape["dom"]
    split = Mesh(mesh.devices.reshape(n_grp, n_dom // 2, 2), ("grp", "zz", "core"))
    by_rows = ("grp", "zz", "core")
    placed = (
        P(by_rows, None),
        P(by_rows),
        P(by_rows, None),
        P(by_rows),
        P(by_rows, None, None, None),
        P(),
        P(by_rows, None),
    )
    return jax.shard_map(
        shards,
        mesh=split,
        in_specs=placed,
        out_specs=(P(by_rows, None), P()),
        check_vma=False,
    )
```

```python
import jax
import jax.numpy as jnp
from jax import lax
from jax.experimental import pallas as pl
from jax.experimental.pallas import tpu as pltpu
from jax.sharding import Mesh, PartitionSpec as P

BF16 = jnp.bfloat16
F32 = jnp.float32
I32 = jnp.int32


def log2(n):
    assert n & (n - 1) == 0
    return n.bit_length() - 1


def iota(shape, dim):
    return lax.broadcasted_iota(I32, shape, dim)


def one_hot(mask):
    return jnp.where(mask, 1.0, 0.0).astype(BF16)


def dot(a, b):
    return jnp.dot(a, b, preferred_element_type=F32)


def dot_rows(a, b):
    return lax.dot_general(a, b, (((0,), (0,)), ((), ())), preferred_element_type=F32)


def call(body, outs, ins, name, us, scratch=(), after=(), token=False, where=pltpu.VMEM):
    smem = pl.BlockSpec(memory_space=pltpu.SMEM)
    vmem = pl.BlockSpec(memory_space=pltpu.VMEM)
    count = len(ins)
    ties = len(after)
    if token:
        outs = [*outs, ((8, 128), F32)]

    def kernel(*refs):
        refs = refs[:count] + refs[count + ties:]
        if token:
            at = count + len(outs) - 1
            refs[at][...] = jnp.zeros((8, 128), F32)
            refs = refs[:at] + refs[at + 1:]
        body(*refs)

    arrays = [jax.ShapeDtypeStruct(s, d) for s, d in outs] + [value for _, value in ins]
    size = sum(a.size * a.dtype.itemsize for a in arrays + [m.get_array_aval() for m in scratch if m.memory_space == pltpu.VMEM])
    return pl.pallas_call(
        kernel,
        out_shape=tuple(jax.ShapeDtypeStruct(s, d) for s, d in outs),
        in_specs=[smem if kind == "s" else vmem for kind, _ in ins]
        + [vmem] * ties,
        out_specs=tuple(pl.BlockSpec(memory_space=where) for _ in outs),
        scratch_shapes=list(scratch),
        compiler_params=pltpu.CompilerParams(vmem_limit_bytes=size + (5 << 20)),
        cost_estimate=pl.CostEstimate(flops=int(us * 1e8), bytes_accessed=0, transcendentals=0),
        name=name,
    )(*(value for _, value in ins), *after)


class Sizes:
    def __init__(self, rows, tiles):
        self.grp, self.zz = lax.axis_size("grp"), lax.axis_size("zz")
        self.dom = 2 * self.zz
        self.rows, self.tiles = rows, tiles
        self.pair = rows // (self.grp * self.dom)
        self.piece = self.grp * self.pair
        self.per_grp = self.dom * self.pair
        assert rows // 128 < 5 and self.pair <= 128


def column(row):
    n = row.shape[1]
    on = iota((n, n), 0) == iota((n, n), 1)
    return jnp.sum(jnp.where(on, row.astype(F32), 0.0), axis=1, keepdims=True).astype(I32)


def index_kernel(z, me_ref, order_ref, out_ref):
    rows = z.rows
    shift = log2(rows)
    order_r = order_ref[...]
    order_c = column(order_r)
    down, across = iota((rows, rows), 0), iota((rows, rows), 1)
    source_r, source_c = order_r >> shift, order_c >> shift
    row_c = order_c & (rows - 1)
    same = jnp.where(source_c == source_r, 1.0, 0.0)
    rank_c = jnp.sum(jnp.where(across < down, same, 0.0), axis=1, keepdims=True).astype(I32)
    rank_r = jnp.sum(jnp.where(down < across, same, 0.0), axis=0, keepdims=True).astype(I32)
    owner = one_hot(iota((z.grp * z.dom, rows), 0) == source_r)
    at_rank = iota((rows, z.pair), 1) == rank_c
    high = jnp.where(at_rank, (row_c >> 4).astype(F32), 0.0).astype(BF16)
    low = jnp.where(at_rank, (row_c & 15).astype(F32), 0.0).astype(BF16)
    want = (dot(owner, high) * 16.0 + dot(owner, low)).astype(I32)
    out_ref[...] = jnp.zeros_like(out_ref)
    for d in range(z.grp * z.dom):
        out_ref[d, 0:1, 0:z.pair] = want[d:d + 1, :]
    across_grp = (source_r >> log2(z.dom)) ^ me_ref[0]
    inner = source_r & (z.dom - 1)
    slot = (inner * z.grp + across_grp) * z.pair + rank_r
    for i in range(rows // 128):
        lanes = slot[:, i * 128:(i + 1) * 128]
        out_ref[:, 1 + i:2 + i, :] = jnp.broadcast_to(lanes[None], (z.grp * z.dom, 1, 128))


def product_kernel(z, me_ref, features_ref, weight_ref, *outs):
    half = outs[0].shape[1]
    for flip, out in enumerate(outs):
        at = pl.multiple_of((me_ref[2] ^ flip) * half, half)
        out[...] = dot(features_ref[...], weight_ref[:, pl.ds(at, half)]).astype(BF16)


def send_kernel(z, me_ref, message_ref, own_ref, other_ref, pick_ref, *outs):
    devices, height, width = message_ref.shape
    message = message_ref[...].reshape(devices * height, width)
    shape = (z.rows, devices * height)
    asker = (iota(shape, 0) >> log2(z.pair)) ^ (me_ref[0] * z.dom)
    spread = one_hot(iota(shape, 1) == asker * height)
    high = dot(spread, (message >> 4).astype(F32).astype(BF16))
    low = dot(spread, (message & 15).astype(F32).astype(BF16))
    mine = iota((z.rows, width), 1) == (iota((z.rows, width), 0) & (z.pair - 1))
    wanted = jnp.sum(jnp.where(mine, high * 16.0 + low, 0.0), axis=1, keepdims=True).astype(I32)
    pick_ref[...] = one_hot(iota((z.rows, z.rows), 1) == wanted)
    for flip, product in enumerate((own_ref, other_ref)):
        got = dot(pick_ref[...], product[...]).astype(BF16)
        for s in range(z.grp):
            outs[s][flip] = got[s * z.per_grp:(s + 1) * z.per_grp, :]


def rows_kernel(z, pick_ref, features_ref, *outs):
    for s, out in enumerate(outs):
        pick = pick_ref[s * z.per_grp:(s + 1) * z.per_grp, :]
        out[...] = dot(pick, features_ref[...]).astype(BF16)


def pack_kernel(z, *refs):
    ins, outs = refs[:z.grp], refs[z.grp:]
    for rel, out in enumerate(outs):
        for s in range(z.grp):
            out[s * z.per_grp:(s + 1) * z.per_grp, :] = ins[s][rel]


def prepare_kernel(z, me_ref, cols_ref, message_ref, vals_ref, *refs):
    outs, (total, dense) = refs[:z.zz], refs[z.zz:]
    tiles, blocks, tile, _ = vals_ref.shape

    @pl.loop(0, tiles)
    def _(t):
        total[...] = jnp.zeros_like(total)
        for k in range(blocks):
            at = pl.multiple_of(cols_ref[t, k] * tile, tile)
            total[pl.ds(at, tile), :] += vals_ref[t, k].T.astype(F32)
        left = pl.multiple_of(t * tile, tile)
        dense[:, pl.ds(left, tile)] = total[pl.ds(0, z.dom * z.rows), :].astype(BF16)

    @pl.loop(0, z.dom)
    def _(n):
        message = message_ref[me_ref[0] * z.dom + n]
        slot = jnp.concatenate([message[1 + i:2 + i, :] for i in range(z.rows // 128)], axis=1)
        rank, at = slot & (z.pair - 1), slot >> log2(z.pair)
        s, at = at & (z.grp - 1), at >> log2(z.grp)
        k, rel = (me_ref[1] - (at >> 1)) & (z.zz - 1), (at & 1) ^ me_ref[2]
        slot = ((k * 2 + rel) * z.grp + s) * z.pair + rank
        place = one_hot(iota((z.rows, z.rows), 0) == slot)
        at = pl.multiple_of(n * z.rows, z.rows)
        part = dot(place, dense[pl.ds(at, z.rows), :]).astype(BF16)
        for k in range(z.zz):
            for p in range(2 * z.grp):
                first = (k * 2 * z.grp + p) * z.pair
                rows = part[first:first + z.pair, :]
                if z.pair % 16 == 0:
                    to = pl.multiple_of(p * z.per_grp + n * z.pair, z.pair)
                    outs[k][pl.ds(to, z.pair), :] = rows
                else:
                    outs[k][p, n] = rows


def turn_kernel(*refs):
    out, height = refs[-1], refs[0].shape[0]
    for s, part in enumerate(refs[:-1]):
        out[:, s * height:(s + 1) * height] = part[...].T


def forward_kernel(z, first, last, *refs):
    turned, refs = refs[:2], refs[2:]
    rows, refs = jnp.concatenate([ref[...] for ref in refs[:2]], axis=0), refs[2:]
    agg = [dot_rows(ref[...], rows) for ref in turned]
    if not first:
        agg = [part + ref[...] for part, ref in zip(agg, refs)]
        refs = refs[2:]
    if not last:
        for ref, part in zip(refs, agg):
            ref[...] = part
        return
    cots, ahead, hiddens, grads = (refs[2 * i:2 * i + 2] for i in range(4))
    for part, cot, hidden, grad in zip(agg, cots, hiddens, grads):
        sig = jax.nn.sigmoid(part)
        hidden[...] = (part * sig).astype(BF16)
        grad[...] = (cot[...].astype(F32) * (sig * (1.0 + part * (1.0 - sig)))).astype(BF16)
    back_kernel(*ahead, *grads, *refs[-2:])


def back_kernel(turned_a, turned_b, grad_a, grad_b, *outs):
    size = outs[0].shape[1]
    for i, out in enumerate(outs):
        cols = pl.ds(i * size, size)
        value = dot(turned_a[...], grad_a[:, cols]) + dot(turned_b[...], grad_b[:, cols])
        out[...] = value.astype(out.dtype)


def pass_kernel(mine_ref, come_ref, out_ref):
    out_ref[...] = (mine_ref[...] + come_ref[...].astype(F32)).astype(BF16)


def grad_kernel(z, me_ref, left_a, left_b, mine_ref, come_ref, *refs):
    outs, whole = refs[:-1], refs[-1]
    grad = (mine_ref[...] + come_ref[...].astype(F32)).astype(BF16)
    total = dot(left_a[...], grad[:z.rows]) + dot(left_b[...], grad[z.rows:])
    whole[...] = total.astype(BF16)
    share = whole.shape[0] // z.grp
    for s in range(z.grp):
        at = pl.multiple_of((me_ref[0] ^ s) * share, share)
        outs[s][...] = whole[pl.ds(at, share), :]


def merge_kernel(*refs):
    terms, out = refs[:-1], refs[-1]
    count, width = len(terms) // 2, terms[0].shape[1]
    for i in range(2):
        value = sum(term[...].astype(F32) for term in terms[i * count:(i + 1) * count])
        out[:, i * width:(i + 1) * width] = value.astype(BF16)


def sum_kernel(*refs):
    refs[-1][...] = sum(term[...].astype(F32) for term in refs[:-1]).astype(BF16)


def last_kernel(z, me_ref, *refs):
    pieces, (out, whole, sems) = refs[:-3], refs[-3:]
    share, half = pieces[0].shape
    copies = []
    for s in range(z.grp):
        rows = pl.ds(s * share, share)
        for rel in range(2):
            left = pl.multiple_of((me_ref[2] ^ rel) * half, half)
            whole[rows, pl.ds(left, half)] = pieces[rel * z.grp + s][...].astype(F32)
        at = pl.multiple_of((me_ref[0] ^ s) * share, share)
        copies.append(
            pltpu.make_async_copy(whole.at[rows], out.at[pl.ds(at, share)], sems.at[s])
        )
        copies[-1].start()
    for copy in copies:
        copy.wait()


def shards(features, node_order, block_cols, block_count, block_vals, weight, cotangent):
    rows, width_in = features.shape
    hidden_units = weight.shape[1]
    half = hidden_units // 2
    tiles, blocks, tile = block_vals.shape[0], block_vals.shape[1], block_vals.shape[-1]
    z = Sizes(rows, tiles)
    at_grp, at_zz, core = lax.axis_index("grp"), lax.axis_index("zz"), lax.axis_index("core")
    me = jnp.stack([at_grp, at_zz, core]).astype(I32)

    def to_core(x):
        return lax.ppermute(x, "core", [(0, 1), (1, 0)])

    def to_grp(x, s):
        return lax.ppermute(x, "grp", [(i, i ^ s) for i in range(z.grp)]) if s else x

    def to_zz(x, k):
        return lax.ppermute(x, "zz", [(i, (i + k) % z.zz) for i in range(z.zz)]) if k else x

    first_half = features[:rows // 2]
    (message,) = call(
        lambda *refs: index_kernel(z, *refs),
        [((z.grp * z.dom, 8, 128), I32)],
        [("s", me), ("v", node_order.reshape(1, rows))],
        "index", 1,
    )
    message, features = lax.optimization_barrier((message, features))
    message = lax.all_to_all(
        message, ("grp", "zz", "core"), split_axis=0, concat_axis=0, tiled=True
    )
    vals_b = to_core(block_vals)

    def across(parts):
        return [to_grp(part, s) for s, part in enumerate(parts)]

    def pack(parts, after=()):
        return call(
            lambda *refs: pack_kernel(z, *refs),
            [((rows, half), BF16)] * 2,
            [("v", part) for part in parts],
            "pack", 0.5, after=after, token=True,
        )

    def rows_of(pick, part, after):
        return call(
            lambda *refs: rows_kernel(z, *refs),
            [((z.per_grp, width_in), BF16)] * z.grp,
            [("v", pick), ("v", part)],
            "rows", 1, after=after, token=True,
        )

    def turned_of(parts):
        left, token = call(
            turn_kernel, [((width_in, rows), BF16)], [("v", part) for part in parts],
            "turn", 0.5, token=True,
        )
        return [left, to_core(left)], token

    products = call(
        lambda *refs: product_kernel(z, *refs),
        [((rows, half), BF16)] * 2,
        [("s", me), ("v", features), ("v", weight)],
        "product", 15,
    )
    pick, *got, token = call(
        lambda *refs: send_kernel(z, *refs),
        [((rows, rows), BF16)] + [((2, z.per_grp, half), BF16)] * z.grp,
        [("s", me), ("v", message)] + [("v", part) for part in products],
        "send", 1.5, token=True,
    )
    token, cotangent, block_cols = lax.optimization_barrier((token, cotangent, block_cols))
    live = iota((tiles, blocks), 1) < block_count[:, None]
    cols_a = jnp.where(live, block_cols, z.dom * tiles)
    cols_b = to_core(cols_a)
    cot_a = lax.dynamic_slice_in_dim(cotangent, core * half, half, axis=1)
    cot_b = to_core(lax.dynamic_slice_in_dim(cotangent, (1 - core) * half, half, axis=1))

    came = across(got)
    *picked, token_r = rows_of(pick, features, [token, cot_a, cot_b])
    own, other, token = pack(came, [token_r])
    ring = [[own, to_core(other)]]
    lefts, token_l = turned_of(across(picked))

    wide = 2 * z.grp * z.per_grp
    inner = (wide, rows) if z.pair % 16 == 0 else (2 * z.grp, z.dom, z.pair, rows)

    def prepared(cols, vals, token, after=()):
        *got, token = call(
            lambda *refs: prepare_kernel(z, *refs),
            [(inner, BF16)] * z.zz,
            [("s", me), ("s", cols), ("v", message), ("v", vals)],
            "prepare", 7,
            (
                pltpu.VMEM((z.dom * rows + tile, tile), F32),
                pltpu.VMEM((z.dom * rows, rows), BF16),
            ),
            after=[token, cols_b, *after], token=True,
        )
        return [part.reshape(wide, rows) for part in got], token

    for k in range(1, z.zz):
        ring.append([to_zz(part, 1) for part in ring[-1]])
        if k == 1:
            turned_a, token = prepared(cols_a, block_vals, token, [vals_b])
            for part in range(2):
                ring[1][part], token = lax.optimization_barrier((ring[1][part], token))
        if k == 2:
            turned_b, token = prepared(cols_b, vals_b, token, [token_l])
            for part in range(2):
                ring[2][part], token = lax.optimization_barrier((ring[2][part], token))
    turned = (turned_a, turned_b)

    agg = []
    for k in range(z.zz):
        last = k == z.zz - 1
        ins = [("v", part) for part in (turned[0][k], turned[1][k], *ring[k], *agg)]
        outs = [((rows, half), F32)] * 2
        if last:
            ahead = (turned[0][k], turned[1][k])
            ins += [("v", part) for part in (cot_a, cot_b, *ahead)]
            outs = [((rows, half), BF16)] * 4 + [((wide, half // 2), BF16)] * 2
        agg = call(
            lambda *refs, k=k, last=last: forward_kernel(z, k == 0, last, *refs),
            outs, ins, "forward", 3 if last else 1,
            after=[token] if k == 0 else (),
        )
    hidden_a, hidden_b, grad_a, grad_b, *came = agg

    def back(k):
        return call(
            back_kernel,
            [((wide, half // 2), F32)] * 2,
            [("v", part) for part in (turned[0][k], turned[1][k], grad_a, grad_b)],
            "back", 1,
        )

    come = to_core(hidden_b)
    for k in range(z.zz - 2, -1, -1):
        came = [to_zz(part, -1) for part in came]
        mine = back(k)
        if k:
            passed = [
                call(
                    pass_kernel, [((wide, half // 2), BF16)], [("v", part), ("v", moved)],
                    "pass", 0.5,
                    after=[come] if i == 1 and k == 1 else (), token=True,
                )
                for i, (part, moved) in enumerate(zip(mine, came))
            ]
            came = [part for part, _ in passed]
    first = core == 0
    hidden = jnp.concatenate(
        [jnp.where(first, hidden_a, come), jnp.where(first, come, hidden_a)], axis=1
    )

    share = width_in // z.grp
    terms = []
    for part, moved in zip(mine, came):
        got = call(
            lambda *refs: grad_kernel(z, *refs),
            [((share, half // 2), BF16)] * z.grp,
            [("s", me)] + [("v", value) for value in (*lefts, part, moved)],
            "grad", 1.5,
            (pltpu.VMEM((width_in, half // 2), BF16),),
        )
        terms += across(got)

    def total_of(parts):
        return call(
            sum_kernel, [((share, half), BF16)], [("v", part) for part in parts], "sum", 0.5
        )[0]

    (mine,) = call(
        merge_kernel, [((share, half), BF16)], [("v", term) for term in terms], "merge", 0.5
    )
    step = 1
    while step < z.zz:
        mine = total_of(
            [mine, lax.ppermute(mine, "zz", [(i, i ^ step) for i in range(z.zz)])]
        )
        step *= 2
    mine = [to_grp(mine, s) for s in range(z.grp)]
    (grad_weight,) = call(
        lambda *refs: last_kernel(z, *refs),
        [((width_in, hidden_units), F32)],
        [("s", me)] + [("v", part) for part in mine + [to_core(part) for part in mine]],
        "last", 2,
        (pltpu.VMEM((width_in, hidden_units), F32), pltpu.SemaphoreType.DMA((z.grp,))),
        where=pl.ANY,
    )
    return hidden, grad_weight


def solution(mesh):
    n_grp, n_dom = mesh.shape["grp"], mesh.shape["dom"]
    split = Mesh(mesh.devices.reshape(n_grp, n_dom // 2, 2), ("grp", "zz", "core"))
    by_rows = ("grp", "zz", "core")
    placed = (
        P(by_rows, None),
        P(by_rows),
        P(by_rows, None),
        P(by_rows),
        P(by_rows, None, None, None),
        P(),
        P(by_rows, None),
    )
    return jax.shard_map(
        shards,
        mesh=split,
        in_specs=placed,
        out_specs=(P(by_rows, None), P()),
        check_vma=False,
    )
```

```python
import jax
import jax.numpy as jnp
from jax import lax
from jax.experimental import pallas as pl
from jax.experimental.pallas import tpu as pltpu
from jax.sharding import Mesh, PartitionSpec as P

BF16 = jnp.bfloat16
F32 = jnp.float32
I32 = jnp.int32


def log2(n):
    assert n & (n - 1) == 0
    return n.bit_length() - 1


def place_of(at, count):
    place = at
    for shift in range(1, log2(count)):
        place = place ^ (at >> shift)
    return place


def iota(shape, dim):
    return lax.broadcasted_iota(I32, shape, dim)


def one_hot(mask):
    return jnp.where(mask, 1.0, 0.0).astype(BF16)


def dot(a, b):
    return jnp.dot(a, b, preferred_element_type=F32)


def dot_rows(a, b):
    return lax.dot_general(a, b, (((0,), (0,)), ((), ())), preferred_element_type=F32)


def call(body, outs, ins, name, us, scratch=(), after=(), token=False):
    smem = pl.BlockSpec(memory_space=pltpu.SMEM)
    vmem = pl.BlockSpec(memory_space=pltpu.VMEM)
    count = len(ins)
    ties = len(after)
    if token:
        outs = [*outs, ((8, 128), F32)]

    def kernel(*refs):
        refs = refs[:count] + refs[count + ties:]
        if token:
            at = count + len(outs) - 1
            refs[at][...] = jnp.zeros((8, 128), F32)
            refs = refs[:at] + refs[at + 1:]
        body(*refs)

    arrays = [jax.ShapeDtypeStruct(s, d) for s, d in outs] + [value for _, value in ins]
    size = sum(a.size * a.dtype.itemsize for a in arrays + [m.get_array_aval() for m in scratch])
    return pl.pallas_call(
        kernel,
        out_shape=tuple(jax.ShapeDtypeStruct(s, d) for s, d in outs),
        in_specs=[smem if where == "s" else vmem for where, _ in ins]
        + [vmem] * ties,
        out_specs=tuple(vmem for _ in outs),
        scratch_shapes=list(scratch),
        compiler_params=pltpu.CompilerParams(vmem_limit_bytes=size + (5 << 20)),
        cost_estimate=pl.CostEstimate(flops=int(us * 1e8), bytes_accessed=0, transcendentals=0),
        name=name,
    )(*(value for _, value in ins), *after)


class Sizes:
    def __init__(self, rows, tiles):
        self.grp, self.zz = lax.axis_size("grp"), lax.axis_size("zz")
        self.dom = 2 * self.zz
        self.rows, self.tiles = rows, tiles
        self.pair = rows // (self.grp * self.dom)
        self.piece = self.grp * self.pair
        self.per_grp = self.dom * self.pair
        assert rows // 128 < 5 and self.pair <= 128


def column(row):
    n = row.shape[1]
    on = iota((n, n), 0) == iota((n, n), 1)
    return jnp.sum(jnp.where(on, row.astype(F32), 0.0), axis=1, keepdims=True).astype(I32)


def index_kernel(z, me_ref, order_ref, out_ref):
    rows = z.rows
    shift = log2(rows)
    order_r = order_ref[...]
    order_c = column(order_r)
    down, across = iota((rows, rows), 0), iota((rows, rows), 1)
    source_r, source_c = order_r >> shift, order_c >> shift
    row_c = order_c & (rows - 1)
    same = jnp.where(source_c == source_r, 1.0, 0.0)
    rank_c = jnp.sum(jnp.where(across < down, same, 0.0), axis=1, keepdims=True).astype(I32)
    rank_r = jnp.sum(jnp.where(down < across, same, 0.0), axis=0, keepdims=True).astype(I32)
    owner = one_hot(iota((z.grp * z.dom, rows), 0) == source_r)
    at_rank = iota((rows, z.pair), 1) == rank_c
    high = jnp.where(at_rank, (row_c >> 4).astype(F32), 0.0).astype(BF16)
    low = jnp.where(at_rank, (row_c & 15).astype(F32), 0.0).astype(BF16)
    want = (dot(owner, high) * 16.0 + dot(owner, low)).astype(I32)
    out_ref[...] = jnp.zeros_like(out_ref)
    for d in range(z.grp * z.dom):
        out_ref[d, 0:1, 0:z.pair] = want[d:d + 1, :]
    across_grp = (source_r >> log2(z.dom)) ^ me_ref[0]
    inner = source_r & (z.dom - 1)
    slot = (inner * z.grp + across_grp) * z.pair + rank_r
    for i in range(rows // 128):
        lanes = slot[:, i * 128:(i + 1) * 128]
        out_ref[:, 1 + i:2 + i, :] = jnp.broadcast_to(lanes[None], (z.grp * z.dom, 1, 128))


def product_kernel(z, me_ref, features_ref, weight_ref, *outs):
    half = outs[0].shape[1]
    for flip, out in enumerate(outs):
        at = pl.multiple_of((me_ref[2] ^ flip) * half, half)
        out[...] = dot(features_ref[...], weight_ref[:, pl.ds(at, half)]).astype(BF16)


def send_kernel(z, me_ref, message_ref, own_ref, other_ref, pick_ref, *outs):
    devices, height, width = message_ref.shape
    message = message_ref[...].reshape(devices * height, width)
    shape = (z.rows, devices * height)
    asker = (iota(shape, 0) >> log2(z.pair)) ^ (me_ref[0] * z.dom)
    spread = one_hot(iota(shape, 1) == asker * height)
    high = dot(spread, (message >> 4).astype(F32).astype(BF16))
    low = dot(spread, (message & 15).astype(F32).astype(BF16))
    mine = iota((z.rows, width), 1) == (iota((z.rows, width), 0) & (z.pair - 1))
    wanted = jnp.sum(jnp.where(mine, high * 16.0 + low, 0.0), axis=1, keepdims=True).astype(I32)
    pick_ref[...] = one_hot(iota((z.rows, z.rows), 1) == wanted)
    for flip, product in enumerate((own_ref, other_ref)):
        got = dot(pick_ref[...], product[...]).astype(BF16)
        for s in range(z.grp):
            outs[s][flip] = got[s * z.per_grp:(s + 1) * z.per_grp, :]


def rows_kernel(z, pick_ref, features_ref, *outs):
    for s, out in enumerate(outs):
        pick = pick_ref[s * z.per_grp:(s + 1) * z.per_grp, :]
        out[...] = dot(pick, features_ref[...]).astype(BF16)


def pack_kernel(z, *refs):
    ins, outs = refs[:z.grp], refs[z.grp:]
    for rel, out in enumerate(outs):
        for s in range(z.grp):
            out[s * z.per_grp:(s + 1) * z.per_grp, :] = ins[s][rel]


def prepare_kernel(z, me_ref, cols_ref, message_ref, vals_ref, *refs):
    outs, (total, dense) = refs[:z.zz], refs[z.zz:]
    tiles, blocks, tile, _ = vals_ref.shape

    @pl.loop(0, tiles)
    def _(t):
        total[...] = jnp.zeros_like(total)
        for k in range(blocks):
            at = pl.multiple_of(cols_ref[t, k] * tile, tile)
            total[pl.ds(at, tile), :] += vals_ref[t, k].T.astype(F32)
        left = pl.multiple_of(t * tile, tile)
        dense[:, pl.ds(left, tile)] = total[pl.ds(0, z.dom * z.rows), :].astype(BF16)

    @pl.loop(0, z.dom)
    def _(n):
        message = message_ref[me_ref[0] * z.dom + n]
        slot = jnp.concatenate([message[1 + i:2 + i, :] for i in range(z.rows // 128)], axis=1)
        rank, at = slot & (z.pair - 1), slot >> log2(z.pair)
        s, at = at & (z.grp - 1), at >> log2(z.grp)
        k = (place_of(me_ref[1], z.zz) - place_of(at >> 1, z.zz)) & (z.zz - 1)
        rel = (at & 1) ^ me_ref[2]
        slot = ((k * 2 + rel) * z.grp + s) * z.pair + rank
        place = one_hot(iota((z.rows, z.rows), 0) == slot)
        at = pl.multiple_of(n * z.rows, z.rows)
        part = dot(place, dense[pl.ds(at, z.rows), :]).astype(BF16)
        for k in range(z.zz):
            for p in range(2 * z.grp):
                first = (k * 2 * z.grp + p) * z.pair
                rows = part[first:first + z.pair, :]
                if z.pair % 16 == 0:
                    to = pl.multiple_of(p * z.per_grp + n * z.pair, z.pair)
                    outs[k][pl.ds(to, z.pair), :] = rows
                else:
                    outs[k][p, n] = rows


def turn_kernel(*refs):
    out, height = refs[-1], refs[0].shape[0]
    for s, part in enumerate(refs[:-1]):
        out[:, s * height:(s + 1) * height] = part[...].T


def forward_kernel(z, first, last, *refs):
    turned, refs = refs[:2], refs[2:]
    rows, refs = jnp.concatenate([ref[...] for ref in refs[:2]], axis=0), refs[2:]
    agg = [dot_rows(ref[...], rows) for ref in turned]
    if not first:
        agg = [part + ref[...] for part, ref in zip(agg, refs)]
        refs = refs[2:]
    if not last:
        for ref, part in zip(refs, agg):
            ref[...] = part
        return
    cots, ahead, hiddens, grads = (refs[2 * i:2 * i + 2] for i in range(4))
    for part, cot, hidden, grad in zip(agg, cots, hiddens, grads):
        sig = jax.nn.sigmoid(part)
        hidden[...] = (part * sig).astype(BF16)
        grad[...] = (cot[...].astype(F32) * (sig * (1.0 + part * (1.0 - sig)))).astype(BF16)
    back_kernel(*ahead, *grads, *refs[-2:])


def back_kernel(turned_a, turned_b, grad_a, grad_b, *outs):
    size = outs[0].shape[0]
    for i, out in enumerate(outs):
        rows = pl.ds(i * size, size)
        value = dot(turned_a[rows, :], grad_a[...]) + dot(turned_b[rows, :], grad_b[...])
        out[...] = value.astype(out.dtype)


def pass_kernel(mine_ref, come_ref, out_ref):
    out_ref[...] = (mine_ref[...] + come_ref[...].astype(F32)).astype(BF16)


def grad_kernel(z, me_ref, left_a, left_b, mine_a, mine_b, come_a, come_b, *refs):
    outs, whole = refs[:-1], refs[-1]
    grads = [
        (mine[...] + come[...].astype(F32)).astype(BF16)
        for mine, come in ((mine_a, come_a), (mine_b, come_b))
    ]
    whole[...] = (dot(left_a[...], grads[0]) + dot(left_b[...], grads[1])).astype(BF16)
    share = whole.shape[0] // z.grp
    for s in range(z.grp):
        at = pl.multiple_of((me_ref[0] ^ s) * share, share)
        outs[s][...] = whole[pl.ds(at, share), :]


def sum_kernel(*refs):
    refs[-1][...] = sum(term[...].astype(F32) for term in refs[:-1]).astype(BF16)


def last_kernel(z, me_ref, *refs):
    pieces, out = refs[:-1], refs[-1]
    share, half = pieces[0].shape
    for rel in range(2):
        left = pl.multiple_of((me_ref[2] ^ rel) * half, half)
        for s in range(z.grp):
            at = pl.multiple_of((me_ref[0] ^ s) * share, share)
            out[pl.ds(at, share), pl.ds(left, half)] = pieces[rel * z.grp + s][...].astype(F32)


def shards(features, node_order, block_cols, block_count, block_vals, weight, cotangent):
    rows, width_in = features.shape
    hidden_units = weight.shape[1]
    half = hidden_units // 2
    tiles, blocks, tile = block_vals.shape[0], block_vals.shape[1], block_vals.shape[-1]
    z = Sizes(rows, tiles)
    at_grp, at_zz, core = lax.axis_index("grp"), lax.axis_index("zz"), lax.axis_index("core")
    me = jnp.stack([at_grp, at_zz, core]).astype(I32)

    def to_core(x):
        return lax.ppermute(x, "core", [(0, 1), (1, 0)])

    def to_grp(x, s):
        return lax.ppermute(x, "grp", [(i, i ^ s) for i in range(z.grp)]) if s else x

    def to_zz(x, k):
        order = [i ^ (i >> 1) for i in range(z.zz)]
        return lax.ppermute(x, "zz", [(order[i], order[(i + k) % z.zz]) for i in range(z.zz)])

    first_half = features[:rows // 2]
    (message,) = call(
        lambda *refs: index_kernel(z, *refs),
        [((z.grp * z.dom, 8, 128), I32)],
        [("s", me), ("v", node_order.reshape(1, rows))],
        "index", 1,
    )
    message, features = lax.optimization_barrier((message, features))
    message = lax.all_to_all(
        message, ("grp", "zz", "core"), split_axis=0, concat_axis=0, tiled=True
    )
    vals_b = to_core(block_vals)

    def across(parts):
        return [to_grp(part, s) for s, part in enumerate(parts)]

    def pack(parts, after=()):
        return call(
            lambda *refs: pack_kernel(z, *refs),
            [((rows, half), BF16)] * 2,
            [("v", part) for part in parts],
            "pack", 0.5, after=after, token=True,
        )

    def rows_of(pick, part, after):
        return call(
            lambda *refs: rows_kernel(z, *refs),
            [((z.per_grp, width_in), BF16)] * z.grp,
            [("v", pick), ("v", part)],
            "rows", 1, after=after, token=True,
        )

    def turned_of(parts):
        left, token = call(
            turn_kernel, [((width_in, rows), BF16)], [("v", part) for part in parts],
            "turn", 0.5, token=True,
        )
        return [left, to_core(left)], token

    products = call(
        lambda *refs: product_kernel(z, *refs),
        [((rows, half), BF16)] * 2,
        [("s", me), ("v", features), ("v", weight)],
        "product", 15,
    )
    pick, *got, token = call(
        lambda *refs: send_kernel(z, *refs),
        [((rows, rows), BF16)] + [((2, z.per_grp, half), BF16)] * z.grp,
        [("s", me), ("v", message)] + [("v", part) for part in products],
        "send", 1.5, token=True,
    )
    token, cotangent, block_cols = lax.optimization_barrier((token, cotangent, block_cols))
    own, other, token = pack(across(got), [token])
    ring = [[own, to_core(other)]]

    live = iota((tiles, blocks), 1) < block_count[:, None]
    cols_a = jnp.where(live, block_cols, z.dom * tiles)
    cols_b = to_core(cols_a)
    cot_a = lax.dynamic_slice_in_dim(cotangent, core * half, half, axis=1)
    cot_b = to_core(lax.dynamic_slice_in_dim(cotangent, (1 - core) * half, half, axis=1))

    wide = 2 * z.grp * z.per_grp
    inner = (wide, rows) if z.pair % 16 == 0 else (2 * z.grp, z.dom, z.pair, rows)

    def prepared(cols, vals, token):
        *got, token = call(
            lambda *refs: prepare_kernel(z, *refs),
            [(inner, BF16)] * z.zz,
            [("s", me), ("s", cols), ("v", message), ("v", vals)],
            "prepare", 7,
            (
                pltpu.VMEM((z.dom * rows + tile, tile), F32),
                pltpu.VMEM((z.dom * rows, rows), BF16),
            ),
            after=[token, cols_b], token=True,
        )
        return [part.reshape(wide, rows) for part in got], token

    for k in range(1, z.zz):
        ring.append([to_zz(part, 1) for part in ring[-1]])
        if k == 1:
            *picked, token = rows_of(pick, features, [token, cot_a, cot_b])
            lefts, token_l = turned_of(across(picked))
            turned_a, token = prepared(cols_a, block_vals, token)
            for part in range(2):
                ring[1][part], token = lax.optimization_barrier((ring[1][part], token))
        if k == 2:
            turned_b, token = prepared(cols_b, vals_b, token)
            ring[2][1], token = lax.optimization_barrier((ring[2][1], token))
    turned = (turned_a, turned_b)

    agg = []
    for k in range(z.zz):
        last = k == z.zz - 1
        ins = [("v", part) for part in (turned[0][k], turned[1][k], *ring[k], *agg)]
        outs = [((rows, half), F32)] * 2
        if last:
            ahead = (turned[0][k], turned[1][k])
            ins += [("v", part) for part in (cot_a, cot_b, *ahead)]
            outs = [((rows, half), BF16)] * 6
        agg = call(
            lambda *refs, k=k, last=last: forward_kernel(z, k == 0, last, *refs),
            outs, ins, "forward", 3 if last else 1,
            after=[token_l] if k == z.zz - 2 else [token] if k == 0 else (),
        )
    hidden_a, hidden_b, grad_a, grad_b, *came = agg

    def back(k):
        return call(
            back_kernel,
            [((rows, half), F32)] * 2,
            [("v", part) for part in (turned[0][k], turned[1][k], grad_a, grad_b)],
            "back", 1,
        )

    come = to_core(hidden_b)
    for k in range(z.zz - 2, -1, -1):
        came = [to_zz(part, -1) for part in came]
        mine = back(k)
        if k:
            passed = [
                call(
                    pass_kernel, [((rows, half), BF16)], [("v", part), ("v", moved)], "pass", 0.5,
                    after=[come] if i == 1 and k == 1 else (), token=True,
                )
                for i, (part, moved) in enumerate(zip(mine, came))
            ]
            came = [part for part, _ in passed]
    first = core == 0
    hidden = jnp.concatenate(
        [jnp.where(first, hidden_a, come), jnp.where(first, come, hidden_a)], axis=1
    )

    share = width_in // z.grp
    terms = call(
        lambda *refs: grad_kernel(z, *refs),
        [((share, half), BF16)] * z.grp,
        [("s", me)] + [("v", part) for part in (*lefts, *mine, *came)],
        "grad", 1.5,
        (pltpu.VMEM((width_in, half), BF16),),
    )

    def total_of(parts):
        return call(
            sum_kernel, [((share, half), BF16)], [("v", part) for part in parts], "sum", 0.5
        )[0]

    mine = total_of([to_grp(terms[s], s) for s in range(z.grp)])
    step = 1
    while step < z.zz:
        mine = total_of(
            [mine, lax.ppermute(mine, "zz", [(i, i ^ step) for i in range(z.zz)])]
        )
        step *= 2
    mine = [to_grp(mine, s) for s in range(z.grp)]
    (grad_weight,) = call(
        lambda *refs: last_kernel(z, *refs),
        [((width_in, hidden_units), F32)],
        [("s", me)] + [("v", part) for part in mine + [to_core(part) for part in mine]],
        "last", 2,
    )
    return hidden, grad_weight


def solution(mesh):
    n_grp, n_dom = mesh.shape["grp"], mesh.shape["dom"]
    split = Mesh(mesh.devices.reshape(n_grp, n_dom // 2, 2), ("grp", "zz", "core"))
    by_rows = ("grp", "zz", "core")
    placed = (
        P(by_rows, None),
        P(by_rows),
        P(by_rows, None),
        P(by_rows),
        P(by_rows, None, None, None),
        P(),
        P(by_rows, None),
    )
    return jax.shard_map(
        shards,
        mesh=split,
        in_specs=placed,
        out_specs=(P(by_rows, None), P()),
        check_vma=False,
    )
```

```python
import jax
import jax.numpy as jnp
from jax import lax
from jax.experimental import pallas as pl
from jax.experimental.pallas import tpu as pltpu
from jax.sharding import Mesh, PartitionSpec as P

BF16 = jnp.bfloat16
F32 = jnp.float32
I32 = jnp.int32


def log2(n):
    assert n & (n - 1) == 0
    return n.bit_length() - 1


def place_of(at, count):
    place = at
    for shift in range(1, log2(count)):
        place = place ^ (at >> shift)
    return place


def iota(shape, dim):
    return lax.broadcasted_iota(I32, shape, dim)


def one_hot(mask):
    return jnp.where(mask, 1.0, 0.0).astype(BF16)


def dot(a, b):
    return jnp.dot(a, b, preferred_element_type=F32)


def dot_rows(a, b):
    return lax.dot_general(a, b, (((0,), (0,)), ((), ())), preferred_element_type=F32)


def call(body, outs, ins, name, us, scratch=(), after=(), token=False):
    smem = pl.BlockSpec(memory_space=pltpu.SMEM)
    vmem = pl.BlockSpec(memory_space=pltpu.VMEM)
    count = len(ins)
    ties = len(after)
    if token:
        outs = [*outs, ((8, 128), F32)]

    def kernel(*refs):
        refs = refs[:count] + refs[count + ties:]
        if token:
            at = count + len(outs) - 1
            refs[at][...] = jnp.zeros((8, 128), F32)
            refs = refs[:at] + refs[at + 1:]
        body(*refs)

    arrays = [jax.ShapeDtypeStruct(s, d) for s, d in outs] + [value for _, value in ins]
    size = sum(a.size * a.dtype.itemsize for a in arrays + [m.get_array_aval() for m in scratch])
    return pl.pallas_call(
        kernel,
        out_shape=tuple(jax.ShapeDtypeStruct(s, d) for s, d in outs),
        in_specs=[smem if where == "s" else vmem for where, _ in ins]
        + [vmem] * ties,
        out_specs=tuple(vmem for _ in outs),
        scratch_shapes=list(scratch),
        compiler_params=pltpu.CompilerParams(vmem_limit_bytes=size + (5 << 20)),
        cost_estimate=pl.CostEstimate(flops=int(us * 1e8), bytes_accessed=0, transcendentals=0),
        name=name,
    )(*(value for _, value in ins), *after)


class Sizes:
    def __init__(self, rows, tiles):
        self.grp, self.zz = lax.axis_size("grp"), lax.axis_size("zz")
        self.dom = 2 * self.zz
        self.rows, self.tiles = rows, tiles
        self.pair = rows // (self.grp * self.dom)
        self.piece = self.grp * self.pair
        self.per_grp = self.dom * self.pair
        assert rows // 128 < 5 and self.pair <= 128


def column(row):
    n = row.shape[1]
    on = iota((n, n), 0) == iota((n, n), 1)
    return jnp.sum(jnp.where(on, row.astype(F32), 0.0), axis=1, keepdims=True).astype(I32)


def index_kernel(z, me_ref, order_ref, out_ref):
    rows = z.rows
    shift = log2(rows)
    order_r = order_ref[...]
    order_c = column(order_r)
    down, across = iota((rows, rows), 0), iota((rows, rows), 1)
    source_r, source_c = order_r >> shift, order_c >> shift
    row_c = order_c & (rows - 1)
    same = jnp.where(source_c == source_r, 1.0, 0.0)
    rank_c = jnp.sum(jnp.where(across < down, same, 0.0), axis=1, keepdims=True).astype(I32)
    rank_r = jnp.sum(jnp.where(down < across, same, 0.0), axis=0, keepdims=True).astype(I32)
    owner = one_hot(iota((z.grp * z.dom, rows), 0) == source_r)
    at_rank = iota((rows, z.pair), 1) == rank_c
    high = jnp.where(at_rank, (row_c >> 4).astype(F32), 0.0).astype(BF16)
    low = jnp.where(at_rank, (row_c & 15).astype(F32), 0.0).astype(BF16)
    want = (dot(owner, high) * 16.0 + dot(owner, low)).astype(I32)
    out_ref[...] = jnp.zeros_like(out_ref)
    for d in range(z.grp * z.dom):
        out_ref[d, 0:1, 0:z.pair] = want[d:d + 1, :]
    across_grp = (source_r >> log2(z.dom)) ^ me_ref[0]
    inner = source_r & (z.dom - 1)
    slot = (inner * z.grp + across_grp) * z.pair + rank_r
    for i in range(rows // 128):
        lanes = slot[:, i * 128:(i + 1) * 128]
        out_ref[:, 1 + i:2 + i, :] = jnp.broadcast_to(lanes[None], (z.grp * z.dom, 1, 128))


def product_kernel(z, me_ref, features_ref, weight_ref, *outs):
    half = outs[0].shape[1]
    for flip, out in enumerate(outs):
        at = pl.multiple_of((me_ref[2] ^ flip) * half, half)
        out[...] = dot(features_ref[...], weight_ref[:, pl.ds(at, half)]).astype(BF16)


def send_kernel(z, me_ref, message_ref, own_ref, other_ref, pick_ref, *outs):
    devices, height, width = message_ref.shape
    message = message_ref[...].reshape(devices * height, width)
    shape = (z.rows, devices * height)
    asker = (iota(shape, 0) >> log2(z.pair)) ^ (me_ref[0] * z.dom)
    spread = one_hot(iota(shape, 1) == asker * height)
    high = dot(spread, (message >> 4).astype(F32).astype(BF16))
    low = dot(spread, (message & 15).astype(F32).astype(BF16))
    mine = iota((z.rows, width), 1) == (iota((z.rows, width), 0) & (z.pair - 1))
    wanted = jnp.sum(jnp.where(mine, high * 16.0 + low, 0.0), axis=1, keepdims=True).astype(I32)
    pick_ref[...] = one_hot(iota((z.rows, z.rows), 1) == wanted)
    for flip, product in enumerate((own_ref, other_ref)):
        got = dot(pick_ref[...], product[...]).astype(BF16)
        for s in range(z.grp):
            outs[s][flip] = got[s * z.per_grp:(s + 1) * z.per_grp, :]


def rows_kernel(z, pick_ref, features_ref, *outs):
    for s, out in enumerate(outs):
        pick = pick_ref[s * z.per_grp:(s + 1) * z.per_grp, :]
        out[...] = dot(pick, features_ref[...]).astype(BF16)


def pack_kernel(z, *refs):
    ins, outs = refs[:z.grp][::-1], refs[z.grp:]
    for rel, out in enumerate(outs):
        for s in range(z.grp):
            out[s * z.per_grp:(s + 1) * z.per_grp, :] = ins[s][rel]


def prepare_kernel(z, me_ref, cols_ref, message_ref, vals_ref, *refs):
    outs, (total, dense) = refs[:z.zz], refs[z.zz:]
    tiles, blocks, tile, _ = vals_ref.shape

    @pl.loop(0, tiles)
    def _(t):
        total[...] = jnp.zeros_like(total)
        for k in range(blocks):
            at = pl.multiple_of(cols_ref[t, k] * tile, tile)
            total[pl.ds(at, tile), :] += vals_ref[t, k].T.astype(F32)
        left = pl.multiple_of(t * tile, tile)
        dense[:, pl.ds(left, tile)] = total[pl.ds(0, z.dom * z.rows), :].astype(BF16)

    @pl.loop(0, z.dom)
    def _(n):
        message = message_ref[me_ref[0] * z.dom + n]
        slot = jnp.concatenate([message[1 + i:2 + i, :] for i in range(z.rows // 128)], axis=1)
        rank, at = slot & (z.pair - 1), slot >> log2(z.pair)
        s, at = at & (z.grp - 1), at >> log2(z.grp)
        k = (place_of(me_ref[1], z.zz) - place_of(at >> 1, z.zz)) & (z.zz - 1)
        rel = (at & 1) ^ me_ref[2]
        slot = ((k * 2 + rel) * z.grp + s) * z.pair + rank
        place = one_hot(iota((z.rows, z.rows), 0) == slot)
        at = pl.multiple_of(n * z.rows, z.rows)
        part = dot(place, dense[pl.ds(at, z.rows), :]).astype(BF16)
        for k in range(z.zz):
            for p in range(2 * z.grp):
                first = (k * 2 * z.grp + p) * z.pair
                rows = part[first:first + z.pair, :]
                if z.pair % 16 == 0:
                    to = pl.multiple_of(p * z.per_grp + n * z.pair, z.pair)
                    outs[k][pl.ds(to, z.pair), :] = rows
                else:
                    outs[k][p, n] = rows


def turn_kernel(*refs):
    out, height = refs[-1], refs[0].shape[0]
    for s, part in enumerate(refs[:-1]):
        out[:, s * height:(s + 1) * height] = part[...].T


def forward_kernel(z, first, last, *refs):
    turned, refs = refs[:2], refs[2:]
    rows, refs = jnp.concatenate([ref[...] for ref in refs[:2]], axis=0), refs[2:]
    agg = [dot_rows(ref[...], rows) for ref in turned]
    if not first:
        agg = [part + ref[...] for part, ref in zip(agg, refs)]
        refs = refs[2:]
    if not last:
        for ref, part in zip(refs, agg):
            ref[...] = part
        return
    cots, ahead, hiddens, grads = (refs[2 * i:2 * i + 2] for i in range(4))
    for part, cot, hidden, grad in zip(agg, cots, hiddens, grads):
        sig = jax.nn.sigmoid(part)
        hidden[...] = (part * sig).astype(BF16)
        grad[...] = (cot[...].astype(F32) * (sig * (1.0 + part * (1.0 - sig)))).astype(BF16)
    back_kernel(*ahead, *grads, *refs[-2:])


def back_kernel(turned_a, turned_b, grad_a, grad_b, *outs):
    size = outs[0].shape[0]
    for i, out in enumerate(outs):
        rows = pl.ds(i * size, size)
        value = dot(turned_a[rows, :], grad_a[...]) + dot(turned_b[rows, :], grad_b[...])
        out[...] = value.astype(out.dtype)


def pass_kernel(mine_ref, come_ref, out_ref):
    out_ref[...] = (mine_ref[...] + come_ref[...].astype(F32)).astype(BF16)


def part_kernel(left_ref, mine_ref, come_ref, out_ref):
    grad = (mine_ref[...] + come_ref[...].astype(F32)).astype(BF16)
    out_ref[...] = dot(left_ref[...], grad)


def grad_kernel(z, me_ref, left_ref, mine_ref, come_ref, part_ref, *refs):
    outs, whole = refs[:-1], refs[-1]
    grad = (mine_ref[...] + come_ref[...].astype(F32)).astype(BF16)
    whole[...] = (part_ref[...] + dot(left_ref[...], grad)).astype(BF16)
    share = whole.shape[0] // z.grp
    for s in range(z.grp):
        at = pl.multiple_of((me_ref[0] ^ s) * share, share)
        outs[s][...] = whole[pl.ds(at, share), :]


def sum_kernel(*refs):
    refs[-1][...] = sum(term[...].astype(F32) for term in refs[:-1]).astype(BF16)


def last_kernel(z, me_ref, *refs):
    pieces, out = refs[:-1], refs[-1]
    share, half = pieces[0].shape
    for rel in range(2):
        left = pl.multiple_of((me_ref[2] ^ rel) * half, half)
        for s in range(z.grp):
            at = pl.multiple_of((me_ref[0] ^ s) * share, share)
            out[pl.ds(at, share), pl.ds(left, half)] = pieces[rel * z.grp + s][...].astype(F32)


def shards(features, node_order, block_cols, block_count, block_vals, weight, cotangent):
    rows, width_in = features.shape
    hidden_units = weight.shape[1]
    half = hidden_units // 2
    tiles, blocks, tile = block_vals.shape[0], block_vals.shape[1], block_vals.shape[-1]
    z = Sizes(rows, tiles)
    at_grp, at_zz, core = lax.axis_index("grp"), lax.axis_index("zz"), lax.axis_index("core")
    me = jnp.stack([at_grp, at_zz, core]).astype(I32)

    def to_core(x):
        return lax.ppermute(x, "core", [(0, 1), (1, 0)])

    def to_grp(x, s):
        return lax.ppermute(x, "grp", [(i, i ^ s) for i in range(z.grp)]) if s else x

    def to_zz(x, k):
        order = [i ^ (i >> 1) for i in range(z.zz)]
        return lax.ppermute(x, "zz", [(order[i], order[(i + k) % z.zz]) for i in range(z.zz)])

    first_half = features[:rows // 2]
    (message,) = call(
        lambda *refs: index_kernel(z, *refs),
        [((z.grp * z.dom, 8, 128), I32)],
        [("s", me), ("v", node_order.reshape(1, rows))],
        "index", 1,
    )
    message, features = lax.optimization_barrier((message, features))
    message = lax.all_to_all(
        message, ("grp", "zz", "core"), split_axis=0, concat_axis=0, tiled=True
    )
    vals_b = to_core(block_vals)

    def across(parts):
        return [to_grp(part, s) for s, part in enumerate(parts)]

    def pack(parts, after=()):
        return call(
            lambda *refs: pack_kernel(z, *refs),
            [((rows, half), BF16)] * 2,
            [("v", part) for part in parts[::-1]],
            "pack", 0.5, after=after, token=True,
        )

    def rows_of(pick, part, after):
        return call(
            lambda *refs: rows_kernel(z, *refs),
            [((z.per_grp, width_in), BF16)] * z.grp,
            [("v", pick), ("v", part)],
            "rows", 1, after=after, token=True,
        )

    def turned_of(parts):
        left, token = call(
            turn_kernel, [((width_in, rows), BF16)], [("v", part) for part in parts],
            "turn", 0.5, token=True,
        )
        return [left, to_core(left)], token

    products = call(
        lambda *refs: product_kernel(z, *refs),
        [((rows, half), BF16)] * 2,
        [("s", me), ("v", features), ("v", weight)],
        "product", 15,
    )
    pick, *got, token = call(
        lambda *refs: send_kernel(z, *refs),
        [((rows, rows), BF16)] + [((2, z.per_grp, half), BF16)] * z.grp,
        [("s", me), ("v", message)] + [("v", part) for part in products],
        "send", 1.5, token=True,
    )
    token, cotangent, block_cols = lax.optimization_barrier((token, cotangent, block_cols))
    own, other, token = pack(across(got), [token])
    ring = [[own, to_core(other)]]

    live = iota((tiles, blocks), 1) < block_count[:, None]
    cols_a = jnp.where(live, block_cols, z.dom * tiles)
    cols_b = to_core(cols_a)
    cot_a = lax.dynamic_slice_in_dim(cotangent, core * half, half, axis=1)
    cot_b = to_core(lax.dynamic_slice_in_dim(cotangent, (1 - core) * half, half, axis=1))

    wide = 2 * z.grp * z.per_grp
    inner = (wide, rows) if z.pair % 16 == 0 else (2 * z.grp, z.dom, z.pair, rows)

    def prepared(cols, vals, token):
        *got, token = call(
            lambda *refs: prepare_kernel(z, *refs),
            [(inner, BF16)] * z.zz,
            [("s", me), ("s", cols), ("v", message), ("v", vals)],
            "prepare", 7,
            (
                pltpu.VMEM((z.dom * rows + tile, tile), F32),
                pltpu.VMEM((z.dom * rows, rows), BF16),
            ),
            after=[token, cols_b], token=True,
        )
        return [part.reshape(wide, rows) for part in got], token

    for k in range(1, z.zz):
        ring.append([to_zz(part, 1) for part in ring[-1]])
        if k == 1:
            *picked, token = rows_of(pick, features, [token, cot_a, cot_b])
            lefts, token_l = turned_of(across(picked))
            turned_a, token = prepared(cols_a, block_vals, token)
            for part in range(2):
                ring[1][part], token = lax.optimization_barrier((ring[1][part], token))
        if k == 2:
            turned_b, token = prepared(cols_b, vals_b, token)
            ring[2][1], token = lax.optimization_barrier((ring[2][1], token))
    turned = (turned_a, turned_b)

    agg = []
    for k in range(z.zz):
        last = k == z.zz - 1
        ins = [("v", part) for part in (turned[0][k], turned[1][k], *ring[k], *agg)]
        outs = [((rows, half), F32)] * 2
        if last:
            ahead = (turned[0][k], turned[1][k])
            ins += [("v", part) for part in (cot_a, cot_b, *ahead)]
            outs = [((rows, half), BF16)] * 6
        agg = call(
            lambda *refs, k=k, last=last: forward_kernel(z, k == 0, last, *refs),
            outs, ins, "forward", 3 if last else 1,
            after=[token_l] if k == z.zz - 2 else [token] if k == 0 else (),
        )
    hidden_a, hidden_b, grad_a, grad_b, *came = agg

    def back(k):
        return call(
            back_kernel,
            [((rows, half), F32)] * 2,
            [("v", part) for part in (turned[0][k], turned[1][k], grad_a, grad_b)],
            "back", 1,
        )

    come = to_core(hidden_b)
    for k in range(z.zz - 2, -1, -1):
        came = [to_zz(part, -1) for part in came]
        mine = back(k)
        if k:
            passed = [
                call(
                    pass_kernel, [((rows, half), BF16)], [("v", part), ("v", moved)], "pass", 0.5,
                    after=[come] if i == 1 and k == 1 else (), token=True,
                )
                for i, (part, moved) in enumerate(zip(mine, came))
            ]
            came = [part for part, _ in passed]
    first = core == 0
    hidden = jnp.concatenate(
        [jnp.where(first, hidden_a, come), jnp.where(first, come, hidden_a)], axis=1
    )

    share = width_in // z.grp
    (part,) = call(
        part_kernel, [((width_in, half), F32)],
        [("v", value) for value in (lefts[0], mine[0], came[0])], "part", 1,
    )
    terms = call(
        lambda *refs: grad_kernel(z, *refs),
        [((share, half), BF16)] * z.grp,
        [("s", me)] + [("v", value) for value in (lefts[1], mine[1], came[1], part)],
        "grad", 1.5,
        (pltpu.VMEM((width_in, half), BF16),),
    )

    def total_of(parts):
        return call(
            sum_kernel, [((share, half), BF16)], [("v", part) for part in parts], "sum", 0.5
        )[0]

    mine = total_of(across(terms)[::-1])
    step = 1
    while step < z.zz:
        mine = total_of(
            [mine, lax.ppermute(mine, "zz", [(i, i ^ step) for i in range(z.zz)])]
        )
        step *= 2
    mine = across([mine] * z.grp)
    (grad_weight,) = call(
        lambda *refs: last_kernel(z, *refs),
        [((width_in, hidden_units), F32)],
        [("s", me)] + [("v", part) for part in mine + [to_core(part) for part in mine]],
        "last", 2,
    )
    return hidden, grad_weight


def solution(mesh):
    n_grp, n_dom = mesh.shape["grp"], mesh.shape["dom"]
    split = Mesh(mesh.devices.reshape(n_grp, n_dom // 2, 2), ("grp", "zz", "core"))
    by_rows = ("grp", "zz", "core")
    placed = (
        P(by_rows, None),
        P(by_rows),
        P(by_rows, None),
        P(by_rows),
        P(by_rows, None, None, None),
        P(),
        P(by_rows, None),
    )
    return jax.shard_map(
        shards,
        mesh=split,
        in_specs=placed,
        out_specs=(P(by_rows, None), P()),
        check_vma=False,
    )
```

```python
import jax
import jax.numpy as jnp
from jax import lax
from jax.experimental import pallas as pl
from jax.experimental.pallas import tpu as pltpu
from jax.sharding import Mesh, PartitionSpec as P

BF16 = jnp.bfloat16
F32 = jnp.float32
I32 = jnp.int32


def log2(n):
    assert n & (n - 1) == 0
    return n.bit_length() - 1


def place_of(at, count):
    place = at
    for shift in range(1, log2(count)):
        place = place ^ (at >> shift)
    return place


def iota(shape, dim):
    return lax.broadcasted_iota(I32, shape, dim)


def one_hot(mask):
    return jnp.where(mask, 1.0, 0.0).astype(BF16)


def dot(a, b):
    return jnp.dot(a, b, preferred_element_type=F32)


def dot_rows(a, b):
    return lax.dot_general(a, b, (((0,), (0,)), ((), ())), preferred_element_type=F32)


def call(body, outs, ins, name, us, scratch=(), after=(), token=False):
    smem = pl.BlockSpec(memory_space=pltpu.SMEM)
    vmem = pl.BlockSpec(memory_space=pltpu.VMEM)
    count = len(ins)
    ties = len(after)
    if token:
        outs = [*outs, ((8, 128), F32)]

    def kernel(*refs):
        refs = refs[:count] + refs[count + ties:]
        if token:
            at = count + len(outs) - 1
            refs[at][...] = jnp.zeros((8, 128), F32)
            refs = refs[:at] + refs[at + 1:]
        body(*refs)

    arrays = [jax.ShapeDtypeStruct(s, d) for s, d in outs] + [value for _, value in ins]
    size = sum(a.size * a.dtype.itemsize for a in arrays + [m.get_array_aval() for m in scratch])
    return pl.pallas_call(
        kernel,
        out_shape=tuple(jax.ShapeDtypeStruct(s, d) for s, d in outs),
        in_specs=[smem if where == "s" else vmem for where, _ in ins]
        + [vmem] * ties,
        out_specs=tuple(vmem for _ in outs),
        scratch_shapes=list(scratch),
        compiler_params=pltpu.CompilerParams(vmem_limit_bytes=size + (5 << 20)),
        cost_estimate=pl.CostEstimate(flops=int(us * 1e8), bytes_accessed=0, transcendentals=0),
        name=name,
    )(*(value for _, value in ins), *after)


class Sizes:
    def __init__(self, rows, tiles):
        self.grp, self.zz = lax.axis_size("grp"), lax.axis_size("zz")
        self.dom = 2 * self.zz
        self.rows, self.tiles = rows, tiles
        self.pair = rows // (self.grp * self.dom)
        self.piece = self.grp * self.pair
        self.per_grp = self.dom * self.pair
        assert rows // 128 < 5 and self.pair <= 128


def column(row):
    n = row.shape[1]
    on = iota((n, n), 0) == iota((n, n), 1)
    return jnp.sum(jnp.where(on, row.astype(F32), 0.0), axis=1, keepdims=True).astype(I32)


def index_kernel(z, me_ref, order_ref, out_ref):
    rows = z.rows
    shift = log2(rows)
    order_r = order_ref[...]
    order_c = column(order_r)
    down, across = iota((rows, rows), 0), iota((rows, rows), 1)
    source_r, source_c = order_r >> shift, order_c >> shift
    row_c = order_c & (rows - 1)
    same = jnp.where(source_c == source_r, 1.0, 0.0)
    rank_c = jnp.sum(jnp.where(across < down, same, 0.0), axis=1, keepdims=True).astype(I32)
    rank_r = jnp.sum(jnp.where(down < across, same, 0.0), axis=0, keepdims=True).astype(I32)
    owner = one_hot(iota((z.grp * z.dom, rows), 0) == source_r)
    at_rank = iota((rows, z.pair), 1) == rank_c
    high = jnp.where(at_rank, (row_c >> 4).astype(F32), 0.0).astype(BF16)
    low = jnp.where(at_rank, (row_c & 15).astype(F32), 0.0).astype(BF16)
    want = (dot(owner, high) * 16.0 + dot(owner, low)).astype(I32)
    out_ref[...] = jnp.zeros_like(out_ref)
    for d in range(z.grp * z.dom):
        out_ref[d, 0:1, 0:z.pair] = want[d:d + 1, :]
    across_grp = (source_r >> log2(z.dom)) ^ me_ref[0]
    inner = source_r & (z.dom - 1)
    slot = (inner * z.grp + across_grp) * z.pair + rank_r
    for i in range(rows // 128):
        lanes = slot[:, i * 128:(i + 1) * 128]
        out_ref[:, 1 + i:2 + i, :] = jnp.broadcast_to(lanes[None], (z.grp * z.dom, 1, 128))


def product_kernel(z, me_ref, features_ref, weight_ref, *outs):
    half = outs[0].shape[1]
    for flip, out in enumerate(outs):
        at = pl.multiple_of((me_ref[2] ^ flip) * half, half)
        out[...] = dot(features_ref[...], weight_ref[:, pl.ds(at, half)]).astype(BF16)


def send_kernel(z, me_ref, message_ref, own_ref, other_ref, pick_ref, *outs):
    devices, height, width = message_ref.shape
    message = message_ref[...].reshape(devices * height, width)
    shape = (z.rows, devices * height)
    asker = (iota(shape, 0) >> log2(z.pair)) ^ (me_ref[0] * z.dom)
    spread = one_hot(iota(shape, 1) == asker * height)
    high = dot(spread, (message >> 4).astype(F32).astype(BF16))
    low = dot(spread, (message & 15).astype(F32).astype(BF16))
    mine = iota((z.rows, width), 1) == (iota((z.rows, width), 0) & (z.pair - 1))
    wanted = jnp.sum(jnp.where(mine, high * 16.0 + low, 0.0), axis=1, keepdims=True).astype(I32)
    pick_ref[...] = one_hot(iota((z.rows, z.rows), 1) == wanted)
    for flip, product in enumerate((own_ref, other_ref)):
        got = dot(pick_ref[...], product[...]).astype(BF16)
        for s in range(z.grp):
            outs[s][flip] = got[s * z.per_grp:(s + 1) * z.per_grp, :]


def rows_kernel(z, pick_ref, features_ref, *outs):
    for s, out in enumerate(outs):
        pick = pick_ref[s * z.per_grp:(s + 1) * z.per_grp, :]
        out[...] = dot(pick, features_ref[...]).astype(BF16)


def pack_kernel(z, *refs):
    ins, outs = refs[:z.grp][::-1], refs[z.grp:]
    for rel, out in enumerate(outs):
        for s in range(z.grp):
            out[s * z.per_grp:(s + 1) * z.per_grp, :] = ins[s][rel]


def prepare_kernel(z, me_ref, cols_ref, message_ref, vals_ref, *refs):
    outs, (total, dense) = refs[:z.zz], refs[z.zz:]
    tiles, blocks, tile, _ = vals_ref.shape

    @pl.loop(0, tiles)
    def _(t):
        total[...] = jnp.zeros_like(total)
        for k in range(blocks):
            at = pl.multiple_of(cols_ref[t, k] * tile, tile)
            total[pl.ds(at, tile), :] += vals_ref[t, k].T.astype(F32)
        left = pl.multiple_of(t * tile, tile)
        dense[:, pl.ds(left, tile)] = total[pl.ds(0, z.dom * z.rows), :].astype(BF16)

    @pl.loop(0, z.dom)
    def _(n):
        message = message_ref[me_ref[0] * z.dom + n]
        slot = jnp.concatenate([message[1 + i:2 + i, :] for i in range(z.rows // 128)], axis=1)
        rank, at = slot & (z.pair - 1), slot >> log2(z.pair)
        s, at = at & (z.grp - 1), at >> log2(z.grp)
        k = (place_of(me_ref[1], z.zz) - place_of(at >> 1, z.zz)) & (z.zz - 1)
        rel = (at & 1) ^ me_ref[2]
        slot = ((k * 2 + rel) * z.grp + s) * z.pair + rank
        place = one_hot(iota((z.rows, z.rows), 0) == slot)
        at = pl.multiple_of(n * z.rows, z.rows)
        part = dot(place, dense[pl.ds(at, z.rows), :]).astype(BF16)
        for k in range(z.zz):
            for p in range(2 * z.grp):
                first = (k * 2 * z.grp + p) * z.pair
                rows = part[first:first + z.pair, :]
                if z.pair % 16 == 0:
                    to = pl.multiple_of(p * z.per_grp + n * z.pair, z.pair)
                    outs[k][pl.ds(to, z.pair), :] = rows
                else:
                    outs[k][p, n] = rows


def turn_kernel(*refs):
    out, height = refs[-1], refs[0].shape[0]
    for s, part in enumerate(refs[:-1]):
        out[:, s * height:(s + 1) * height] = part[...].T


def forward_kernel(z, first, last, *refs):
    turned, refs = refs[:2], refs[2:]
    rows, refs = jnp.concatenate([ref[...] for ref in refs[:2]], axis=0), refs[2:]
    agg = [dot_rows(ref[...], rows) for ref in turned]
    if not first:
        agg = [part + ref[...] for part, ref in zip(agg, refs)]
        refs = refs[2:]
    if not last:
        for ref, part in zip(refs, agg):
            ref[...] = part
        return
    cots, ahead, hiddens, grads = (refs[2 * i:2 * i + 2] for i in range(4))
    for part, cot, hidden, grad in zip(agg, cots, hiddens, grads):
        sig = jax.nn.sigmoid(part)
        hidden[...] = (part * sig).astype(BF16)
        grad[...] = (cot[...].astype(F32) * (sig * (1.0 + part * (1.0 - sig)))).astype(BF16)
    back_kernel(*ahead, *grads, *refs[-2:])


def back_kernel(turned_a, turned_b, grad_a, grad_b, *outs):
    size = outs[0].shape[0]
    for i, out in enumerate(outs):
        rows = pl.ds(i * size, size)
        value = dot(turned_a[rows, :], grad_a[...]) + dot(turned_b[rows, :], grad_b[...])
        out[...] = value.astype(out.dtype)


def pass_kernel(mine_ref, come_ref, out_ref):
    out_ref[...] = (mine_ref[...] + come_ref[...].astype(F32)).astype(BF16)


def part_kernel(left_ref, mine_ref, come_ref, out_ref):
    grad = (mine_ref[...] + come_ref[...].astype(F32)).astype(BF16)
    out_ref[...] = dot(left_ref[...], grad)


def grad_kernel(z, me_ref, left_ref, mine_ref, come_ref, part_ref, *refs):
    outs, whole = refs[:-1], refs[-1]
    grad = (mine_ref[...] + come_ref[...].astype(F32)).astype(BF16)
    whole[...] = (part_ref[...] + dot(left_ref[...], grad)).astype(BF16)
    share = whole.shape[0] // z.grp
    for s in range(z.grp):
        at = pl.multiple_of((me_ref[0] ^ s) * share, share)
        outs[s][...] = whole[pl.ds(at, share), :]


def sum_kernel(*refs):
    refs[-1][...] = sum(term[...].astype(F32) for term in refs[:-1]).astype(BF16)


def last_kernel(z, me_ref, *refs):
    pieces, out = refs[:-1], refs[-1]
    share, half = pieces[0].shape
    for rel in range(2):
        left = pl.multiple_of((me_ref[2] ^ rel) * half, half)
        for s in range(z.grp):
            at = pl.multiple_of((me_ref[0] ^ s) * share, share)
            out[pl.ds(at, share), pl.ds(left, half)] = pieces[rel * z.grp + s][...].astype(F32)


def shards(features, node_order, block_cols, block_count, block_vals, weight, cotangent):
    rows, width_in = features.shape
    hidden_units = weight.shape[1]
    half = hidden_units // 2
    tiles, blocks, tile = block_vals.shape[0], block_vals.shape[1], block_vals.shape[-1]
    z = Sizes(rows, tiles)
    at_grp, at_zz, core = lax.axis_index("grp"), lax.axis_index("zz"), lax.axis_index("core")
    me = jnp.stack([at_grp, at_zz, core]).astype(I32)

    def to_core(x):
        return lax.ppermute(x, "core", [(0, 1), (1, 0)])

    def to_grp(x, s):
        return lax.ppermute(x, "grp", [(i, i ^ s) for i in range(z.grp)]) if s else x

    def to_zz(x, k):
        order = [i ^ (i >> 1) for i in range(z.zz)]
        return lax.ppermute(x, "zz", [(order[i], order[(i + k) % z.zz]) for i in range(z.zz)])

    first_half = features[:rows // 2]
    (message,) = call(
        lambda *refs: index_kernel(z, *refs),
        [((z.grp * z.dom, 8, 128), I32)],
        [("s", me), ("v", node_order.reshape(1, rows))],
        "index", 1,
    )
    message, features = lax.optimization_barrier((message, features))
    message = lax.all_to_all(
        message, ("grp", "zz", "core"), split_axis=0, concat_axis=0, tiled=True
    )
    vals_b = to_core(block_vals)

    def across(parts):
        return [to_grp(part, s) for s, part in enumerate(parts)]

    def pack(parts, after=()):
        return call(
            lambda *refs: pack_kernel(z, *refs),
            [((rows, half), BF16)] * 2,
            [("v", part) for part in parts[::-1]],
            "pack", 0.5, after=after, token=True,
        )

    def rows_of(pick, part, after):
        return call(
            lambda *refs: rows_kernel(z, *refs),
            [((z.per_grp, width_in), BF16)] * z.grp,
            [("v", pick), ("v", part)],
            "rows", 1, after=after, token=True,
        )

    def turned_of(parts):
        left, token = call(
            turn_kernel, [((width_in, rows), BF16)], [("v", part) for part in parts],
            "turn", 0.5, token=True,
        )
        return [left, to_core(left)], token

    products = call(
        lambda *refs: product_kernel(z, *refs),
        [((rows, half), BF16)] * 2,
        [("s", me), ("v", features), ("v", weight)],
        "product", 15,
    )
    pick, *got, token = call(
        lambda *refs: send_kernel(z, *refs),
        [((rows, rows), BF16)] + [((2, z.per_grp, half), BF16)] * z.grp,
        [("s", me), ("v", message)] + [("v", part) for part in products],
        "send", 1.5, token=True,
    )
    token, cotangent, block_cols = lax.optimization_barrier((token, cotangent, block_cols))
    own, other, token = pack(across(got), [token])
    ring = [[own, to_core(other)]]

    live = iota((tiles, blocks), 1) < block_count[:, None]
    cols_a = jnp.where(live, block_cols, z.dom * tiles)
    cols_b = to_core(cols_a)
    cot_a = lax.dynamic_slice_in_dim(cotangent, core * half, half, axis=1)
    cot_b = to_core(lax.dynamic_slice_in_dim(cotangent, (1 - core) * half, half, axis=1))

    wide = 2 * z.grp * z.per_grp
    inner = (wide, rows) if z.pair % 16 == 0 else (2 * z.grp, z.dom, z.pair, rows)

    def prepared(cols, vals, token):
        *got, token = call(
            lambda *refs: prepare_kernel(z, *refs),
            [(inner, BF16)] * z.zz,
            [("s", me), ("s", cols), ("v", message), ("v", vals)],
            "prepare", 7,
            (
                pltpu.VMEM((z.dom * rows + tile, tile), F32),
                pltpu.VMEM((z.dom * rows, rows), BF16),
            ),
            after=[token, cols_b], token=True,
        )
        return [part.reshape(wide, rows) for part in got], token

    for k in range(1, z.zz):
        ring.append([to_zz(part, 1) for part in ring[-1]])
        if k == 1:
            *picked, token = rows_of(pick, features, [token, cot_a, cot_b])
            lefts, token_l = turned_of(across(picked))
            turned_a, token = prepared(cols_a, block_vals, token)
            for part in range(2):
                ring[1][part], token = lax.optimization_barrier((ring[1][part], token))
        if k == 2:
            turned_b, token = prepared(cols_b, vals_b, token)
            ring[2][1], token = lax.optimization_barrier((ring[2][1], token))
    turned = (turned_a, turned_b)

    agg = []
    for k in range(z.zz):
        last = k == z.zz - 1
        ins = [("v", part) for part in (turned[0][k], turned[1][k], *ring[k], *agg)]
        outs = [((rows, half), F32)] * 2
        if last:
            ahead = (turned[0][k], turned[1][k])
            ins += [("v", part) for part in (cot_a, cot_b, *ahead)]
            outs = [((rows, half), BF16)] * 6
        agg = call(
            lambda *refs, k=k, last=last: forward_kernel(z, k == 0, last, *refs),
            outs, ins, "forward", 3 if last else 1,
            after=[token_l] if k == z.zz - 2 else [token] if k == 0 else (),
        )
    hidden_a, hidden_b, grad_a, grad_b, *came = agg

    def back(k):
        return call(
            back_kernel,
            [((rows, half), F32)] * 2,
            [("v", part) for part in (turned[0][k], turned[1][k], grad_a, grad_b)],
            "back", 1,
        )

    come = to_core(hidden_b)
    for k in range(z.zz - 2, -1, -1):
        came = [to_zz(part, -1) for part in came]
        mine = back(k)
        if k:
            passed = [
                call(
                    pass_kernel, [((rows, half), BF16)], [("v", part), ("v", moved)], "pass", 0.5,
                    after=[come] if i == 1 and k == z.zz - 2 else (), token=True,
                )
                for i, (part, moved) in enumerate(zip(mine, came))
            ]
            came = [part for part, _ in passed]
    first = core == 0
    hidden = jnp.concatenate(
        [jnp.where(first, hidden_a, come), jnp.where(first, come, hidden_a)], axis=1
    )

    share = width_in // z.grp
    (part,) = call(
        part_kernel, [((width_in, half), F32)],
        [("v", value) for value in (lefts[0], mine[0], came[0])], "part", 1,
    )
    terms = call(
        lambda *refs: grad_kernel(z, *refs),
        [((share, half), BF16)] * z.grp,
        [("s", me)] + [("v", value) for value in (lefts[1], mine[1], came[1], part)],
        "grad", 1.5,
        (pltpu.VMEM((width_in, half), BF16),),
    )

    def total_of(parts):
        return call(
            sum_kernel, [((share, half), BF16)], [("v", part) for part in parts], "sum", 0.5
        )[0]

    mine = total_of(across(terms)[::-1])
    step = 1
    while step < z.zz:
        mine = total_of(
            [mine, lax.ppermute(mine, "zz", [(i, i ^ step) for i in range(z.zz)])]
        )
        step *= 2
    mine = across([mine] * z.grp)
    (grad_weight,) = call(
        lambda *refs: last_kernel(z, *refs),
        [((width_in, hidden_units), F32)],
        [("s", me)] + [("v", part) for part in mine + [to_core(part) for part in mine]],
        "last", 2,
    )
    return hidden, grad_weight


def solution(mesh):
    n_grp, n_dom = mesh.shape["grp"], mesh.shape["dom"]
    split = Mesh(mesh.devices.reshape(n_grp, n_dom // 2, 2), ("grp", "zz", "core"))
    by_rows = ("grp", "zz", "core")
    placed = (
        P(by_rows, None),
        P(by_rows),
        P(by_rows, None),
        P(by_rows),
        P(by_rows, None, None, None),
        P(),
        P(by_rows, None),
    )
    return jax.shard_map(
        shards,
        mesh=split,
        in_specs=placed,
        out_specs=(P(by_rows, None), P()),
        check_vma=False,
    )
```

```python
import jax
import jax.numpy as jnp
from jax import lax
from jax.experimental import pallas as pl
from jax.experimental.pallas import tpu as pltpu
from jax.sharding import Mesh, PartitionSpec as P

BF16 = jnp.bfloat16
F32 = jnp.float32
I32 = jnp.int32


def log2(n):
    assert n & (n - 1) == 0
    return n.bit_length() - 1


def place_of(at, count):
    place = at
    for shift in range(1, log2(count)):
        place = place ^ (at >> shift)
    return place


def iota(shape, dim):
    return lax.broadcasted_iota(I32, shape, dim)


def one_hot(mask):
    return jnp.where(mask, 1.0, 0.0).astype(BF16)


def dot(a, b):
    return jnp.dot(a, b, preferred_element_type=F32)


def dot_rows(a, b):
    return lax.dot_general(a, b, (((0,), (0,)), ((), ())), preferred_element_type=F32)


def call(body, outs, ins, name, us, scratch=(), after=(), token=False):
    smem = pl.BlockSpec(memory_space=pltpu.SMEM)
    vmem = pl.BlockSpec(memory_space=pltpu.VMEM)
    count = len(ins)
    ties = len(after)
    if token:
        outs = [*outs, ((8, 128), F32)]

    def kernel(*refs):
        refs = refs[:count] + refs[count + ties:]
        if token:
            at = count + len(outs) - 1
            refs[at][...] = jnp.zeros((8, 128), F32)
            refs = refs[:at] + refs[at + 1:]
        body(*refs)

    arrays = [jax.ShapeDtypeStruct(s, d) for s, d in outs] + [value for _, value in ins]
    size = sum(a.size * a.dtype.itemsize for a in arrays + [m.get_array_aval() for m in scratch])
    return pl.pallas_call(
        kernel,
        out_shape=tuple(jax.ShapeDtypeStruct(s, d) for s, d in outs),
        in_specs=[smem if where == "s" else vmem for where, _ in ins]
        + [vmem] * ties,
        out_specs=tuple(vmem for _ in outs),
        scratch_shapes=list(scratch),
        compiler_params=pltpu.CompilerParams(vmem_limit_bytes=size + (5 << 20)),
        cost_estimate=pl.CostEstimate(flops=int(us * 1e8), bytes_accessed=0, transcendentals=0),
        name=name,
    )(*(value for _, value in ins), *after)


class Sizes:
    def __init__(self, rows, tiles):
        self.grp, self.zz = lax.axis_size("grp"), lax.axis_size("zz")
        self.dom = 2 * self.zz
        self.rows, self.tiles = rows, tiles
        self.pair = rows // (self.grp * self.dom)
        self.piece = self.grp * self.pair
        self.per_grp = self.dom * self.pair
        assert rows // 128 < 5 and self.pair <= 128


def column(row):
    n = row.shape[1]
    on = iota((n, n), 0) == iota((n, n), 1)
    return jnp.sum(jnp.where(on, row.astype(F32), 0.0), axis=1, keepdims=True).astype(I32)


def index_kernel(z, me_ref, order_ref, out_ref):
    rows = z.rows
    shift = log2(rows)
    order_r = order_ref[...]
    order_c = column(order_r)
    down, across = iota((rows, rows), 0), iota((rows, rows), 1)
    source_r, source_c = order_r >> shift, order_c >> shift
    row_c = order_c & (rows - 1)
    same = jnp.where(source_c == source_r, 1.0, 0.0)
    rank_c = jnp.sum(jnp.where(across < down, same, 0.0), axis=1, keepdims=True).astype(I32)
    rank_r = jnp.sum(jnp.where(down < across, same, 0.0), axis=0, keepdims=True).astype(I32)
    owner = one_hot(iota((z.grp * z.dom, rows), 0) == source_r)
    at_rank = iota((rows, z.pair), 1) == rank_c
    high = jnp.where(at_rank, (row_c >> 4).astype(F32), 0.0).astype(BF16)
    low = jnp.where(at_rank, (row_c & 15).astype(F32), 0.0).astype(BF16)
    want = (dot(owner, high) * 16.0 + dot(owner, low)).astype(I32)
    out_ref[...] = jnp.zeros_like(out_ref)
    for d in range(z.grp * z.dom):
        out_ref[d, 0:1, 0:z.pair] = want[d:d + 1, :]
    across_grp = (source_r >> log2(z.dom)) ^ me_ref[0]
    inner = source_r & (z.dom - 1)
    slot = (inner * z.grp + across_grp) * z.pair + rank_r
    for i in range(rows // 128):
        lanes = slot[:, i * 128:(i + 1) * 128]
        out_ref[:, 1 + i:2 + i, :] = jnp.broadcast_to(lanes[None], (z.grp * z.dom, 1, 128))


def product_kernel(z, me_ref, features_ref, weight_ref, *outs):
    half = outs[0].shape[1]
    for flip, out in enumerate(outs):
        at = pl.multiple_of((me_ref[2] ^ flip) * half, half)
        out[...] = dot(features_ref[...], weight_ref[:, pl.ds(at, half)]).astype(BF16)


def send_kernel(z, me_ref, message_ref, own_ref, other_ref, pick_ref, *outs):
    devices, height, width = message_ref.shape
    message = message_ref[...].reshape(devices * height, width)
    shape = (z.rows, devices * height)
    asker = (iota(shape, 0) >> log2(z.pair)) ^ (me_ref[0] * z.dom)
    spread = one_hot(iota(shape, 1) == asker * height)
    high = dot(spread, (message >> 4).astype(F32).astype(BF16))
    low = dot(spread, (message & 15).astype(F32).astype(BF16))
    mine = iota((z.rows, width), 1) == (iota((z.rows, width), 0) & (z.pair - 1))
    wanted = jnp.sum(jnp.where(mine, high * 16.0 + low, 0.0), axis=1, keepdims=True).astype(I32)
    pick_ref[...] = one_hot(iota((z.rows, z.rows), 1) == wanted)
    for flip, product in enumerate((own_ref, other_ref)):
        got = dot(pick_ref[...], product[...]).astype(BF16)
        for s in range(z.grp):
            outs[s][flip] = got[s * z.per_grp:(s + 1) * z.per_grp, :]


def rows_kernel(z, pick_ref, features_ref, *outs):
    for s, out in enumerate(outs):
        pick = pick_ref[s * z.per_grp:(s + 1) * z.per_grp, :]
        out[...] = dot(pick, features_ref[...]).astype(BF16)


def pack_kernel(z, *refs):
    ins, outs = refs[:z.grp][::-1], refs[z.grp:]
    for rel, out in enumerate(outs):
        for s in range(z.grp):
            out[s * z.per_grp:(s + 1) * z.per_grp, :] = ins[s][rel]


def prepare_kernel(z, me_ref, cols_ref, message_ref, vals_ref, *refs):
    outs, (total, dense) = refs[:z.zz], refs[z.zz:]
    tiles, blocks, tile, _ = vals_ref.shape

    @pl.loop(0, tiles)
    def _(t):
        total[...] = jnp.zeros_like(total)
        for k in range(blocks):
            at = pl.multiple_of(cols_ref[t, k] * tile, tile)
            total[pl.ds(at, tile), :] += vals_ref[t, k].T.astype(F32)
        left = pl.multiple_of(t * tile, tile)
        dense[:, pl.ds(left, tile)] = total[pl.ds(0, z.dom * z.rows), :].astype(BF16)

    @pl.loop(0, z.dom)
    def _(n):
        message = message_ref[me_ref[0] * z.dom + n]
        slot = jnp.concatenate([message[1 + i:2 + i, :] for i in range(z.rows // 128)], axis=1)
        rank, at = slot & (z.pair - 1), slot >> log2(z.pair)
        s, at = at & (z.grp - 1), at >> log2(z.grp)
        k = (place_of(me_ref[1], z.zz) - place_of(at >> 1, z.zz)) & (z.zz - 1)
        rel = (at & 1) ^ me_ref[2]
        slot = ((k * 2 + rel) * z.grp + s) * z.pair + rank
        place = one_hot(iota((z.rows, z.rows), 0) == slot)
        at = pl.multiple_of(n * z.rows, z.rows)
        part = dot(place, dense[pl.ds(at, z.rows), :]).astype(BF16)
        for k in range(z.zz):
            for p in range(2 * z.grp):
                first = (k * 2 * z.grp + p) * z.pair
                rows = part[first:first + z.pair, :]
                if z.pair % 16 == 0:
                    to = pl.multiple_of(p * z.per_grp + n * z.pair, z.pair)
                    outs[k][pl.ds(to, z.pair), :] = rows
                else:
                    outs[k][p, n] = rows


def turn_kernel(*refs):
    out, height = refs[-1], refs[0].shape[0]
    for s, part in enumerate(refs[:-1]):
        out[:, s * height:(s + 1) * height] = part[...].T


def forward_kernel(z, first, last, *refs):
    turned, refs = refs[:2], refs[2:]
    rows, refs = jnp.concatenate([ref[...] for ref in refs[:2]], axis=0), refs[2:]
    agg = [dot_rows(ref[...], rows) for ref in turned]
    if not first:
        agg = [part + ref[...] for part, ref in zip(agg, refs)]
        refs = refs[2:]
    if not last:
        for ref, part in zip(refs, agg):
            ref[...] = part
        return
    cots, ahead, hiddens, grads = (refs[2 * i:2 * i + 2] for i in range(4))
    for part, cot, hidden, grad in zip(agg, cots, hiddens, grads):
        sig = jax.nn.sigmoid(part)
        hidden[...] = (part * sig).astype(BF16)
        grad[...] = (cot[...].astype(F32) * (sig * (1.0 + part * (1.0 - sig)))).astype(BF16)
    back_kernel(*ahead, *grads, *refs[-2:])


def back_kernel(turned_a, turned_b, grad_a, grad_b, *outs):
    size = outs[0].shape[0]
    for i, out in enumerate(outs):
        rows = pl.ds(i * size, size)
        value = dot(turned_a[rows, :], grad_a[...]) + dot(turned_b[rows, :], grad_b[...])
        out[...] = value.astype(out.dtype)


def pass_kernel(mine_ref, come_ref, out_ref):
    out_ref[...] = (mine_ref[...] + come_ref[...].astype(F32)).astype(BF16)


def part_kernel(left_ref, mine_ref, come_ref, out_ref):
    grad = (mine_ref[...] + come_ref[...].astype(F32)).astype(BF16)
    out_ref[...] = dot(left_ref[...], grad)


def grad_kernel(z, me_ref, left_ref, mine_ref, come_ref, part_ref, *refs):
    outs, whole = refs[:-1], refs[-1]
    grad = (mine_ref[...] + come_ref[...].astype(F32)).astype(BF16)
    whole[...] = (part_ref[...] + dot(left_ref[...], grad)).astype(BF16)
    share = whole.shape[0] // z.grp
    for s in range(z.grp):
        at = pl.multiple_of((me_ref[0] ^ s) * share, share)
        outs[s][...] = whole[pl.ds(at, share), :]


def sum_kernel(*refs):
    refs[-1][...] = sum(term[...].astype(F32) for term in refs[:-1]).astype(BF16)


def last_kernel(z, me_ref, *refs):
    pieces, out = refs[:-1], refs[-1]
    share, half = pieces[0].shape
    for rel in range(2):
        left = pl.multiple_of((me_ref[2] ^ rel) * half, half)
        for s in range(z.grp):
            at = pl.multiple_of((me_ref[0] ^ s) * share, share)
            out[pl.ds(at, share), pl.ds(left, half)] = pieces[rel * z.grp + s][...].astype(F32)


def shards(features, node_order, block_cols, block_count, block_vals, weight, cotangent):
    rows, width_in = features.shape
    hidden_units = weight.shape[1]
    half = hidden_units // 2
    tiles, blocks, tile = block_vals.shape[0], block_vals.shape[1], block_vals.shape[-1]
    z = Sizes(rows, tiles)
    at_grp, at_zz, core = lax.axis_index("grp"), lax.axis_index("zz"), lax.axis_index("core")
    me = jnp.stack([at_grp, at_zz, core]).astype(I32)

    def to_core(x):
        return lax.ppermute(x, "core", [(0, 1), (1, 0)])

    def to_grp(x, s):
        return lax.ppermute(x, "grp", [(i, i ^ s) for i in range(z.grp)]) if s else x

    def to_zz(x, k):
        order = [i ^ (i >> 1) for i in range(z.zz)]
        return lax.ppermute(x, "zz", [(order[i], order[(i + k) % z.zz]) for i in range(z.zz)])

    first_half = features[:rows // 2]
    (message,) = call(
        lambda *refs: index_kernel(z, *refs),
        [((z.grp * z.dom, 8, 128), I32)],
        [("s", me), ("v", node_order.reshape(1, rows))],
        "index", 1,
    )
    message, features = lax.optimization_barrier((message, features))
    message = lax.all_to_all(
        message, ("grp", "zz", "core"), split_axis=0, concat_axis=0, tiled=True
    )
    vals_b = to_core(block_vals)

    def across(parts):
        return [to_grp(part, s) for s, part in enumerate(parts)]

    def pack(parts, after=()):
        return call(
            lambda *refs: pack_kernel(z, *refs),
            [((rows, half), BF16)] * 2,
            [("v", part) for part in parts[::-1]],
            "pack", 0.5, after=after, token=True,
        )

    def rows_of(pick, part, after):
        return call(
            lambda *refs: rows_kernel(z, *refs),
            [((z.per_grp, width_in), BF16)] * z.grp,
            [("v", pick), ("v", part)],
            "rows", 1, after=after, token=True,
        )

    def turned_of(parts):
        left, token = call(
            turn_kernel, [((width_in, rows), BF16)], [("v", part) for part in parts],
            "turn", 0.5, token=True,
        )
        return [left, to_core(left)], token

    products = call(
        lambda *refs: product_kernel(z, *refs),
        [((rows, half), BF16)] * 2,
        [("s", me), ("v", features), ("v", weight)],
        "product", 15,
    )
    pick, *got, token = call(
        lambda *refs: send_kernel(z, *refs),
        [((rows, rows), BF16)] + [((2, z.per_grp, half), BF16)] * z.grp,
        [("s", me), ("v", message)] + [("v", part) for part in products],
        "send", 1.5, token=True,
    )
    token, cotangent, block_cols = lax.optimization_barrier((token, cotangent, block_cols))
    own, other, token = pack(across(got), [token])
    ring = [[own, to_core(other)]]

    live = iota((tiles, blocks), 1) < block_count[:, None]
    cols_a = jnp.where(live, block_cols, z.dom * tiles)
    cols_b = to_core(cols_a)
    cot_a = lax.dynamic_slice_in_dim(cotangent, core * half, half, axis=1)
    cot_b = to_core(lax.dynamic_slice_in_dim(cotangent, (1 - core) * half, half, axis=1))

    wide = 2 * z.grp * z.per_grp
    inner = (wide, rows) if z.pair % 16 == 0 else (2 * z.grp, z.dom, z.pair, rows)

    def prepared(cols, vals, token):
        *got, token = call(
            lambda *refs: prepare_kernel(z, *refs),
            [(inner, BF16)] * z.zz,
            [("s", me), ("s", cols), ("v", message), ("v", vals)],
            "prepare", 7,
            (
                pltpu.VMEM((z.dom * rows + tile, tile), F32),
                pltpu.VMEM((z.dom * rows, rows), BF16),
            ),
            after=[token, cols_b], token=True,
        )
        return [part.reshape(wide, rows) for part in got], token

    for k in range(1, z.zz):
        ring.append([to_zz(part, 1) for part in ring[-1]])
        if k == 1:
            *picked, token = rows_of(pick, features, [token, cot_a, cot_b])
            lefts, token_l = turned_of(across(picked))
            turned_a, token = prepared(cols_a, block_vals, token)
            for part in range(2):
                ring[1][part], token = lax.optimization_barrier((ring[1][part], token))
        if k == 2:
            turned_b, token = prepared(cols_b, vals_b, token)
            ring[2][1], token = lax.optimization_barrier((ring[2][1], token))
    turned = (turned_a, turned_b)

    agg = []
    for k in range(z.zz):
        last = k == z.zz - 1
        ins = [("v", part) for part in (turned[0][k], turned[1][k], *ring[k], *agg)]
        outs = [((rows, half), F32)] * 2
        if last:
            ahead = (turned[0][k], turned[1][k])
            ins += [("v", part) for part in (cot_a, cot_b, *ahead)]
            outs = [((rows, half), BF16)] * 6
        agg = call(
            lambda *refs, k=k, last=last: forward_kernel(z, k == 0, last, *refs),
            outs, ins, "forward", 3 if last else 1,
            after=[token_l] if k == z.zz - 2 else [token] if k == 0 else (),
        )
    hidden_a, hidden_b, grad_a, grad_b, *came = agg

    def back(k):
        return call(
            back_kernel,
            [((rows, half), F32)] * 2,
            [("v", part) for part in (turned[0][k], turned[1][k], grad_a, grad_b)],
            "back", 1,
        )

    for k in range(z.zz - 2, -1, -1):
        came = [to_zz(part, -1) for part in came]
        mine = back(k)
        if k:
            passed = [
                call(
                    pass_kernel, [((rows, half), BF16)], [("v", part), ("v", moved)], "pass", 0.5,
                    token=True,
                )
                for i, (part, moved) in enumerate(zip(mine, came))
            ]
            came = [part for part, _ in passed]
            if k == 1:
                hidden_b, token = lax.optimization_barrier((hidden_b, passed[1][1]))
                come = to_core(hidden_b)
    first = core == 0
    hidden = jnp.concatenate(
        [jnp.where(first, hidden_a, come), jnp.where(first, come, hidden_a)], axis=1
    )

    share = width_in // z.grp
    (part,) = call(
        part_kernel, [((width_in, half), F32)],
        [("v", value) for value in (lefts[0], mine[0], came[0])], "part", 1,
        after=[come, token],
    )
    terms = call(
        lambda *refs: grad_kernel(z, *refs),
        [((share, half), BF16)] * z.grp,
        [("s", me)] + [("v", value) for value in (lefts[1], mine[1], came[1], part)],
        "grad", 1.5,
        (pltpu.VMEM((width_in, half), BF16),),
    )

    def total_of(parts):
        return call(
            sum_kernel, [((share, half), BF16)], [("v", part) for part in parts], "sum", 0.5
        )[0]

    mine = total_of(across(terms)[::-1])
    step = 1
    while step < z.zz:
        mine = total_of(
            [mine, lax.ppermute(mine, "zz", [(i, i ^ step) for i in range(z.zz)])]
        )
        step *= 2
    mine = across([mine] * z.grp)
    (grad_weight,) = call(
        lambda *refs: last_kernel(z, *refs),
        [((width_in, hidden_units), F32)],
        [("s", me)] + [("v", part) for part in mine + [to_core(part) for part in mine]],
        "last", 2,
    )
    return hidden, grad_weight


def solution(mesh):
    n_grp, n_dom = mesh.shape["grp"], mesh.shape["dom"]
    split = Mesh(mesh.devices.reshape(n_grp, n_dom // 2, 2), ("grp", "zz", "core"))
    by_rows = ("grp", "zz", "core")
    placed = (
        P(by_rows, None),
        P(by_rows),
        P(by_rows, None),
        P(by_rows),
        P(by_rows, None, None, None),
        P(),
        P(by_rows, None),
    )
    return jax.shard_map(
        shards,
        mesh=split,
        in_specs=placed,
        out_specs=(P(by_rows, None), P()),
        check_vma=False,
    )
```

```python
import jax
import jax.numpy as jnp
from jax import lax
from jax.experimental import pallas as pl
from jax.experimental.pallas import tpu as pltpu
from jax.sharding import Mesh, PartitionSpec as P

BF16 = jnp.bfloat16
F32 = jnp.float32
I32 = jnp.int32


def log2(n):
    assert n & (n - 1) == 0
    return n.bit_length() - 1


def place_of(at, count):
    place = at
    for shift in range(1, log2(count)):
        place = place ^ (at >> shift)
    return place


def iota(shape, dim):
    return lax.broadcasted_iota(I32, shape, dim)


def one_hot(mask):
    return jnp.where(mask, 1.0, 0.0).astype(BF16)


def dot(a, b):
    return jnp.dot(a, b, preferred_element_type=F32)


def dot_rows(a, b):
    return lax.dot_general(a, b, (((0,), (0,)), ((), ())), preferred_element_type=F32)


def call(body, outs, ins, name, us, scratch=(), after=(), token=False):
    smem = pl.BlockSpec(memory_space=pltpu.SMEM)
    vmem = pl.BlockSpec(memory_space=pltpu.VMEM)
    count = len(ins)
    ties = len(after)
    if token:
        outs = [*outs, ((8, 128), F32)]

    def kernel(*refs):
        refs = refs[:count] + refs[count + ties:]
        if token:
            at = count + len(outs) - 1
            refs[at][...] = jnp.zeros((8, 128), F32)
            refs = refs[:at] + refs[at + 1:]
        body(*refs)

    arrays = [jax.ShapeDtypeStruct(s, d) for s, d in outs] + [value for _, value in ins]
    size = sum(a.size * a.dtype.itemsize for a in arrays + [m.get_array_aval() for m in scratch])
    return pl.pallas_call(
        kernel,
        out_shape=tuple(jax.ShapeDtypeStruct(s, d) for s, d in outs),
        in_specs=[smem if where == "s" else vmem for where, _ in ins]
        + [vmem] * ties,
        out_specs=tuple(vmem for _ in outs),
        scratch_shapes=list(scratch),
        compiler_params=pltpu.CompilerParams(vmem_limit_bytes=size + (5 << 20)),
        cost_estimate=pl.CostEstimate(flops=int(us * 1e8), bytes_accessed=0, transcendentals=0),
        name=name,
    )(*(value for _, value in ins), *after)


class Sizes:
    def __init__(self, rows, tiles):
        self.grp, self.zz = lax.axis_size("grp"), lax.axis_size("zz")
        self.dom = 2 * self.zz
        self.rows, self.tiles = rows, tiles
        self.pair = rows // (self.grp * self.dom)
        self.piece = self.grp * self.pair
        self.per_grp = self.dom * self.pair
        assert rows // 128 < 5 and self.pair <= 128


def column(row):
    n = row.shape[1]
    on = iota((n, n), 0) == iota((n, n), 1)
    return jnp.sum(jnp.where(on, row.astype(F32), 0.0), axis=1, keepdims=True).astype(I32)


def index_kernel(z, me_ref, order_ref, out_ref):
    rows = z.rows
    shift = log2(rows)
    order_r = order_ref[...]
    order_c = column(order_r)
    down, across = iota((rows, rows), 0), iota((rows, rows), 1)
    source_r, source_c = order_r >> shift, order_c >> shift
    row_c = order_c & (rows - 1)
    same = jnp.where(source_c == source_r, 1.0, 0.0)
    rank_c = jnp.sum(jnp.where(across < down, same, 0.0), axis=1, keepdims=True).astype(I32)
    rank_r = jnp.sum(jnp.where(down < across, same, 0.0), axis=0, keepdims=True).astype(I32)
    owner = one_hot(iota((z.grp * z.dom, rows), 0) == source_r)
    at_rank = iota((rows, z.pair), 1) == rank_c
    high = jnp.where(at_rank, (row_c >> 4).astype(F32), 0.0).astype(BF16)
    low = jnp.where(at_rank, (row_c & 15).astype(F32), 0.0).astype(BF16)
    want = (dot(owner, high) * 16.0 + dot(owner, low)).astype(I32)
    out_ref[...] = jnp.zeros_like(out_ref)
    for d in range(z.grp * z.dom):
        out_ref[d, 0:1, 0:z.pair] = want[d:d + 1, :]
    across_grp = (source_r >> log2(z.dom)) ^ me_ref[0]
    inner = source_r & (z.dom - 1)
    slot = (inner * z.grp + across_grp) * z.pair + rank_r
    for i in range(rows // 128):
        lanes = slot[:, i * 128:(i + 1) * 128]
        out_ref[:, 1 + i:2 + i, :] = jnp.broadcast_to(lanes[None], (z.grp * z.dom, 1, 128))


def product_kernel(z, me_ref, features_ref, weight_ref, *outs):
    half = outs[0].shape[1]
    for flip, out in enumerate(outs):
        at = pl.multiple_of((me_ref[2] ^ flip) * half, half)
        out[...] = dot(features_ref[...], weight_ref[:, pl.ds(at, half)]).astype(BF16)


def send_kernel(z, me_ref, message_ref, own_ref, other_ref, pick_ref, *outs):
    devices, height, width = message_ref.shape
    message = message_ref[...].reshape(devices * height, width)
    shape = (z.rows, devices * height)
    asker = (iota(shape, 0) >> log2(z.pair)) ^ (me_ref[0] * z.dom)
    spread = one_hot(iota(shape, 1) == asker * height)
    high = dot(spread, (message >> 4).astype(F32).astype(BF16))
    low = dot(spread, (message & 15).astype(F32).astype(BF16))
    mine = iota((z.rows, width), 1) == (iota((z.rows, width), 0) & (z.pair - 1))
    wanted = jnp.sum(jnp.where(mine, high * 16.0 + low, 0.0), axis=1, keepdims=True).astype(I32)
    pick_ref[...] = one_hot(iota((z.rows, z.rows), 1) == wanted)
    for flip, product in enumerate((own_ref, other_ref)):
        got = dot(pick_ref[...], product[...]).astype(BF16)
        for s in range(z.grp):
            outs[s][flip] = got[s * z.per_grp:(s + 1) * z.per_grp, :]


def rows_kernel(z, pick_ref, features_ref, *outs):
    for s, out in enumerate(outs):
        pick = pick_ref[s * z.per_grp:(s + 1) * z.per_grp, :]
        out[...] = dot(pick, features_ref[...]).astype(BF16)


def pack_kernel(z, *refs):
    ins, outs = refs[:z.grp][::-1], refs[z.grp:]
    for rel, out in enumerate(outs):
        for s in range(z.grp):
            out[s * z.per_grp:(s + 1) * z.per_grp, :] = ins[s][rel]


def prepare_kernel(z, me_ref, cols_ref, message_ref, vals_ref, *refs):
    outs, (total, dense) = refs[:z.zz], refs[z.zz:]
    tiles, blocks, tile, _ = vals_ref.shape

    @pl.loop(0, tiles)
    def _(t):
        total[...] = jnp.zeros_like(total)
        for k in range(blocks):
            at = pl.multiple_of(cols_ref[t, k] * tile, tile)
            total[pl.ds(at, tile), :] += vals_ref[t, k].T.astype(F32)
        left = pl.multiple_of(t * tile, tile)
        dense[:, pl.ds(left, tile)] = total[pl.ds(0, z.dom * z.rows), :].astype(BF16)

    @pl.loop(0, z.dom)
    def _(n):
        message = message_ref[me_ref[0] * z.dom + n]
        slot = jnp.concatenate([message[1 + i:2 + i, :] for i in range(z.rows // 128)], axis=1)
        rank, at = slot & (z.pair - 1), slot >> log2(z.pair)
        s, at = at & (z.grp - 1), at >> log2(z.grp)
        k = (place_of(me_ref[1], z.zz) - place_of(at >> 1, z.zz)) & (z.zz - 1)
        rel = (at & 1) ^ me_ref[2]
        slot = ((k * 2 + rel) * z.grp + s) * z.pair + rank
        place = one_hot(iota((z.rows, z.rows), 0) == slot)
        at = pl.multiple_of(n * z.rows, z.rows)
        part = dot(place, dense[pl.ds(at, z.rows), :]).astype(BF16)
        for k in range(z.zz):
            for p in range(2 * z.grp):
                first = (k * 2 * z.grp + p) * z.pair
                rows = part[first:first + z.pair, :]
                if z.pair % 16 == 0:
                    to = pl.multiple_of(p * z.per_grp + n * z.pair, z.pair)
                    outs[k][pl.ds(to, z.pair), :] = rows
                else:
                    outs[k][p, n] = rows


def turn_kernel(*refs):
    out, height = refs[-1], refs[0].shape[0]
    for s, part in enumerate(refs[:-1]):
        out[:, s * height:(s + 1) * height] = part[...].T


def forward_kernel(z, first, last, *refs):
    turned, refs = refs[:2], refs[2:]
    rows, refs = jnp.concatenate([ref[...] for ref in refs[:2]], axis=0), refs[2:]
    agg = [dot_rows(ref[...], rows) for ref in turned]
    if not first:
        agg = [part + ref[...] for part, ref in zip(agg, refs)]
        refs = refs[2:]
    if not last:
        for ref, part in zip(refs, agg):
            ref[...] = part
        return
    cots, ahead, hiddens, grads = (refs[2 * i:2 * i + 2] for i in range(4))
    for part, cot, hidden, grad in zip(agg, cots, hiddens, grads):
        sig = jax.nn.sigmoid(part)
        hidden[...] = (part * sig).astype(BF16)
        grad[...] = (cot[...].astype(F32) * (sig * (1.0 + part * (1.0 - sig)))).astype(BF16)
    back_kernel(*ahead, *grads, *refs[-2:])


def back_kernel(turned_a, turned_b, grad_a, grad_b, *outs):
    size = outs[0].shape[0]
    for i, out in enumerate(outs):
        rows = pl.ds(i * size, size)
        value = dot(turned_a[rows, :], grad_a[...]) + dot(turned_b[rows, :], grad_b[...])
        out[...] = value.astype(out.dtype)


def pass_kernel(mine_ref, come_ref, out_ref):
    out_ref[...] = (mine_ref[...] + come_ref[...].astype(F32)).astype(BF16)


def part_kernel(left_ref, mine_ref, come_ref, out_ref):
    grad = (mine_ref[...] + come_ref[...].astype(F32)).astype(BF16)
    out_ref[...] = dot(left_ref[...], grad)


def grad_kernel(z, me_ref, left_ref, mine_ref, come_ref, part_ref, *refs):
    outs, whole = refs[:-1], refs[-1]
    grad = (mine_ref[...] + come_ref[...].astype(F32)).astype(BF16)
    whole[...] = (part_ref[...] + dot(left_ref[...], grad)).astype(BF16)
    share = whole.shape[0] // z.grp
    for s in range(z.grp):
        at = pl.multiple_of((me_ref[0] ^ s) * share, share)
        outs[s][...] = whole[pl.ds(at, share), :]


def sum_kernel(*refs):
    refs[-1][...] = sum(term[...].astype(F32) for term in refs[:-1]).astype(BF16)


def last_kernel(z, me_ref, *refs):
    first, *rest, out = refs
    pieces = [*rest[:z.grp], first, *rest[z.grp:]]
    share, half = pieces[0].shape
    for rel in range(2):
        left = pl.multiple_of((me_ref[2] ^ rel) * half, half)
        for s in range(z.grp):
            at = pl.multiple_of((me_ref[0] ^ s) * share, share)
            out[pl.ds(at, share), pl.ds(left, half)] = pieces[rel * z.grp + s][...].astype(F32)


def shards(features, node_order, block_cols, block_count, block_vals, weight, cotangent):
    rows, width_in = features.shape
    hidden_units = weight.shape[1]
    half = hidden_units // 2
    tiles, blocks, tile = block_vals.shape[0], block_vals.shape[1], block_vals.shape[-1]
    z = Sizes(rows, tiles)
    at_grp, at_zz, core = lax.axis_index("grp"), lax.axis_index("zz"), lax.axis_index("core")
    me = jnp.stack([at_grp, at_zz, core]).astype(I32)

    def to_core(x):
        return lax.ppermute(x, "core", [(0, 1), (1, 0)])

    def to_grp(x, s):
        return lax.ppermute(x, "grp", [(i, i ^ s) for i in range(z.grp)]) if s else x

    def to_zz(x, k):
        order = [i ^ (i >> 1) for i in range(z.zz)]
        return lax.ppermute(x, "zz", [(order[i], order[(i + k) % z.zz]) for i in range(z.zz)])

    first_half = features[:rows // 2]
    (message,) = call(
        lambda *refs: index_kernel(z, *refs),
        [((z.grp * z.dom, 8, 128), I32)],
        [("s", me), ("v", node_order.reshape(1, rows))],
        "index", 1,
    )
    message, features = lax.optimization_barrier((message, features))
    message = lax.all_to_all(
        message, ("grp", "zz", "core"), split_axis=0, concat_axis=0, tiled=True
    )
    vals_b = to_core(block_vals)

    def across(parts):
        return [to_grp(part, s) for s, part in enumerate(parts)]

    def pack(parts, after=()):
        return call(
            lambda *refs: pack_kernel(z, *refs),
            [((rows, half), BF16)] * 2,
            [("v", part) for part in parts[::-1]],
            "pack", 0.5, after=after, token=True,
        )

    def rows_of(pick, part, after):
        return call(
            lambda *refs: rows_kernel(z, *refs),
            [((z.per_grp, width_in), BF16)] * z.grp,
            [("v", pick), ("v", part)],
            "rows", 1, after=after, token=True,
        )

    def turned_of(parts):
        left, token = call(
            turn_kernel, [((width_in, rows), BF16)], [("v", part) for part in parts],
            "turn", 0.5, token=True,
        )
        return [left, to_core(left)], token

    products = call(
        lambda *refs: product_kernel(z, *refs),
        [((rows, half), BF16)] * 2,
        [("s", me), ("v", features), ("v", weight)],
        "product", 15,
    )
    pick, *got, token = call(
        lambda *refs: send_kernel(z, *refs),
        [((rows, rows), BF16)] + [((2, z.per_grp, half), BF16)] * z.grp,
        [("s", me), ("v", message)] + [("v", part) for part in products],
        "send", 1.5, token=True,
    )
    token, cotangent, block_cols = lax.optimization_barrier((token, cotangent, block_cols))
    own, other, token = pack(across(got), [token])
    ring = [[own, to_core(other)]]

    live = iota((tiles, blocks), 1) < block_count[:, None]
    cols_a = jnp.where(live, block_cols, z.dom * tiles)
    cols_b = to_core(cols_a)
    cot_a = lax.dynamic_slice_in_dim(cotangent, core * half, half, axis=1)
    cot_b = to_core(lax.dynamic_slice_in_dim(cotangent, (1 - core) * half, half, axis=1))

    wide = 2 * z.grp * z.per_grp
    inner = (wide, rows) if z.pair % 16 == 0 else (2 * z.grp, z.dom, z.pair, rows)

    def prepared(cols, vals, token):
        *got, token = call(
            lambda *refs: prepare_kernel(z, *refs),
            [(inner, BF16)] * z.zz,
            [("s", me), ("s", cols), ("v", message), ("v", vals)],
            "prepare", 7,
            (
                pltpu.VMEM((z.dom * rows + tile, tile), F32),
                pltpu.VMEM((z.dom * rows, rows), BF16),
            ),
            after=[token, cols_b], token=True,
        )
        return [part.reshape(wide, rows) for part in got], token

    for k in range(1, z.zz):
        ring.append([to_zz(part, 1) for part in ring[-1]])
        if k == 1:
            *picked, token = rows_of(pick, features, [token, cot_a, cot_b])
            lefts, token_l = turned_of(across(picked))
            turned_a, token = prepared(cols_a, block_vals, token)
            for part in range(2):
                ring[1][part], token = lax.optimization_barrier((ring[1][part], token))
        if k == 2:
            turned_b, token = prepared(cols_b, vals_b, token)
            ring[2][1], token = lax.optimization_barrier((ring[2][1], token))
    turned = (turned_a, turned_b)

    agg = []
    for k in range(z.zz):
        last = k == z.zz - 1
        ins = [("v", part) for part in (turned[0][k], turned[1][k], *ring[k], *agg)]
        outs = [((rows, half), F32)] * 2
        if last:
            ahead = (turned[0][k], turned[1][k])
            ins += [("v", part) for part in (cot_a, cot_b, *ahead)]
            outs = [((rows, half), BF16)] * 6
        agg = call(
            lambda *refs, k=k, last=last: forward_kernel(z, k == 0, last, *refs),
            outs, ins, "forward", 3 if last else 1,
            after=[token_l] if k == z.zz - 2 else [token] if k == 0 else (),
        )
    hidden_a, hidden_b, grad_a, grad_b, *came = agg

    def back(k):
        return call(
            back_kernel,
            [((rows, half), F32)] * 2,
            [("v", part) for part in (turned[0][k], turned[1][k], grad_a, grad_b)],
            "back", 1,
        )

    come = to_core(hidden_b)
    for k in range(z.zz - 2, -1, -1):
        came = [to_zz(part, -1) for part in came]
        mine = back(k)
        if k:
            passed = [
                call(
                    pass_kernel, [((rows, half), BF16)], [("v", part), ("v", moved)], "pass", 0.5,
                    after=[come] if i == 1 and k == 1 else (), token=True,
                )
                for i, (part, moved) in enumerate(zip(mine, came))
            ]
            came = [part for part, _ in passed]
    first = core == 0
    hidden = jnp.concatenate(
        [jnp.where(first, hidden_a, come), jnp.where(first, come, hidden_a)], axis=1
    )

    share = width_in // z.grp
    (part,) = call(
        part_kernel, [((width_in, half), F32)],
        [("v", value) for value in (lefts[0], mine[0], came[0])], "part", 1,
    )
    terms = call(
        lambda *refs: grad_kernel(z, *refs),
        [((share, half), BF16)] * z.grp,
        [("s", me)] + [("v", value) for value in (lefts[1], mine[1], came[1], part)],
        "grad", 1.5,
        (pltpu.VMEM((width_in, half), BF16),),
    )

    def total_of(parts):
        return call(
            sum_kernel, [((share, half), BF16)], [("v", part) for part in parts], "sum", 0.5
        )[0]

    mine = total_of(across(terms)[::-1])
    step = 1
    while step < z.zz:
        mine = total_of(
            [mine, lax.ppermute(mine, "zz", [(i, i ^ step) for i in range(z.zz)])]
        )
        step *= 2
    come = [to_core(mine)]
    mine, come[0] = lax.optimization_barrier((mine, come[0]))
    mine = across([mine] * z.grp)
    come += [to_core(part) for part in mine[1:]]
    (grad_weight,) = call(
        lambda *refs: last_kernel(z, *refs),
        [((width_in, hidden_units), F32)],
        [("s", me)] + [("v", part) for part in [come[0], *mine, *come[1:]]],
        "last", 2,
    )
    return hidden, grad_weight


def solution(mesh):
    n_grp, n_dom = mesh.shape["grp"], mesh.shape["dom"]
    split = Mesh(mesh.devices.reshape(n_grp, n_dom // 2, 2), ("grp", "zz", "core"))
    by_rows = ("grp", "zz", "core")
    placed = (
        P(by_rows, None),
        P(by_rows),
        P(by_rows, None),
        P(by_rows),
        P(by_rows, None, None, None),
        P(),
        P(by_rows, None),
    )
    return jax.shard_map(
        shards,
        mesh=split,
        in_specs=placed,
        out_specs=(P(by_rows, None), P()),
        check_vma=False,
    )
```

```python
import jax
import jax.numpy as jnp
from jax import lax
from jax.experimental import pallas as pl
from jax.experimental.pallas import tpu as pltpu
from jax.sharding import Mesh, PartitionSpec as P

BF16 = jnp.bfloat16
F32 = jnp.float32
I32 = jnp.int32


def log2(n):
    assert n & (n - 1) == 0
    return n.bit_length() - 1


def place_of(at, count):
    place = at
    for shift in range(1, log2(count)):
        place = place ^ (at >> shift)
    return place


def iota(shape, dim):
    return lax.broadcasted_iota(I32, shape, dim)


def one_hot(mask):
    return jnp.where(mask, 1.0, 0.0).astype(BF16)


def dot(a, b):
    return jnp.dot(a, b, preferred_element_type=F32)


def dot_rows(a, b):
    return lax.dot_general(a, b, (((0,), (0,)), ((), ())), preferred_element_type=F32)


def call(body, outs, ins, name, us, scratch=(), after=(), token=False):
    smem = pl.BlockSpec(memory_space=pltpu.SMEM)
    vmem = pl.BlockSpec(memory_space=pltpu.VMEM)
    count = len(ins)
    ties = len(after)
    if token:
        outs = [*outs, ((8, 128), F32)]

    def kernel(*refs):
        refs = refs[:count] + refs[count + ties:]
        if token:
            at = count + len(outs) - 1
            refs[at][...] = jnp.zeros((8, 128), F32)
            refs = refs[:at] + refs[at + 1:]
        body(*refs)

    arrays = [jax.ShapeDtypeStruct(s, d) for s, d in outs] + [value for _, value in ins]
    size = sum(a.size * a.dtype.itemsize for a in arrays + [m.get_array_aval() for m in scratch])
    return pl.pallas_call(
        kernel,
        out_shape=tuple(jax.ShapeDtypeStruct(s, d) for s, d in outs),
        in_specs=[smem if where == "s" else vmem for where, _ in ins]
        + [vmem] * ties,
        out_specs=tuple(vmem for _ in outs),
        scratch_shapes=list(scratch),
        compiler_params=pltpu.CompilerParams(vmem_limit_bytes=size + (5 << 20)),
        cost_estimate=pl.CostEstimate(flops=int(us * 1e8), bytes_accessed=0, transcendentals=0),
        name=name,
    )(*(value for _, value in ins), *after)


class Sizes:
    def __init__(self, rows, tiles):
        self.grp, self.zz = lax.axis_size("grp"), lax.axis_size("zz")
        self.dom = 2 * self.zz
        self.rows, self.tiles = rows, tiles
        self.pair = rows // (self.grp * self.dom)
        self.piece = self.grp * self.pair
        self.per_grp = self.dom * self.pair
        assert rows // 128 < 5 and self.pair <= 128


def column(row):
    n = row.shape[1]
    on = iota((n, n), 0) == iota((n, n), 1)
    return jnp.sum(jnp.where(on, row.astype(F32), 0.0), axis=1, keepdims=True).astype(I32)


def index_kernel(z, me_ref, order_ref, out_ref):
    rows = z.rows
    shift = log2(rows)
    order_r = order_ref[...]
    order_c = column(order_r)
    down, across = iota((rows, rows), 0), iota((rows, rows), 1)
    source_r, source_c = order_r >> shift, order_c >> shift
    row_c = order_c & (rows - 1)
    same = jnp.where(source_c == source_r, 1.0, 0.0)
    rank_c = jnp.sum(jnp.where(across < down, same, 0.0), axis=1, keepdims=True).astype(I32)
    rank_r = jnp.sum(jnp.where(down < across, same, 0.0), axis=0, keepdims=True).astype(I32)
    owner = one_hot(iota((z.grp * z.dom, rows), 0) == source_r)
    at_rank = iota((rows, z.pair), 1) == rank_c
    high = jnp.where(at_rank, (row_c >> 4).astype(F32), 0.0).astype(BF16)
    low = jnp.where(at_rank, (row_c & 15).astype(F32), 0.0).astype(BF16)
    want = (dot(owner, high) * 16.0 + dot(owner, low)).astype(I32)
    out_ref[...] = jnp.zeros_like(out_ref)
    for d in range(z.grp * z.dom):
        out_ref[d, 0:1, 0:z.pair] = want[d:d + 1, :]
    across_grp = (source_r >> log2(z.dom)) ^ me_ref[0]
    inner = source_r & (z.dom - 1)
    slot = (inner * z.grp + across_grp) * z.pair + rank_r
    for i in range(rows // 128):
        lanes = slot[:, i * 128:(i + 1) * 128]
        out_ref[:, 1 + i:2 + i, :] = jnp.broadcast_to(lanes[None], (z.grp * z.dom, 1, 128))


def product_kernel(z, me_ref, features_ref, weight_ref, *outs):
    half = outs[0].shape[1]
    for flip, out in enumerate(outs):
        at = pl.multiple_of((me_ref[2] ^ flip) * half, half)
        out[...] = dot(features_ref[...], weight_ref[:, pl.ds(at, half)]).astype(BF16)


def send_kernel(z, me_ref, message_ref, own_ref, other_ref, pick_ref, *outs):
    devices, height, width = message_ref.shape
    message = message_ref[...].reshape(devices * height, width)
    shape = (z.rows, devices * height)
    asker = (iota(shape, 0) >> log2(z.pair)) ^ (me_ref[0] * z.dom)
    spread = one_hot(iota(shape, 1) == asker * height)
    high = dot(spread, (message >> 4).astype(F32).astype(BF16))
    low = dot(spread, (message & 15).astype(F32).astype(BF16))
    mine = iota((z.rows, width), 1) == (iota((z.rows, width), 0) & (z.pair - 1))
    wanted = jnp.sum(jnp.where(mine, high * 16.0 + low, 0.0), axis=1, keepdims=True).astype(I32)
    pick_ref[...] = one_hot(iota((z.rows, z.rows), 1) == wanted)
    for flip, product in enumerate((own_ref, other_ref)):
        got = dot(pick_ref[...], product[...]).astype(BF16)
        for s in range(z.grp):
            outs[s][flip] = got[s * z.per_grp:(s + 1) * z.per_grp, :]


def rows_kernel(z, pick_ref, features_ref, *outs):
    for s, out in enumerate(outs):
        pick = pick_ref[s * z.per_grp:(s + 1) * z.per_grp, :]
        out[...] = dot(pick, features_ref[...]).astype(BF16)


def pack_kernel(z, *refs):
    ins, outs = refs[:z.grp][::-1], refs[z.grp:]
    for rel, out in enumerate(outs):
        for s in range(z.grp):
            out[s * z.per_grp:(s + 1) * z.per_grp, :] = ins[s][rel]


def prepare_kernel(z, me_ref, cols_ref, message_ref, vals_ref, *refs):
    outs, (total, dense) = refs[:z.zz], refs[z.zz:]
    tiles, blocks, tile, _ = vals_ref.shape

    @pl.loop(0, tiles)
    def _(t):
        total[...] = jnp.zeros_like(total)
        for k in range(blocks):
            at = pl.multiple_of(cols_ref[t, k] * tile, tile)
            total[pl.ds(at, tile), :] += vals_ref[t, k].T.astype(F32)
        left = pl.multiple_of(t * tile, tile)
        dense[:, pl.ds(left, tile)] = total[pl.ds(0, z.dom * z.rows), :].astype(BF16)

    @pl.loop(0, z.dom)
    def _(n):
        message = message_ref[me_ref[0] * z.dom + n]
        slot = jnp.concatenate([message[1 + i:2 + i, :] for i in range(z.rows // 128)], axis=1)
        rank, at = slot & (z.pair - 1), slot >> log2(z.pair)
        s, at = at & (z.grp - 1), at >> log2(z.grp)
        k = (place_of(me_ref[1], z.zz) - place_of(at >> 1, z.zz)) & (z.zz - 1)
        rel = (at & 1) ^ me_ref[2]
        slot = ((k * 2 + rel) * z.grp + s) * z.pair + rank
        place = one_hot(iota((z.rows, z.rows), 0) == slot)
        at = pl.multiple_of(n * z.rows, z.rows)
        part = dot(place, dense[pl.ds(at, z.rows), :]).astype(BF16)
        for k in range(z.zz):
            for p in range(2 * z.grp):
                first = (k * 2 * z.grp + p) * z.pair
                rows = part[first:first + z.pair, :]
                if z.pair % 16 == 0:
                    to = pl.multiple_of(p * z.per_grp + n * z.pair, z.pair)
                    outs[k][pl.ds(to, z.pair), :] = rows
                else:
                    outs[k][p, n] = rows


def turn_kernel(*refs):
    out, height = refs[-1], refs[0].shape[0]
    for s, part in enumerate(refs[:-1]):
        out[:, s * height:(s + 1) * height] = part[...].T


def forward_kernel(z, first, last, *refs):
    turned, refs = refs[:2], refs[2:]
    rows, refs = jnp.concatenate([ref[...] for ref in refs[:2]], axis=0), refs[2:]
    agg = [dot_rows(ref[...], rows) for ref in turned]
    if not first:
        agg = [part + ref[...] for part, ref in zip(agg, refs)]
        refs = refs[2:]
    if not last:
        for ref, part in zip(refs, agg):
            ref[...] = part
        return
    cots, ahead, hiddens, grads = (refs[2 * i:2 * i + 2] for i in range(4))
    for part, cot, hidden, grad in zip(agg, cots, hiddens, grads):
        sig = jax.nn.sigmoid(part)
        hidden[...] = (part * sig).astype(BF16)
        grad[...] = (cot[...].astype(F32) * (sig * (1.0 + part * (1.0 - sig)))).astype(BF16)
    back_kernel(*ahead, *grads, *refs[-2:])


def back_kernel(turned_a, turned_b, grad_a, grad_b, *outs):
    size = outs[0].shape[0]
    for i, out in enumerate(outs):
        rows = pl.ds(i * size, size)
        value = dot(turned_a[rows, :], grad_a[...]) + dot(turned_b[rows, :], grad_b[...])
        out[...] = value.astype(out.dtype)


def pass_kernel(mine_ref, come_ref, out_ref):
    out_ref[...] = (mine_ref[...] + come_ref[...].astype(F32)).astype(BF16)


def part_kernel(left_ref, mine_ref, come_ref, out_ref):
    grad = (mine_ref[...] + come_ref[...].astype(F32)).astype(BF16)
    out_ref[...] = dot(left_ref[...], grad)


def grad_kernel(z, me_ref, left_ref, mine_ref, come_ref, part_ref, *refs):
    outs, whole = refs[:-1], refs[-1]
    grad = (mine_ref[...] + come_ref[...].astype(F32)).astype(BF16)
    whole[...] = (part_ref[...] + dot(left_ref[...], grad)).astype(BF16)
    share = whole.shape[0] // z.grp
    for s in range(z.grp):
        at = pl.multiple_of((me_ref[0] ^ s) * share, share)
        outs[s][...] = whole[pl.ds(at, share), :]


def sum_kernel(*refs):
    refs[-1][...] = sum(term[...].astype(F32) for term in refs[:-1]).astype(BF16)


def last_kernel(z, me_ref, *refs):
    pieces, out = refs[:-1], refs[-1]
    share, half = pieces[0].shape
    for rel in range(2):
        left = pl.multiple_of((me_ref[2] ^ rel) * half, half)
        for s in range(z.grp):
            at = pl.multiple_of((me_ref[0] ^ s) * share, share)
            out[pl.ds(at, share), pl.ds(left, half)] = pieces[rel * z.grp + s][...].astype(F32)


def shards(features, node_order, block_cols, block_count, block_vals, weight, cotangent):
    rows, width_in = features.shape
    hidden_units = weight.shape[1]
    half = hidden_units // 2
    tiles, blocks, tile = block_vals.shape[0], block_vals.shape[1], block_vals.shape[-1]
    z = Sizes(rows, tiles)
    at_grp, at_zz, core = lax.axis_index("grp"), lax.axis_index("zz"), lax.axis_index("core")
    me = jnp.stack([at_grp, at_zz, core]).astype(I32)

    def to_core(x):
        return lax.ppermute(x, "core", [(0, 1), (1, 0)])

    def to_grp(x, s):
        return lax.ppermute(x, "grp", [(i, i ^ s) for i in range(z.grp)]) if s else x

    def to_zz(x, k):
        order = [i ^ (i >> 1) for i in range(z.zz)]
        return lax.ppermute(x, "zz", [(order[i], order[(i + k) % z.zz]) for i in range(z.zz)])

    first_half = features[:rows // 2]
    (message,) = call(
        lambda *refs: index_kernel(z, *refs),
        [((z.grp * z.dom, 8, 128), I32)],
        [("s", me), ("v", node_order.reshape(1, rows))],
        "index", 1,
    )
    message, features = lax.optimization_barrier((message, features))
    message = lax.all_to_all(
        message, ("grp", "zz", "core"), split_axis=0, concat_axis=0, tiled=True
    )
    vals_b = to_core(block_vals)

    def across(parts):
        return [to_grp(part, s) for s, part in enumerate(parts)]

    def pack(parts, after=()):
        return call(
            lambda *refs: pack_kernel(z, *refs),
            [((rows, half), BF16)] * 2,
            [("v", part) for part in parts[::-1]],
            "pack", 0.5, after=after, token=True,
        )

    def rows_of(pick, part, after):
        return call(
            lambda *refs: rows_kernel(z, *refs),
            [((z.per_grp, width_in), BF16)] * z.grp,
            [("v", pick), ("v", part)],
            "rows", 1, after=after, token=True,
        )

    def turned_of(parts):
        left, token = call(
            turn_kernel, [((width_in, rows), BF16)], [("v", part) for part in parts],
            "turn", 0.5, token=True,
        )
        return [left, to_core(left)], token

    products = call(
        lambda *refs: product_kernel(z, *refs),
        [((rows, half), BF16)] * 2,
        [("s", me), ("v", features), ("v", weight)],
        "product", 15,
    )
    pick, *got, token = call(
        lambda *refs: send_kernel(z, *refs),
        [((rows, rows), BF16)] + [((2, z.per_grp, half), BF16)] * z.grp,
        [("s", me), ("v", message)] + [("v", part) for part in products],
        "send", 1.5, token=True,
    )
    token, cotangent, block_cols = lax.optimization_barrier((token, cotangent, block_cols))
    own, other, token = pack(across(got), [token])
    ring = [[own, to_core(other)]]

    live = iota((tiles, blocks), 1) < block_count[:, None]
    cols_a = jnp.where(live, block_cols, z.dom * tiles)
    cols_b = to_core(cols_a)
    cot_a = lax.dynamic_slice_in_dim(cotangent, core * half, half, axis=1)
    cot_b = to_core(lax.dynamic_slice_in_dim(cotangent, (1 - core) * half, half, axis=1))

    wide = 2 * z.grp * z.per_grp
    inner = (wide, rows) if z.pair % 16 == 0 else (2 * z.grp, z.dom, z.pair, rows)

    def prepared(cols, vals, token):
        *got, token = call(
            lambda *refs: prepare_kernel(z, *refs),
            [(inner, BF16)] * z.zz,
            [("s", me), ("s", cols), ("v", message), ("v", vals)],
            "prepare", 7,
            (
                pltpu.VMEM((z.dom * rows + tile, tile), F32),
                pltpu.VMEM((z.dom * rows, rows), BF16),
            ),
            after=[token, cols_b], token=True,
        )
        return [part.reshape(wide, rows) for part in got], token

    for k in range(1, z.zz):
        ring.append([to_zz(part, 1) for part in ring[-1]])
        if k == 1:
            *picked, token = rows_of(pick, features, [token, cot_a, cot_b])
            lefts, token_l = turned_of(across(picked))
            turned_a, token = prepared(cols_a, block_vals, token)
            for part in range(2):
                ring[1][part], token = lax.optimization_barrier((ring[1][part], token))
        if k == 2:
            turned_b, token = prepared(cols_b, vals_b, token)
            ring[2][1], token = lax.optimization_barrier((ring[2][1], token))
    turned = (turned_a, turned_b)

    agg = []
    for k in range(z.zz):
        last = k == z.zz - 1
        ins = [("v", part) for part in (turned[0][k], turned[1][k], *ring[k], *agg)]
        outs = [((rows, half), F32)] * 2
        if last:
            ahead = (turned[0][k], turned[1][k])
            ins += [("v", part) for part in (cot_a, cot_b, *ahead)]
            outs = [((rows, half), BF16)] * 6
        agg = call(
            lambda *refs, k=k, last=last: forward_kernel(z, k == 0, last, *refs),
            outs, ins, "forward", 3 if last else 1,
            after=[token_l] if k == z.zz - 2 else [token] if k == 0 else (),
        )
    hidden_a, hidden_b, grad_a, grad_b, *came = agg

    def back(k):
        return call(
            back_kernel,
            [((rows, half), F32)] * 2,
            [("v", part) for part in (turned[0][k], turned[1][k], grad_a, grad_b)],
            "back", 1,
        )

    come = to_core(hidden_b)
    for k in range(z.zz - 2, -1, -1):
        came = [to_zz(part, -1) for part in came]
        mine = back(k)
        if k:
            passed = [
                call(
                    pass_kernel, [((rows, half), BF16)], [("v", part), ("v", moved)], "pass", 0.5,
                    after=[come] if i == 1 and k == 1 else (), token=True,
                )
                for i, (part, moved) in enumerate(zip(mine, came))
            ]
            came = [part for part, _ in passed]
    first = core == 0
    hidden = jnp.concatenate(
        [jnp.where(first, hidden_a, come), jnp.where(first, come, hidden_a)], axis=1
    )

    share = width_in // z.grp
    (part,) = call(
        part_kernel, [((width_in, half), F32)],
        [("v", value) for value in (lefts[0], mine[0], came[0])], "part", 1,
    )
    terms = call(
        lambda *refs: grad_kernel(z, *refs),
        [((share, half), BF16)] * z.grp,
        [("s", me)] + [("v", value) for value in (lefts[1], mine[1], came[1], part)],
        "grad", 1.5,
        (pltpu.VMEM((width_in, half), BF16),),
    )

    def total_of(parts):
        return call(
            sum_kernel, [((share, half), BF16)], [("v", part) for part in parts], "sum", 0.5
        )[0]

    mine = total_of(across(terms)[::-1])
    step = z.zz // 2
    while step:
        mine = total_of(
            [mine, lax.ppermute(mine, "zz", [(i, i ^ step) for i in range(z.zz)])]
        )
        step //= 2
    mine = across([mine] * z.grp)
    (grad_weight,) = call(
        lambda *refs: last_kernel(z, *refs),
        [((width_in, hidden_units), F32)],
        [("s", me)] + [("v", part) for part in mine + [to_core(part) for part in mine]],
        "last", 2,
    )
    return hidden, grad_weight


def solution(mesh):
    n_grp, n_dom = mesh.shape["grp"], mesh.shape["dom"]
    split = Mesh(mesh.devices.reshape(n_grp, n_dom // 2, 2), ("grp", "zz", "core"))
    by_rows = ("grp", "zz", "core")
    placed = (
        P(by_rows, None),
        P(by_rows),
        P(by_rows, None),
        P(by_rows),
        P(by_rows, None, None, None),
        P(),
        P(by_rows, None),
    )
    return jax.shard_map(
        shards,
        mesh=split,
        in_specs=placed,
        out_specs=(P(by_rows, None), P()),
        check_vma=False,
    )
```
